32 devices in a mesh: row: 4 (over x, core), col: 8 (over z, y).
Axes of the slice: x: 2, y: 2, z: 4, core: 2. Of those that a mesh axis runs over, the one named last changes fastest.
Arguments:
- hidden_in: bfloat16 [14336, 2048], P('col', 'row'), may hold values from -6 to 6
- gain_before: float32 [2048], P('row'), may hold values from 0.25 to 1.75
- query_weight: bfloat16 [2048, 2048], P('row', 'col'), may hold values from -0.125 to 0.125
- key_weight: bfloat16 [2048, 2048], P('row', 'col'), may hold values from -0.125 to 0.125
- value_weight: bfloat16 [2048, 2048], P('row', 'col'), may hold values from -0.125 to 0.125
- output_weight: bfloat16 [2048, 2048], P('col', 'row'), may hold values from -2 to 2
- gain_middle: float32 [2048], P('row'), may hold values from 0.25 to 1.75
- gate_weight: bfloat16 [2048, 8192], P('row', 'col'), may hold values from -0.125 to 0.125
- up_weight: bfloat16 [2048, 8192], P('row', 'col'), may hold values from -0.125 to 0.125
- down_weight: bfloat16 [8192, 2048], P('col', 'row'), may hold values from -0.0625 to 0.0625
- cotangent: bfloat16 [14336, 2048], P('col', 'row'), may hold values from -6 to 6
- branch_points: int32 [4, 6], replicated, may hold values from 1024 to 2048, as said below
- lengths: int32 [4, 6], replicated, may hold values from 128 to 256, as said below
Outputs:
- layer_out: bfloat16 [14336, 2048], P('col', 'row')
- input_grad: float32 [14336, 2048], P('col', 'row')
- before_grad: float32 [2048], P('row')
- query_grad: float32 [2048, 2048], P('row', 'col')
- key_grad: float32 [2048, 2048], P('row', 'col')
- value_grad: float32 [2048, 2048], P('row', 'col')
- output_grad: float32 [2048, 2048], P('col', 'row')
- middle_grad: float32 [2048], P('row')
- gate_grad: float32 [2048, 8192], P('row', 'col')
- up_grad: float32 [2048, 8192], P('row', 'col')
- down_grad: float32 [8192, 2048], P('col', 'row')
- rms_values: float32 [3], replicated
The draws below stay inside these ranges and needn't reach their ends.
Inputs may be any that keep to these rules, and one draw needn't show every extreme that they name: `branch_points`: in every group one continuation follows the whole prompt of 2048 tokens. `lengths`: in every group one continuation fills all 256 slots.
All inputs are finite; a program needn't handle non-finite values.
Results may differ from the reference program's by a relative error of at most 0.014.
Values may be sent and summed in bfloat16 or wider, within the bound.
No kernel may reach another device: no remote copies, remote signals or barrier semaphores. Data moves between devices by JAX's collectives and lax.ppermute only.
A program may use at most 768 MiB of HBM per device.

```python
import jax
import jax.numpy as jnp
from jax import lax

D = 2048
HEADS = 32
HD = 64
FF = 8192
PROMPT = 2048
CLEN = 256
CONTS = 6
GROUPS = 4
GTOK = 3584
TOKENS = 14336
QD = 2048


def spread_table(key, lowest, limit, fullest):
    key_values, key_chosen = jax.random.split(key)
    values = jax.random.randint(key_values, (GROUPS, CONTS), lowest, limit)
    chosen = jax.random.randint(key_chosen, (GROUPS, 1), 0, CONTS)
    places = jnp.arange(CONTS, dtype=jnp.int32)[None, :]
    return jnp.where(places == chosen, fullest, values).astype(jnp.int32)


def draw_branch_points(key, part):
    key = jax.random.fold_in(key, 7)
    return spread_table(key, PROMPT // 2, PROMPT + 1, PROMPT)


def draw_lengths(key, part):
    key = jax.random.fold_in(key, 13)
    return spread_table(key, CLEN // 2, CLEN + 1, CLEN)


def block_scale(own_key, shape, cuts, low, high):
    loudness, own = 1.0, jax.random.fold_in(own_key, 6)
    for position, parts in cuts:
        steps = jnp.exp(jax.random.uniform(jax.random.fold_in(own, position), (parts,), jnp.float32, low / len(cuts), high / len(cuts)))
        loudness = loudness * jnp.repeat(steps, shape[position] // parts).reshape([-1 if axis == position else 1 for axis in range(len(shape))])
    return loudness


def scatter_about(own_key, shape, deviation, most, pieces=(), kind=jnp.bfloat16):
    loudness = block_scale(own_key, shape, pieces, -0.22, 0.18) if pieces else 1.0
    entries = jax.random.normal(own_key, shape, jnp.float32) * deviation * loudness
    return jnp.minimum(jnp.maximum(entries, -most), most).astype(kind)


def setup_inputs(seed: int = 0) -> dict:
    arg_keys = jax.random.split(jax.random.key(seed), 14)
    hidden_in = scatter_about(arg_keys[0], (TOKENS, D), 1.0, 6.0, ((0, 8), (1, 4)))
    gain_before = jnp.clip(1.0 + 0.15 * jax.random.normal(arg_keys[1], (D,), jnp.float32), 0.25, 1.75)
    query_weight = scatter_about(arg_keys[2], (D, QD), D ** -0.5, 0.125, ((0, 4), (1, 8)))
    key_weight = scatter_about(arg_keys[3], (D, QD), D ** -0.5, 0.125, ((0, 4), (1, 8)))
    value_weight = scatter_about(arg_keys[4], (D, QD), D ** -0.5, 0.125, ((0, 4), (1, 8)))
    output_weight = scatter_about(arg_keys[5], (QD, D), (max(8 * QD // PROMPT, 1)) ** -0.5, 2.0, ((0, 8), (1, 4)))
    gain_middle = jnp.clip(1.0 + 0.15 * jax.random.normal(arg_keys[6], (D,), jnp.float32), 0.25, 1.75)
    gate_weight = scatter_about(arg_keys[7], (D, FF), D ** -0.5, 0.125, ((0, 4), (1, 8)))
    up_weight = scatter_about(arg_keys[8], (D, FF), D ** -0.5, 0.125, ((0, 4), (1, 8)))
    down_weight = scatter_about(arg_keys[9], (FF, D), FF ** -0.5, 0.0625, ((0, 8), (1, 4)))
    cotangent = scatter_about(arg_keys[10], (TOKENS, D), 1.0, 6.0, ((0, 8), (1, 4)))
    branch_points = draw_branch_points(jax.random.fold_in(arg_keys[13], 71), 0)
    lengths = draw_lengths(jax.random.fold_in(arg_keys[13], 71), 0)
    return dict(hidden_in=hidden_in, gain_before=gain_before, query_weight=query_weight, key_weight=key_weight, value_weight=value_weight, output_weight=output_weight, gain_middle=gain_middle, gate_weight=gate_weight, up_weight=up_weight, down_weight=down_weight, cotangent=cotangent, branch_points=branch_points, lengths=lengths)


EPSILON = 1e-05
THETA = 130000.0
NEGATIVE = -1e+30

@jax.custom_vjp
def low(v):
    return lax.optimization_barrier(v.astype(jnp.bfloat16)).astype(jnp.float32)

@jax.custom_vjp
def low_back(v):
    return v

def low_keep(v):
    return (low(v), None)

def low_pass(kept, grad):
    return (grad,)

def back_keep(v):
    return (v, None)

def back_low(kept, grad):
    return (low(grad),)
low.defvjp(low_keep, low_pass)
low_back.defvjp(back_keep, back_low)

def product(left, right):
    return jnp.dot(left, right, precision=lax.Precision.HIGHEST)

def rope_tables(positions):
    halfway = HD // 2
    frequency = THETA ** (-2.0 * jnp.arange(halfway, dtype=jnp.float32) / HD)
    angles = positions.astype(jnp.float32)[:, None] * frequency[None, :]
    return (jnp.cos(angles), jnp.sin(angles))

def rotate(values, cosine, sine):
    halfway = values.shape[-1] // 2
    former = values[..., :halfway]
    latter = values[..., halfway:]
    cos_rows = cosine[:, None, :]
    sin_rows = sine[:, None, :]
    return jnp.concatenate([former * cos_rows - latter * sin_rows, latter * cos_rows + former * sin_rows], -1)

def group_positions(branch_row):
    prompt_part = jnp.arange(PROMPT, dtype=jnp.int32)
    branch_part = branch_row[:, None] + jnp.arange(CLEN, dtype=jnp.int32)[None, :]
    return jnp.concatenate([prompt_part, branch_part.reshape(-1)])

def group_masks(branch_row, length_row):
    prompt_index = jnp.arange(PROMPT, dtype=jnp.int32)
    prompt_allowed = prompt_index[None, :] <= prompt_index[:, None]
    slots = jnp.arange(CONTS * CLEN, dtype=jnp.int32)
    slot_cont = slots // CLEN
    slot_step = slots % CLEN
    reach = branch_row[slot_cont]
    from_prompt = prompt_index[None, :] < reach[:, None]
    from_own = (slot_cont[None, :] == slot_cont[:, None]) & (slot_step[None, :] <= slot_step[:, None])
    from_own = from_own & (slot_step[None, :] < length_row[slot_cont][None, :])
    return (prompt_allowed, jnp.concatenate([from_prompt, from_own], 1))

def masked_softmax(scores, allowed):
    shifted = jnp.where(allowed, scores, NEGATIVE)
    peak = lax.optimization_barrier(jnp.max(shifted, -1, keepdims=True))
    weights = jnp.exp(shifted - peak)
    return weights / lax.optimization_barrier(jnp.sum(weights, -1, keepdims=True))

def group_layer(residual, probe, gain_before, query_weight, key_weight, value_weight, output_weight, gain_middle, gate_weight, up_weight, down_weight, branch_row, length_row):
    scale = HD ** (-0.5)
    scale_one = lax.rsqrt(lax.optimization_barrier(jnp.mean(residual * residual, -1, keepdims=True)) + EPSILON)
    low_one = low(residual * scale_one * gain_before)
    query_raw = low_back(product(low_one, query_weight))
    key_raw = low_back(product(low_one, key_weight))
    value_raw = low(low_back(product(low_one, value_weight)))
    cosine, sine = rope_tables(group_positions(branch_row))
    query = low(rotate(query_raw.reshape(GTOK, HEADS, HD), cosine, sine))
    keys = low(rotate(key_raw.reshape(GTOK, HEADS, HD), cosine, sine))
    values = value_raw.reshape(GTOK, HEADS, HD)
    prompt_allowed, branch_allowed = group_masks(branch_row, length_row)

    def one_head(item):
        head_query, head_keys, head_values = item
        prompt_scores = low_back(product(head_query[:PROMPT], head_keys[:PROMPT].T) * scale)
        prompt_probs = masked_softmax(prompt_scores, prompt_allowed)
        prompt_out = product(low(prompt_probs), head_values[:PROMPT])
        branch_scores = low_back(product(head_query[PROMPT:], head_keys.T) * scale)
        branch_probs = masked_softmax(branch_scores, branch_allowed)
        branch_out = product(low(branch_probs), head_values)
        return jnp.concatenate([prompt_out, branch_out], 0)
    heads_out = lax.map(jax.checkpoint(one_head), (query.transpose(1, 0, 2), keys.transpose(1, 0, 2), values.transpose(1, 0, 2)))
    heads = low(low_back(heads_out.transpose(1, 0, 2).reshape(GTOK, HEADS * HD)))
    attention = low_back(product(heads, output_weight))
    middle = residual + attention + probe
    scale_two = lax.rsqrt(lax.optimization_barrier(jnp.mean(middle * middle, -1, keepdims=True)) + EPSILON)
    low_two = low(middle * scale_two * gain_middle)
    gate = low_back(product(low_two, gate_weight))
    up = low_back(product(low_two, up_weight))
    hidden = low(jax.nn.silu(gate) * up)
    return (middle + product(hidden, down_weight), attention)

def reference(hidden_in, gain_before, query_weight, key_weight, value_weight, output_weight, gain_middle, gate_weight, up_weight, down_weight, cotangent, branch_points, lengths):
    residual = hidden_in.astype(jnp.float32).reshape(GROUPS, GTOK, D)
    probe = jnp.zeros((GROUPS, GTOK, D), jnp.float32)

    def whole(residual, probe, gain_before, query_weight, key_weight, value_weight, output_weight, gain_middle, gate_weight, up_weight, down_weight):

        def one_group(item):
            return group_layer(item[0], item[1], gain_before, query_weight, key_weight, value_weight, output_weight, gain_middle, gate_weight, up_weight, down_weight, item[2], item[3])
        outputs, attention = lax.map(jax.checkpoint(one_group), (residual, probe, branch_points, lengths))
        return (outputs, attention)
    outputs, pullback, attention = jax.vjp(whole, residual, probe, gain_before.astype(jnp.float32), query_weight.astype(jnp.float32), key_weight.astype(jnp.float32), value_weight.astype(jnp.float32), output_weight.astype(jnp.float32), gain_middle.astype(jnp.float32), gate_weight.astype(jnp.float32), up_weight.astype(jnp.float32), down_weight.astype(jnp.float32), has_aux=True)
    grads = pullback(cotangent.astype(jnp.float32).reshape(GROUPS, GTOK, D))
    steps = jnp.arange(CLEN, dtype=jnp.int32)
    branch_valid = jnp.where(steps[None, None, :] < lengths[:, :, None], 1.0, 0.0).reshape(GROUPS, CONTS * CLEN)
    valid = jnp.concatenate([jnp.ones((GROUPS, PROMPT), jnp.float32), branch_valid.astype(jnp.float32)], 1)
    count = jnp.sum(valid) * D
    rounded = low(outputs)
    squares = jnp.stack([jnp.sum(valid * lax.optimization_barrier(jnp.sum(rounded * rounded, -1))), jnp.sum(valid * lax.optimization_barrier(jnp.sum(attention * attention, -1))), jnp.sum(valid * lax.optimization_barrier(jnp.sum(grads[1] * grads[1], -1)))])
    rms_values = jnp.sqrt(squares / count)
    return (outputs.reshape(TOKENS, D).astype(jnp.bfloat16), grads[0].reshape(TOKENS, D), grads[2], grads[3], grads[4], grads[5], grads[6], grads[7], grads[8], grads[9], grads[10], rms_values)
```

```python
import functools
import jax
import jax.numpy as jnp
from jax import lax
from jax.experimental import pallas as pl
from jax.experimental.pallas import tpu as pltpu
from jax.sharding import Mesh
from jax.sharding import PartitionSpec as P

HD = 64
PROMPT = 2048
CLEN = 256
CONTS = 6
GTOK = 3584
BLK = 256
PBLKS = PROMPT // BLK
BLOCKS = GTOK // BLK
ROWS = 3 * HD
BF = jnp.bfloat16
F32 = jnp.float32
LOW = -1e30
LOG2E = 1.4426950408889634
FACTOR = HD ** (-0.5) * LOG2E
VMEM_LIMIT = 56 * 1024 * 1024

NN = (((1,), (0,)), ((), ()))
NT = (((1,), (1,)), ((), ()))


def mm(a, b, dims=NN):
    return lax.dot_general(a, b, dims, preferred_element_type=F32)


def block_plan(info, block):
    cont = jnp.maximum(block - PBLKS, 0)
    is_cont = block >= PBLKS
    reach = info[cont]
    full = jnp.where(is_cont, reach // BLK, block)
    rest = jnp.where(is_cont, reach - full * BLK, 0)
    limit = jnp.where(is_cont, info[CONTS + cont], BLK)
    masked = 1 + (rest > 0).astype(jnp.int32)
    return full, rest, limit, masked


def local_ids(info, shape, axis):
    return lax.broadcasted_iota(jnp.int32, shape, axis) ^ info[2 * CONTS]


def masked_step(info, block, full, rest, limit, index):
    own = index == 0
    target = jnp.where(own, block, full)
    query_ids = local_ids(info, (1, BLK), 1)
    bound = jnp.where(own, jnp.minimum(query_ids + 1, limit), rest)
    key_ids = local_ids(info, (BLK, BLK), 0)
    return target, key_ids < bound


def columns(block):
    return pl.ds(pl.multiple_of(block * BLK, BLK), BLK)


def forward_kernel(heads, first, info, qkv, knat, out, lse, acc, top, tot):
    block = pl.program_id(0) + first
    full, rest, limit, masked = block_plan(info, block)
    here = columns(block)
    acc[...] = jnp.zeros_like(acc)
    top[...] = jnp.full_like(top, LOW)
    tot[...] = jnp.zeros_like(tot)

    def step(target, allowed):
        span = columns(target)
        for h in range(heads):
            query = qkv[h * ROWS : h * ROWS + HD, here]
            value = qkv[h * ROWS + 2 * HD : (h + 1) * ROWS, span]
            scores = mm(knat[h, span, :], query) * FACTOR
            if allowed is not None:
                scores = jnp.where(allowed, scores, LOW)
            old = top[h : h + 1, :]
            new = jnp.maximum(old, jnp.max(scores, 0, keepdims=True))
            weights = jnp.exp2(scores - new)
            shrink = jnp.exp2(old - new)
            top[h : h + 1, :] = new
            tot[h : h + 1, :] = tot[h : h + 1, :] * shrink + jnp.sum(weights, 0, keepdims=True)
            acc[h] = acc[h] * shrink + mm(value, weights.astype(BF))

    def full_step(index, carry):
        step(index, None)
        return carry

    def mask_step(index, carry):
        target, allowed = masked_step(info, block, full, rest, limit, index)
        step(target, allowed)
        return carry

    lax.fori_loop(0, full, full_step, 0)
    lax.fori_loop(0, masked, mask_step, 0)
    for h in range(heads):
        total = tot[h : h + 1, :]
        out[h * HD : (h + 1) * HD, :] = (acc[h] / total).astype(BF)
        lse[h : h + 1, :] = top[h : h + 1, :] + jnp.log2(total)


def attend_forward(info, qkv, knat, heads, first, count):
    pad = max(8, heads)
    return pl.pallas_call(
        functools.partial(forward_kernel, heads, first),
        grid=(count,),
        in_specs=[
            pl.BlockSpec(memory_space=pltpu.SMEM),
            pl.BlockSpec(qkv.shape, lambda i: (0, 0)),
            pl.BlockSpec(knat.shape, lambda i: (0, 0, 0)),
        ],
        out_specs=[
            pl.BlockSpec((heads * HD, BLK), lambda i: (0, i)),
            pl.BlockSpec((pad, BLK), lambda i: (0, i)),
        ],
        out_shape=[
            jax.ShapeDtypeStruct((heads * HD, count * BLK), BF),
            jax.ShapeDtypeStruct((pad, count * BLK), F32),
        ],
        scratch_shapes=[
            pltpu.VMEM((heads, HD, BLK), F32),
            pltpu.VMEM((pad, BLK), F32),
            pltpu.VMEM((pad, BLK), F32),
        ],
        compiler_params=pltpu.CompilerParams(vmem_limit_bytes=VMEM_LIMIT),
        cost_estimate=pl.CostEstimate(
            flops=heads * count * 6 * BLK * BLK * 1024,
            bytes_accessed=16 << 20,
            transcendentals=heads * count * 6 * BLK * BLK,
        ),
    )(info, qkv, knat)


def backward_kernel(heads, info, qkv, knat, vnat, d_out, heads_out, lse, cosine, sine, d_qkv, inner, d_keys, d_values, d_query):
    block = pl.program_id(0)
    full, rest, limit, masked = block_plan(info, block)
    here = columns(block)

    @pl.when(block == 0)
    def _():
        d_keys[...] = jnp.zeros_like(d_keys)
        d_values[...] = jnp.zeros_like(d_values)
        inner[...] = jnp.zeros_like(inner)

    d_query[...] = jnp.zeros_like(d_query)
    deltas = []
    for h in range(heads):
        rows = slice(h * HD, (h + 1) * HD)
        deltas.append(
            jnp.sum(d_out[rows, here].astype(F32) * heads_out[rows, here].astype(F32), 0, keepdims=True)
        )

    def step(target, allowed):
        span = columns(target)
        for h in range(heads):
            rows = slice(h * HD, (h + 1) * HD)
            query = qkv[h * ROWS : h * ROWS + HD, here]
            key = qkv[h * ROWS + HD : h * ROWS + 2 * HD, span]
            gradient = d_out[rows, here]
            scores = mm(knat[h, span, :], query) * FACTOR - lse[h : h + 1, here]
            if allowed is not None:
                scores = jnp.where(allowed, scores, LOW)
            probs = jnp.exp2(scores)
            d_probs = mm(vnat[h, span, :], gradient)
            d_scores = (probs * (d_probs - deltas[h])).astype(BF)
            d_query[h] += mm(key, d_scores)
            d_keys[rows, span] += mm(query, d_scores, NT)
            d_values[rows, span] += mm(gradient, probs.astype(BF), NT)

    def full_step(index, carry):
        step(index, None)
        return carry

    def mask_step(index, carry):
        target, allowed = masked_step(info, block, full, rest, limit, index)
        step(target, allowed)
        return carry

    lax.fori_loop(0, full, full_step, 0)
    lax.fori_loop(0, masked, mask_step, 0)

    half = HD // 2

    def turn(values, at):
        cos, sin = cosine[:, at], sine[:, at]
        former, latter = values[:half], values[half:]
        return former * cos + latter * sin, latter * cos - former * sin

    share = jnp.zeros((1, BLK), F32)
    for h in range(heads):
        start = h * ROWS
        values = d_query[h] * HD ** (-0.5)
        share += jnp.sum(values * qkv[start : start + HD, here].astype(F32), 0, keepdims=True)
        low, high = turn(values, here)
        d_qkv[start : start + half, here] = low.astype(BF)
        d_qkv[start + half : start + HD, here] = high.astype(BF)
    inner[0:1, here] = share

    @pl.when(block == BLOCKS - 1)
    def _():
        def finish(index, carry):
            at = columns(index)
            share = inner[0:1, at]
            for h in range(heads):
                start = h * ROWS + HD
                rows = slice(h * HD, (h + 1) * HD)
                values = d_keys[rows, at] * HD ** (-0.5)
                share += jnp.sum(values * qkv[start : start + HD, at].astype(F32), 0, keepdims=True)
                low, high = turn(values, at)
                d_qkv[start : start + half, at] = low.astype(BF)
                d_qkv[start + half : start + HD, at] = high.astype(BF)
                start += HD
                values = d_values[rows, at]
                share += jnp.sum(values * qkv[start : start + HD, at].astype(F32), 0, keepdims=True)
                d_qkv[start : start + HD, at] = values.astype(BF)
            inner[0:1, at] = share
            return carry

        lax.fori_loop(0, BLOCKS, finish, 0)


def attend_backward(info, qkv, knat, vnat, d_out, heads_out, lse, cosine, sine, heads):
    whole = lambda a: pl.BlockSpec(a.shape, lambda i, n=len(a.shape): (0,) * n)
    return pl.pallas_call(
        functools.partial(backward_kernel, heads),
        grid=(BLOCKS,),
        in_specs=[pl.BlockSpec(memory_space=pltpu.SMEM)]
        + [whole(a) for a in (qkv, knat, vnat, d_out, heads_out, lse, cosine, sine)],
        out_specs=[
            pl.BlockSpec(qkv.shape, lambda i: (0, 0)),
            pl.BlockSpec((8, GTOK), lambda i: (0, 0)),
        ],
        out_shape=[jax.ShapeDtypeStruct(qkv.shape, BF), jax.ShapeDtypeStruct((8, GTOK), F32)],
        scratch_shapes=[
            pltpu.VMEM((heads * HD, GTOK), F32),
            pltpu.VMEM((heads * HD, GTOK), F32),
            pltpu.VMEM((heads, HD, BLK), F32),
        ],
        compiler_params=pltpu.CompilerParams(vmem_limit_bytes=VMEM_LIMIT),
        cost_estimate=pl.CostEstimate(
            flops=heads * BLOCKS * 6 * BLK * BLK * 2560,
            bytes_accessed=32 << 20,
            transcendentals=heads * BLOCKS * 6 * BLK * BLK,
        ),
    )(info, qkv, knat, vnat, d_out, heads_out, lse, cosine, sine)


EPSILON = 1e-05
THETA = 130000.0
GROUPS = 4
CHUNKS = (4, 4, 3, 3)
ROW = ("x", "c")
TEAM = ("y", "x", "c")
EVERY = ("x", "c", "z", "y")


def flip(values, axis):
    return lax.ppermute(values, axis, [(0, 1), (1, 0)])


def pick(stack, index, axis=0):
    return lax.dynamic_index_in_dim(stack, index, axis, keepdims=False)


def in_order(mine, other, bit, axis):
    return jnp.where(
        bit == 0, jnp.stack([mine, other], axis), jnp.stack([other, mine], axis)
    )


def spread(pieces):
    x, c = lax.axis_index("x"), lax.axis_index("c")
    pieces = pieces.reshape((2, 2) + pieces.shape[1:])
    got = flip(pick(pieces, 1 - x), "x")
    pieces = in_order(pick(pieces, x), got, x, 0)
    got = flip(pick(pieces, 1 - c, 1), "c")
    pieces = in_order(pick(pieces, c, 1), got, c, 1)
    return pieces.reshape((4,) + pieces.shape[2:])


def row_gather(values):
    x, c = lax.axis_index("x"), lax.axis_index("c")
    pair = in_order(values, flip(values, "x"), x, 0)
    four = in_order(pair, flip(pair, "c"), c, 1)
    return four.reshape((4,) + values.shape)


def row_sum(values):
    values = values + flip(values, "x")
    return values + flip(values, "c")


def halves(values):
    middle = values.shape[0] // 2
    return values[:middle], values[middle:]


def team_gather(own):
    from_x, from_y = flip(own, "x"), flip(own, "y")
    former, latter = halves(from_y)[0], halves(from_x)[1]
    corner = jnp.concatenate([flip(former, "x"), flip(latter, "y")], 0)
    found = []
    for piece in (own, from_x, from_y, corner):
        found += [piece, flip(piece, "c")]
    return found


def team_scatter(pieces):
    got = flip(jnp.stack([pieces[k] for k in (1, 3, 5, 7)]), "c")
    sums = [pieces[2 * k].astype(F32) + got[k].astype(F32) for k in range(4)]
    low = [halves(s.astype(BF)) for s in sums[1:]]
    by_x = flip(jnp.stack([low[0][0], low[2][0]]), "x")
    by_y = flip(jnp.stack([low[1][1], low[2][1]]), "y")
    own = halves(sums[0])
    turn_y = flip((halves(sums[2])[0] + by_x[1].astype(F32)).astype(BF), "y")
    turn_x = flip((halves(sums[1])[1] + by_y[1].astype(F32)).astype(BF), "x")
    former = own[0] + by_x[0].astype(F32) + turn_y.astype(F32)
    latter = own[1] + by_y[0].astype(F32) + turn_x.astype(F32)
    return jnp.concatenate([former, latter], 0)


def norm_kernel(places, *refs):
    own, other, (gain, low, share, whole) = refs[:4], refs[4:8], refs[8:]
    half, row, rank = places[0], places[1], places[2]
    mine = pl.program_id(0) // (BLOCKS // 2) == half
    width = own[0].shape[1]

    def place(sources):
        for k, source in enumerate(sources):
            at = pl.multiple_of((row ^ k) * width, width)
            whole[:, pl.ds(at, width)] = source[...]

    @pl.when(mine)
    def _():
        place(own)

    @pl.when(jnp.logical_not(mine))
    def _():
        place(other)

    sub = share.shape[0]
    for k in range(BLK // sub):
        at = pl.multiple_of((rank ^ k) * sub, sub)
        rows = whole[pl.ds(at, sub), :]
        if k == 0:
            share[...] = rows
        if gain is None:
            low[k * sub : (k + 1) * sub, :] = rows
        else:
            wide = rows.astype(F32)
            scale = lax.rsqrt(jnp.sum(wide * wide, 1, keepdims=True) / wide.shape[1] + EPSILON)
            low[k * sub : (k + 1) * sub, :] = (wide * scale * gain[...]).astype(BF)


def plain_kernel(places, *refs):
    norm_kernel(places, *refs[:8], None, *refs[8:])


def assemble(places, pieces, gain, sub):
    per = BLOCKS // 2
    width = pieces[0].shape[1]
    whole = 4 * width

    def own_map(i, places):
        return jnp.where(i // per == places[0], i % per, 0), 0

    def other_map(i, places):
        return jnp.where(i // per == places[0], 0, i % per), 0

    ordered = [pieces[k] for k in range(8)]
    specs = [pl.BlockSpec((BLK, width), own_map)] * 4 + [pl.BlockSpec((BLK, width), other_map)] * 4
    if gain is not None:
        specs = specs + [pl.BlockSpec((1, whole), lambda i, places: (0, 0))]
        ordered = ordered + [gain.reshape(1, whole)]
    return pl.pallas_call(
        plain_kernel if gain is None else norm_kernel,
        grid_spec=pltpu.PrefetchScalarGridSpec(
            num_scalar_prefetch=1,
            grid=(BLOCKS,),
            in_specs=specs,
            out_specs=[
                pl.BlockSpec((BLK, whole), lambda i, places: (i, 0)),
                pl.BlockSpec((sub, whole), lambda i, places: (i, 0)),
            ],
            scratch_shapes=[pltpu.VMEM((BLK, whole), BF)],
        ),
        out_shape=[
            jax.ShapeDtypeStruct((GTOK, whole), BF),
            jax.ShapeDtypeStruct((BLOCKS * sub, whole), BF),
        ],
        compiler_params=pltpu.CompilerParams(vmem_limit_bytes=VMEM_LIMIT),
        cost_estimate=pl.CostEstimate(
            flops=GTOK * whole * 6, bytes_accessed=GTOK * whole * 5, transcendentals=0
        ),
    )(places, *ordered)


def straighten(values, rank):
    sub = values.shape[2]
    count = values.shape[1]
    return jnp.stack([pick(values, j ^ rank, 1) for j in range(count)], 1)


def local(
    quick,
    hidden_in,
    gain_before,
    query_weight,
    key_weight,
    value_weight,
    output_weight,
    gain_middle,
    gate_weight,
    up_weight,
    down_weight,
    cotangent,
    branch_points,
    lengths,
):
    width = hidden_in.shape[1]
    depth = 4 * width
    head_width = query_weight.shape[1]
    heads = head_width // HD
    units = gate_weight.shape[1]
    local_tokens = hidden_in.shape[0]
    team = 4 * lax.axis_size("y")
    sub = BLK // team
    x, c = lax.axis_index("x"), lax.axis_index("c")
    z, y = lax.axis_index("z"), lax.axis_index("y")
    row = 2 * x + c
    rank = 4 * y + row
    order = rank if quick else jnp.int32(0)
    branch_row = pick(branch_points, z)
    length_row = pick(lengths, z)
    info = jnp.concatenate(
        [branch_row, length_row, jnp.stack([order * sub, rank * sub, jnp.int32(0), jnp.int32(0)])]
    ).astype(jnp.int32)

    def join(pieces):
        blocks = pieces[0].shape[0] // sub
        return jnp.stack([p.reshape(blocks, sub, depth) for p in pieces], 1).reshape(-1, depth)

    def token_gather(share):
        if quick:
            return join(team_gather(share))
        blocks = share.shape[0] // sub
        got = lax.all_gather(share.reshape(blocks, sub, depth), TEAM, axis=1, tiled=False)
        return got.reshape(-1, depth)

    def token_scatter(partial):
        parts = partial.reshape(-1, team, sub, depth)
        if quick:
            return team_scatter([parts[:, k].reshape(-1, depth) for k in range(8)])
        parts = lax.psum_scatter(parts, TEAM, scatter_dimension=1, tiled=False)
        return parts.reshape(-1, depth).astype(F32)

    joined = jnp.stack([query_weight, key_weight, value_weight]).transpose(0, 2, 1)
    joined = jnp.concatenate([joined, output_weight[None]], 0)
    if heads % 4 == 0:
        per = heads // 4
        pieces = joined.reshape(4, 4, per * HD, width).transpose(1, 0, 2, 3)
        pieces = spread(pieces)
        pieces = pieces.reshape(4, 4, per, HD, width).transpose(2, 1, 3, 0, 4)
        pieces = pieces.reshape(per, 4 * HD, depth)
        attend_weights = lax.all_gather(pieces, "z", axis=0, tiled=True)
    else:
        pieces = lax.all_gather(joined, "z", axis=0, tiled=False)
        pieces = spread(pieces).reshape(4, 4, heads, HD, width).transpose(2, 1, 3, 0, 4)
        attend_weights = pieces.reshape(heads, 4 * HD, depth)
    join_weight = attend_weights[:, :ROWS].reshape(heads * ROWS, depth)
    out_weight = attend_weights[:, ROWS:].reshape(heads * HD, depth)

    def unit_rows(weight):
        pieces = spread(weight.reshape(4, units // 4, width))
        pieces = pieces.transpose(1, 0, 2).reshape(units // 4, depth)
        return lax.all_gather(pieces, "z", axis=0, tiled=True)

    gains = row_gather(jnp.stack([gain_before, gain_middle])).transpose(1, 0, 2).reshape(2, depth)
    gain_one, gain_two = gains[0], gains[1]

    places = jnp.stack([y, row, rank]).astype(jnp.int32)
    if quick:
        low_one, residual = assemble(places, team_gather(hidden_in), gain_one, sub)
        upstream_rows, upstream = assemble(places, team_gather(cotangent), None, sub)
    else:

        def full(values):
            values = lax.all_gather(values, "y", axis=0, tiled=True)
            return lax.all_gather(values, ROW, axis=1, tiled=True)

        def share_of(values):
            return pick(values.reshape(BLOCKS, team, sub, depth), rank, 1).reshape(-1, depth)

        hidden_rows = full(hidden_in)
        upstream_rows = full(cotangent)
        residual, upstream = share_of(hidden_rows), share_of(upstream_rows)
        wide = hidden_rows.astype(F32)
        scale = lax.rsqrt(jnp.mean(wide * wide, -1, keepdims=True) + EPSILON)
        low_one = (wide * scale * gain_one).astype(BF)

    gate_rows = unit_rows(gate_weight.T)
    up_rows = unit_rows(up_weight.T)
    down_rows = unit_rows(down_weight)
    gate_up_rows = jnp.concatenate([gate_rows, up_rows], 0)

    ids = jnp.arange(GTOK, dtype=jnp.int32)
    block_ids, slot_ids = ids // BLK, (ids % BLK) ^ (order * sub)
    starts = jnp.concatenate([jnp.arange(PBLKS, dtype=jnp.int32) * BLK, branch_row])
    positions = jnp.repeat(starts, BLK) + slot_ids
    frequency = THETA ** (-2.0 * jnp.arange(HD // 2, dtype=F32) / HD)
    angles = positions.astype(F32)[None, :] * frequency[:, None]
    cosine, sine = jnp.cos(angles), jnp.sin(angles)
    raw = mm(join_weight, low_one, NT).reshape(heads, 3, HD, GTOK)
    former, latter = raw[:, :2, : HD // 2], raw[:, :2, HD // 2 :]
    turned = jnp.concatenate([former * cosine - latter * sine, latter * cosine + former * sine], 2)
    qkv = jnp.concatenate([turned, raw[:, 2:]], 1).astype(BF)
    natural = qkv[:, 1:].transpose(1, 0, 3, 2)
    keys, values = natural[0], natural[1]
    qkv = qkv.reshape(heads * ROWS, GTOK)

    heads_parts, lse_parts, low_parts, d_low_parts, hidden_parts, d_unit_parts = [], [], [], [], [], []
    d_attention_parts, d_head_parts, out_parts = [], [], []
    middle_local = jnp.zeros((depth,), F32)
    squares = jnp.zeros((3,), F32)
    first = 0
    for count in CHUNKS:
        span = slice(first * BLK, (first + count) * BLK)
        shares = slice(first * sub, (first + count) * sub)
        head_part, lse = attend_forward(info, qkv, keys, heads, first, count)
        heads_parts.append(head_part)
        lse_parts.append(lse)
        partial = mm(head_part, out_weight, (((0,), (0,)), ((), ()))).astype(BF)
        attention = token_scatter(partial)
        middle = residual[shares].astype(F32) + attention
        scale_two = lax.rsqrt(jnp.mean(middle * middle, -1, keepdims=True) + EPSILON)
        norm_two = middle * scale_two
        low_two = token_gather((norm_two * gain_two).astype(BF))
        low_parts.append(low_two)
        gate = mm(low_two, gate_rows, NT)
        up = mm(low_two, up_rows, NT)
        sigma = jax.nn.sigmoid(gate)
        hidden = (gate * sigma * up).astype(BF)
        hidden_parts.append(hidden)
        d_hidden = mm(upstream_rows[span], down_rows, NT)
        d_gate = (d_hidden * up * sigma * (1.0 + gate * (1.0 - sigma))).astype(BF)
        d_up = (d_hidden * (gate * sigma)).astype(BF)
        d_units = jnp.concatenate([d_gate, d_up], 1)
        d_unit_parts.append(d_units)
        d_two = token_scatter(mm(d_units, gate_up_rows).astype(BF))
        middle_local += jnp.sum(d_two * norm_two, 0)
        scaled_two = d_two * gain_two
        inner_two = jnp.mean(scaled_two * norm_two, -1, keepdims=True)
        d_middle = upstream[shares].astype(F32) + scale_two * (scaled_two - norm_two * inner_two)
        d_attention = token_gather(d_middle.astype(BF))
        d_attention_parts.append(d_attention)
        d_head_parts.append(mm(out_weight, d_attention, NT).astype(BF))
        mixed = token_scatter(mm(hidden, down_rows).astype(BF))
        layer_out = (middle + mixed).astype(BF)
        out_parts.append(layer_out)
        here = first + jnp.arange(count, dtype=jnp.int32)
        bound = jnp.where(here < PBLKS, BLK, jnp.take(length_row, jnp.maximum(here - PBLKS, 0)))
        slots = rank * sub + jnp.arange(sub, dtype=jnp.int32)
        valid = (slots[None, :] < bound[:, None]).astype(F32).reshape(-1)
        wide = layer_out.astype(F32)
        squares += jnp.stack(
            [jnp.sum(valid * jnp.sum(v * v, -1)) for v in (wide, attention, d_middle)]
        )
        first += count

    low_two = jnp.concatenate(low_parts, 0)
    hidden = jnp.concatenate(hidden_parts, 0)
    d_units = jnp.concatenate(d_unit_parts, 0)
    d_attention = jnp.concatenate(d_attention_parts, 0)
    d_heads = jnp.concatenate(d_head_parts, 1)
    heads_out = jnp.concatenate(heads_parts, 1)
    lse = jnp.concatenate(lse_parts, 1)

    TN = (((0,), (0,)), ((), ()))

    def home(grad):
        part = lax.psum_scatter(grad, "z", scatter_dimension=0, tiled=True)
        part = part.reshape(part.shape[0], 4, width).transpose(1, 0, 2)
        return spread(part).reshape(-1, width)

    unit_grads = mm(d_units, low_two, TN).astype(BF)
    gate_grad = home(unit_grads[:units]).T.astype(F32)
    up_grad = home(unit_grads[units:]).T.astype(F32)
    down_grad = home(mm(hidden, upstream_rows, TN).astype(BF)).astype(F32)

    d_qkv, inner = attend_backward(
        info, qkv, keys, values, d_heads, heads_out, lse, cosine, sine, heads
    )
    partial = mm(d_qkv, join_weight, TN).astype(BF)
    join_grad = mm(d_qkv, low_one)
    before_local = jnp.sum(join_grad * join_weight.astype(F32), 0) / gain_one
    out_grad = mm(heads_out, d_attention)
    attend_grad = jnp.concatenate(
        [join_grad.reshape(heads, ROWS, depth), out_grad.reshape(heads, HD, depth)], 1
    ).astype(BF)
    if heads % 4 == 0:
        part = lax.psum_scatter(attend_grad, "z", scatter_dimension=0, tiled=True)
        part = part.reshape(heads // 4, 4, HD, 4, width).transpose(3, 1, 0, 2, 4)
        part = spread(part).transpose(1, 0, 2, 3, 4).reshape(4, head_width, width)
    else:
        part = attend_grad.reshape(heads, 4, HD, 4, width).transpose(3, 1, 0, 2, 4)
        part = spread(part.reshape(4, 4, heads * HD, width))
        part = lax.psum_scatter(part, "z", scatter_dimension=0, tiled=False)
    part = part.astype(F32)
    query_grad, key_grad, value_grad, output_grad = part[0].T, part[1].T, part[2].T, part[3]

    parts = partial.reshape(BLOCKS, team, sub, depth)
    inner = inner[0].reshape(BLOCKS, team, sub)
    d_middle = d_attention.reshape(BLOCKS, team, sub, depth)
    layer_out = jnp.concatenate(out_parts, 0)
    if quick:
        parts = straighten(parts, rank).reshape(2, -1, 4, width)
        pieces = []
        for k in range(8):
            piece = lax.dynamic_slice(
                parts,
                (y ^ (k >> 2), jnp.int32(0), row ^ (k & 3), jnp.int32(0)),
                (1, local_tokens, 1, width),
            )
            pieces.append(piece.reshape(local_tokens, width))
        d_one = team_scatter(pieces)
        inner = straighten(inner, rank).reshape(2, local_tokens)
        inner = row_sum(inner + flip(inner, "y"))
        inner = pick(inner, y)
        d_middle = lax.dynamic_slice(
            d_middle.reshape(2, BLOCKS // 2, team, sub, 4, width),
            (y, 0, 0, 0, row, 0),
            (1, BLOCKS // 2, team, sub, 1, width),
        ).reshape(BLOCKS // 2, team, sub, width)
        d_middle = straighten(d_middle, rank).reshape(local_tokens, width).astype(F32)
        layer_out = layer_out.reshape(2, local_tokens // team, 4, width).transpose(0, 2, 1, 3)
        layer_out = lax.all_to_all(
            layer_out.reshape(team, local_tokens // team, width), TEAM, 0, 0, tiled=True
        )
        layer_out = layer_out.reshape(team, BLOCKS // 2, sub, width).transpose(1, 0, 2, 3)
        layer_out = layer_out.reshape(local_tokens, width)
    else:
        d_one = lax.psum_scatter(
            parts.reshape(GTOK, depth), "y", scatter_dimension=0, tiled=True
        )
        d_one = lax.psum_scatter(d_one, ROW, scatter_dimension=1, tiled=True).astype(F32)
        inner = lax.psum(inner.reshape(GTOK), TEAM)
        inner = lax.dynamic_slice(inner, (y * local_tokens,), (local_tokens,))
        corner = (y * local_tokens, row * width)
        d_middle = lax.dynamic_slice(
            d_middle.reshape(GTOK, depth), corner, (local_tokens, width)
        ).astype(F32)
        layer_out = lax.all_gather(
            layer_out.reshape(BLOCKS, sub, depth), TEAM, axis=1, tiled=False
        ).reshape(GTOK, depth)
        layer_out = lax.dynamic_slice(layer_out, corner, (local_tokens, width))
    wide = hidden_in.astype(F32)
    scale_one = lax.rsqrt(row_sum(jnp.sum(wide * wide, -1)) / depth + EPSILON)[:, None]
    norm_one = wide * scale_one
    input_grad = d_middle + scale_one * (d_one * gain_before - norm_one * (inner / depth)[:, None])

    sums = lax.psum(jnp.concatenate([before_local, middle_local, squares]), EVERY)
    before_grad = lax.dynamic_slice(sums, (row * width,), (width,))
    middle_grad = lax.dynamic_slice(sums, (depth + row * width,), (width,))
    valid_count = (lengths.shape[0] * PROMPT + jnp.sum(lengths)).astype(F32)
    rms_values = jnp.sqrt(sums[2 * depth :] / (valid_count * depth))
    return (
        layer_out,
        input_grad,
        before_grad,
        query_grad,
        key_grad,
        value_grad,
        output_grad,
        middle_grad,
        gate_grad,
        up_grad,
        down_grad,
        rms_values,
    )


def solution(mesh):
    split = mesh.shape["col"] // GROUPS
    grid = Mesh(mesh.devices.reshape(2, 2, GROUPS, split), ("x", "c", "z", "y"))
    row, col = ("x", "c"), ("z", "y")
    return jax.shard_map(
        functools.partial(local, split == 2),
        mesh=grid,
        in_specs=(
            P(col, row),
            P(row),
            P(row, col),
            P(row, col),
            P(row, col),
            P(col, row),
            P(row),
            P(row, col),
            P(row, col),
            P(col, row),
            P(col, row),
            P(),
            P(),
        ),
        out_specs=(
            P(col, row),
            P(col, row),
            P(row),
            P(row, col),
            P(row, col),
            P(row, col),
            P(col, row),
            P(row),
            P(row, col),
            P(row, col),
            P(col, row),
            P(),
        ),
        check_vma=False,
    )
```

```python
import functools
import jax
import jax.numpy as jnp
from jax import lax
from jax.experimental import pallas as pl
from jax.experimental.pallas import tpu as pltpu
from jax.sharding import Mesh
from jax.sharding import PartitionSpec as P

HD = 64
PROMPT = 2048
CLEN = 256
CONTS = 6
GTOK = 3584
BLK = 256
PBLKS = PROMPT // BLK
BLOCKS = GTOK // BLK
ROWS = 3 * HD
BF = jnp.bfloat16
F32 = jnp.float32
LOW = -1e30
LOG2E = 1.4426950408889634
FACTOR = HD ** (-0.5) * LOG2E
VMEM_LIMIT = 56 * 1024 * 1024

NN = (((1,), (0,)), ((), ()))
NT = (((1,), (1,)), ((), ()))
TN = (((0,), (0,)), ((), ()))


def mm(a, b, dims=NN):
    return lax.dot_general(a, b, dims, preferred_element_type=F32)


def block_plan(info, block):
    cont = jnp.maximum(block - PBLKS, 0)
    is_cont = block >= PBLKS
    reach = info[cont]
    full = jnp.where(is_cont, reach // BLK, block)
    rest = jnp.where(is_cont, reach - full * BLK, 0)
    limit = jnp.where(is_cont, info[CONTS + cont], BLK)
    masked = 1 + (rest > 0).astype(jnp.int32)
    return full, rest, limit, masked


def local_ids(info, shape, axis):
    return lax.broadcasted_iota(jnp.int32, shape, axis) ^ info[2 * CONTS]


def masked_step(info, block, full, rest, limit, index):
    own = index == 0
    target = jnp.where(own, block, full)
    query_ids = local_ids(info, (1, BLK), 1)
    bound = jnp.where(own, jnp.minimum(query_ids + 1, limit), rest)
    key_ids = local_ids(info, (BLK, BLK), 0)
    return target, key_ids < bound


def columns(block):
    return pl.ds(pl.multiple_of(block * BLK, BLK), BLK)


def forward_kernel(heads, first, info, qkv, knat, out, lse, acc, top, tot):
    block = pl.program_id(0) + first
    full, rest, limit, masked = block_plan(info, block)
    here = columns(block)
    acc[...] = jnp.zeros_like(acc)
    top[...] = jnp.full_like(top, LOW)
    tot[...] = jnp.zeros_like(tot)

    def step(target, allowed, wide=1):
        span = pl.ds(pl.multiple_of(target * BLK, BLK), wide * BLK)
        weights, shrinks = [], []
        scores = [
            mm(knat[h, span, :], qkv[h * ROWS : h * ROWS + HD, here]) for h in range(heads)
        ]
        for h in range(heads):
            score = scores[h] * FACTOR
            if allowed is not None:
                score = jnp.where(allowed, score, LOW)
            old = top[h : h + 1, :]
            new = jnp.maximum(old, jnp.max(score, 0, keepdims=True))
            weight = jnp.exp2(score - new)
            shrink = jnp.exp2(old - new)
            top[h : h + 1, :] = new
            tot[h : h + 1, :] = tot[h : h + 1, :] * shrink + jnp.sum(weight, 0, keepdims=True)
            weights.append(weight.astype(BF))
            shrinks.append(shrink)
        for h in range(heads):
            value = qkv[h * ROWS + 2 * HD : (h + 1) * ROWS, span]
            acc[h] = acc[h] * shrinks[h] + mm(value, weights[h])

    def full_step(index, carry):
        step(index, None)
        return carry

    def mask_step(index, carry):
        target, allowed = masked_step(info, block, full, rest, limit, index)
        step(target, allowed)
        return carry

    def wide_step(index, carry):
        step(index * 4, None, 4)
        return carry

    lax.fori_loop(0, full // 4, wide_step, 0)
    lax.fori_loop(full // 4 * 4, full, full_step, 0)
    lax.fori_loop(0, masked, mask_step, 0)
    for h in range(heads):
        total = tot[h : h + 1, :]
        out[h * HD : (h + 1) * HD, :] = (acc[h] / total).astype(BF)
        lse[h : h + 1, :] = top[h : h + 1, :] + jnp.log2(total)


def attend_forward(info, qkv, knat, heads, first, count):
    pad = max(8, heads)
    return pl.pallas_call(
        functools.partial(forward_kernel, heads, first),
        grid=(count,),
        in_specs=[
            pl.BlockSpec(memory_space=pltpu.SMEM),
            pl.BlockSpec(qkv.shape, lambda i: (0, 0)),
            pl.BlockSpec(knat.shape, lambda i: (0, 0, 0)),
        ],
        out_specs=[
            pl.BlockSpec((heads * HD, BLK), lambda i: (0, i)),
            pl.BlockSpec((pad, BLK), lambda i: (0, i)),
        ],
        out_shape=[
            jax.ShapeDtypeStruct((heads * HD, count * BLK), BF),
            jax.ShapeDtypeStruct((pad, count * BLK), F32),
        ],
        scratch_shapes=[
            pltpu.VMEM((heads, HD, BLK), F32),
            pltpu.VMEM((pad, BLK), F32),
            pltpu.VMEM((pad, BLK), F32),
        ],
        compiler_params=pltpu.CompilerParams(vmem_limit_bytes=VMEM_LIMIT),
        cost_estimate=pl.CostEstimate(
            flops=heads * count * 6 * BLK * BLK * 2560,
            bytes_accessed=16 << 20,
            transcendentals=heads * count * 6 * BLK * BLK,
        ),
    )(info, qkv, knat)


def turn(values, cosine, sine, at):
    half = HD // 2
    cos, sin = cosine[:, at], sine[:, at]
    former, latter = values[:half], values[half:]
    return former * cos + latter * sin, latter * cos - former * sin


def backward_kernel(heads, first, final, info, qkv, knat, vnat, d_out, heads_out, lse, cosine, sine, *refs):
    if final:
        d_old_keys, d_old_values, d_old_query, old_inner, d_qkv, inner, d_keys, d_values, d_query = refs
    else:
        d_keys, d_values, d_turned, share_out, d_query = refs
    block = pl.program_id(0) + first
    full, rest, limit, masked = block_plan(info, block)
    here = columns(block)
    there = columns(pl.program_id(0))

    @pl.when(pl.program_id(0) == 0)
    def _():
        if final:
            d_keys[...] = d_old_keys[...]
            d_values[...] = d_old_values[...]
            inner[...] = jnp.zeros_like(inner)
        else:
            d_keys[...] = jnp.zeros_like(d_keys)
            d_values[...] = jnp.zeros_like(d_values)

    d_query[...] = jnp.zeros_like(d_query)
    deltas = []
    for h in range(heads):
        rows = slice(h * HD, (h + 1) * HD)
        deltas.append(
            jnp.sum(d_out[rows, there].astype(F32) * heads_out[rows, here].astype(F32), 0, keepdims=True)
        )

    def step(target, allowed, wide=1):
        span = pl.ds(pl.multiple_of(target * BLK, BLK), wide * BLK)
        for first in range(0, heads, 4):
            team = range(first, min(first + 4, heads))
            scores = [
                mm(knat[h, span, :], qkv[h * ROWS : h * ROWS + HD, here]) for h in team
            ]
            d_probs = [
                mm(vnat[h, span, :], d_out[h * HD : (h + 1) * HD, there]) for h in team
            ]
            low_probs, d_scores = [], []
            for h, score, d_prob in zip(team, scores, d_probs):
                score = score * FACTOR - lse[h : h + 1, here]
                if allowed is not None:
                    score = jnp.where(allowed, score, LOW)
                probs = jnp.exp2(score)
                low_probs.append(probs.astype(BF))
                d_scores.append((probs * (d_prob - deltas[h])).astype(BF))
            for h, low, d_score in zip(team, low_probs, d_scores):
                rows = slice(h * HD, (h + 1) * HD)
                query = qkv[h * ROWS : h * ROWS + HD, here]
                key = qkv[h * ROWS + HD : h * ROWS + 2 * HD, span]
                d_query[h] += mm(key, d_score)
                d_keys[rows, span] += mm(query, d_score, NT)
                d_values[rows, span] += mm(d_out[rows, there], low, NT)

    def full_step(index, carry):
        step(index, None)
        return carry

    def mask_step(index, carry):
        target, allowed = masked_step(info, block, full, rest, limit, index)
        step(target, allowed)
        return carry

    def wide_step(index, carry):
        step(index * 2, None, 2)
        return carry

    lax.fori_loop(0, full // 2, wide_step, 0)
    lax.fori_loop(full // 2 * 2, full, full_step, 0)
    lax.fori_loop(0, masked, mask_step, 0)

    half = HD // 2
    share = jnp.zeros((1, BLK), F32)
    for h in range(heads):
        start = h * ROWS
        values = d_query[h] * HD ** (-0.5)
        share += jnp.sum(values * qkv[start : start + HD, here].astype(F32), 0, keepdims=True)
        low, high = turn(values, cosine, sine, here)
        if final:
            d_qkv[start : start + half, here] = low.astype(BF)
            d_qkv[start + half : start + HD, here] = high.astype(BF)
        else:
            d_turned[h * HD : h * HD + half, :] = low.astype(BF)
            d_turned[h * HD + half : (h + 1) * HD, :] = high.astype(BF)
    if not final:
        share_out[0:1, :] = share
        return
    inner[0:1, here] = share

    @pl.when(block == PBLKS - 1)
    def _():
        inner[:, PROMPT:] = old_inner[...]
        for h in range(heads):
            d_qkv[h * ROWS : h * ROWS + HD, PROMPT:] = d_old_query[h * HD : (h + 1) * HD, :]

        def finish(index, carry):
            at = columns(index)
            share = inner[0:1, at]
            for h in range(heads):
                start = h * ROWS + HD
                rows = slice(h * HD, (h + 1) * HD)
                values = d_keys[rows, at] * HD ** (-0.5)
                share += jnp.sum(values * qkv[start : start + HD, at].astype(F32), 0, keepdims=True)
                low, high = turn(values, cosine, sine, at)
                d_qkv[start : start + half, at] = low.astype(BF)
                d_qkv[start + half : start + HD, at] = high.astype(BF)
                start += HD
                values = d_values[rows, at]
                share += jnp.sum(values * qkv[start : start + HD, at].astype(F32), 0, keepdims=True)
                d_qkv[start : start + HD, at] = values.astype(BF)
            inner[0:1, at] = share
            return carry

        lax.fori_loop(0, BLOCKS, finish, 0)


def attend_backward(info, operands, heads, before=None):
    whole = lambda a: pl.BlockSpec(a.shape, lambda i, n=len(a.shape): (0,) * n)
    final = before is not None
    operands = tuple(operands) + (tuple(before) if final else ())
    sums = jax.ShapeDtypeStruct((heads * HD, GTOK), F32)
    rest = GTOK - PROMPT
    if final:
        shapes = [jax.ShapeDtypeStruct((heads * ROWS, GTOK), BF), jax.ShapeDtypeStruct((8, GTOK), F32)]
        specs = [whole(a) for a in shapes]
        scratch = [pltpu.VMEM(sums.shape, F32), pltpu.VMEM(sums.shape, F32)]
    else:
        shapes = [sums, sums, jax.ShapeDtypeStruct((heads * HD, rest), BF), jax.ShapeDtypeStruct((8, rest), F32)]
        specs = [whole(sums), whole(sums)]
        specs += [
            pl.BlockSpec((heads * HD, BLK), lambda i: (0, i)),
            pl.BlockSpec((8, BLK), lambda i: (0, i)),
        ]
        scratch = []
    return pl.pallas_call(
        functools.partial(backward_kernel, heads, 0 if final else PBLKS, final),
        grid=(PBLKS if final else CONTS,),
        in_specs=[pl.BlockSpec(memory_space=pltpu.SMEM)] + [whole(a) for a in operands],
        out_specs=specs,
        out_shape=shapes,
        scratch_shapes=scratch + [pltpu.VMEM((heads, HD, BLK), F32)],
        compiler_params=pltpu.CompilerParams(vmem_limit_bytes=VMEM_LIMIT),
        cost_estimate=pl.CostEstimate(
            flops=heads * BLOCKS * 3 * BLK * BLK * 4096,
            bytes_accessed=32 << 20,
            transcendentals=heads * BLOCKS * 3 * BLK * BLK,
        ),
    )(info, *operands)


def project_kernel(heads, weight, low, cosine, sine, qkv, knat, vnat):
    raw = mm(weight[...], low[...], NT)
    half = HD // 2
    cos, sin = cosine[...], sine[...]
    for h in range(heads):
        for part in range(2):
            start = h * ROWS + part * HD
            former, latter = raw[start : start + half], raw[start + half : start + HD]
            turned = jnp.concatenate(
                [former * cos - latter * sin, latter * cos + former * sin], 0
            )
            qkv[start : start + HD, :] = turned.astype(BF)
            if part:
                knat[h] = turned.T.astype(BF)
        start = h * ROWS + 2 * HD
        value = raw[start : start + HD]
        qkv[start : start + HD, :] = value.astype(BF)
        vnat[h] = value.T.astype(BF)


def project(weight, low, cosine, sine, heads):
    depth = weight.shape[1]
    natural = jax.ShapeDtypeStruct((heads, GTOK, HD), BF)
    return pl.pallas_call(
        functools.partial(project_kernel, heads),
        grid=(BLOCKS,),
        in_specs=[
            pl.BlockSpec(weight.shape, lambda i: (0, 0)),
            pl.BlockSpec((BLK, depth), lambda i: (i, 0)),
            pl.BlockSpec((HD // 2, BLK), lambda i: (0, i)),
            pl.BlockSpec((HD // 2, BLK), lambda i: (0, i)),
        ],
        out_specs=[pl.BlockSpec((heads * ROWS, BLK), lambda i: (0, i))]
        + [pl.BlockSpec((heads, BLK, HD), lambda i: (0, i, 0))] * 2,
        out_shape=[jax.ShapeDtypeStruct((heads * ROWS, GTOK), BF), natural, natural],
        compiler_params=pltpu.CompilerParams(vmem_limit_bytes=VMEM_LIMIT),
        cost_estimate=pl.CostEstimate(
            flops=2 * GTOK * depth * heads * ROWS, bytes_accessed=3 * GTOK * depth, transcendentals=0
        ),
    )(weight, low, cosine, sine)


EPSILON = 1e-05
THETA = 130000.0
GROUPS = 4
CHUNKS = ((8, 3), (11, 3), (0, 4), (4, 4))
ROW = ("x", "c")
TEAM = ("y", "x", "c")
EVERY = ("x", "c", "z", "y")


def after(values, *earlier):
    return lax.optimization_barrier((values, earlier))[0]


def flip(values, axis):
    return lax.ppermute(values, axis, [(0, 1), (1, 0)])


def send(values, axis):
    if axis == "z1":
        return lax.ppermute(values, "z", [(0, 1), (1, 0), (2, 3), (3, 2)])
    if axis == "z2":
        return lax.ppermute(values, "z", [(0, 2), (1, 3), (2, 0), (3, 1)])
    return flip(values, axis)


def pick(stack, index, axis=0):
    return lax.dynamic_index_in_dim(stack, index, axis, keepdims=False)


def in_order(mine, other, bit, axis):
    return jnp.where(
        bit == 0, jnp.stack([mine, other], axis), jnp.stack([other, mine], axis)
    )


def spread_steps(pieces):
    x, c = lax.axis_index("x"), lax.axis_index("c")
    pieces = pieces.reshape((2, 2) + pieces.shape[1:])
    (got,) = yield [(pick(pieces, 1 - x), "x")]
    pieces = in_order(pick(pieces, x), got, x, 0)
    (got,) = yield [(pick(pieces, 1 - c, 1), "c")]
    pieces = in_order(pick(pieces, c, 1), got, c, 1)
    return pieces.reshape((4,) + pieces.shape[2:])


def complete(steps):
    try:
        wanted = next(steps)
        while True:
            wanted = steps.send([flip(*w) for w in wanted])
    except StopIteration as end:
        return end.value


def spread(pieces):
    return complete(spread_steps(pieces))


class Lines:
    def __init__(self):
        self.wanted = {}
        self.flying = {}
        self.results = {}
        self.last = []
        self.extra = []

    def start(self, name, steps):
        self.wanted[name] = (steps, next(steps))

    def launch(self, name):
        steps, wanted = self.wanted.pop(name)
        wanted = [(after(v, *self.last) if self.last else v, axis) for v, axis in wanted]
        self.extra += [v for v, _ in wanted]
        self.flying[name] = (steps, [send(v, axis) for v, axis in wanted])

    def land(self, name):
        steps, got = self.flying.pop(name)
        self.proceed(name, steps, after(got, *self.last))

    def proceed(self, name, steps, got):
        try:
            self.wanted[name] = (steps, steps.send(got))
        except StopIteration as end:
            self.results[name] = end.value
            value = end.value[-1] if isinstance(end.value, list) else end.value
            if value is not None:
                self.extra.append(value)

    def tick(self, large, *names):
        if large is None:
            for name in names:
                steps, wanted = self.wanted.pop(name)
                wanted = [(after(v, *self.last) if self.last else v, axis) for v, axis in wanted]
                self.proceed(name, steps, [send(*w) for w in wanted])
            return None
        sent = {}
        for name in names:
            steps, wanted = self.wanted.pop(name)
            sent[name] = (steps, [(after(v, *self.last) if self.last else v, axis) for v, axis in wanted])
        operands = [v for _, part in sent.values() for v, _ in part]
        done = large(self.last + self.extra + operands)
        self.extra = []
        self.last = [done[0] if isinstance(done, (tuple, list)) else done]
        for name, (steps, wanted) in sent.items():
            self.proceed(name, steps, after([send(*w) for w in wanted], *self.last))
        return done


def row_gather(values):
    x, c = lax.axis_index("x"), lax.axis_index("c")
    pair = in_order(values, flip(values, "x"), x, 0)
    four = in_order(pair, flip(pair, "c"), c, 1)
    return four.reshape((4,) + values.shape)


def row_sum(values):
    values = values + flip(values, "x")
    return values + flip(values, "c")


def halves(values):
    middle = values.shape[0] // 2
    return values[:middle], values[middle:]


def place_steps(own):
    from_x, from_y, from_c = yield [(own, "x"), (own, "y"), (own, "c")]
    former, latter, by_x, by_y = yield [
        (halves(from_y)[0], "x"),
        (halves(from_x)[1], "y"),
        (from_x, "c"),
        (from_y, "c"),
    ]
    corner = jnp.concatenate([former, latter], 0)
    (other,) = yield [(corner, "c")]
    return [own, from_c, from_x, by_x, from_y, by_y, corner, other]


def gather_steps(own):
    from_x, from_y = yield [(own, "x"), (own, "y")]
    former, latter = yield [(halves(from_y)[0], "x"), (halves(from_x)[1], "y")]
    four = jnp.concatenate([own, from_x, from_y, former, latter], 0)
    (other,) = yield [(four, "c")]
    return [four, other]


def sum_steps(keep, send):
    (got,) = yield [(send, "c")]
    sums = [halves(keep[k].astype(F32) + got[k].astype(F32)) for k in range(4)]
    to_x = jnp.stack([sums[1][0], sums[3][0]]).astype(BF)
    to_y = jnp.stack([sums[2][1], sums[3][1]]).astype(BF)
    by_x, by_y = yield [(to_x, "x"), (to_y, "y")]
    over_y = (sums[2][0] + by_x[1].astype(F32)).astype(BF)
    over_x = (sums[1][1] + by_y[1].astype(F32)).astype(BF)
    former = sums[0][0] + by_x[0].astype(F32)
    latter = sums[0][1] + by_y[0].astype(F32)
    by_y, by_x = yield [(over_y, "y"), (over_x, "x")]
    return jnp.concatenate([former + by_y.astype(F32), latter + by_x.astype(F32)], 0)


def norm_kernel(mode, heads, places, *refs):
    own, other, refs = refs[:4], refs[4:8], refs[8:]
    if mode:
        gain, weight, cosine, sine, low, share, qkv, knat, vnat, whole = refs
    else:
        low, share, whole = refs
    half, row, rank = places[0], places[1], places[2]
    mine = pl.program_id(0) // (BLOCKS // 2) == half
    width = own[0].shape[1]

    def place(sources):
        for k, source in enumerate(sources):
            at = pl.multiple_of((row ^ k) * width, width)
            whole[:, pl.ds(at, width)] = source[...]

    @pl.when(mine)
    def _():
        place(own)

    @pl.when(jnp.logical_not(mine))
    def _():
        place(other)

    sub = share.shape[0]
    for k in range(BLK // sub):
        at = pl.multiple_of((rank ^ k) * sub, sub)
        rows = whole[pl.ds(at, sub), :]
        if k == 0:
            share[...] = rows
        if not mode:
            low[k * sub : (k + 1) * sub, :] = rows
        else:
            wide = rows.astype(F32)
            scale = lax.rsqrt(jnp.sum(wide * wide, 1, keepdims=True) / wide.shape[1] + EPSILON)
            low[k * sub : (k + 1) * sub, :] = (wide * scale * gain[...]).astype(BF)
    if mode:
        project_kernel(heads, weight, low, cosine, sine, qkv, knat, vnat)


def assemble(places, pieces, gain, sub, projection=(), heads=0):
    per = BLOCKS // 2
    width = pieces[0].shape[1]
    whole = 4 * width
    mode = gain is not None

    def own_map(i, places):
        return jnp.where(i // per == places[0], i % per, 0), 0

    def other_map(i, places):
        return jnp.where(i // per == places[0], 0, i % per), 0

    operands = list(pieces)
    specs = [pl.BlockSpec((BLK, width), own_map)] * 4 + [pl.BlockSpec((BLK, width), other_map)] * 4
    outs = [pl.BlockSpec((BLK, whole), lambda i, p: (i, 0)), pl.BlockSpec((sub, whole), lambda i, p: (i, 0))]
    shapes = [jax.ShapeDtypeStruct((GTOK, whole), BF), jax.ShapeDtypeStruct((BLOCKS * sub, whole), BF)]
    flops = 0
    if mode:
        table = pl.BlockSpec((HD // 2, BLK), lambda i, p: (0, i))
        specs += [pl.BlockSpec((1, whole), lambda i, p: (0, 0))]
        specs += [pl.BlockSpec(projection[0].shape, lambda i, p: (0, 0)), table, table]
        operands += [gain.reshape(1, whole), *projection]
        outs += [pl.BlockSpec((heads * ROWS, BLK), lambda i, p: (0, i))]
        outs += [pl.BlockSpec((heads, BLK, HD), lambda i, p: (0, i, 0))] * 2
        natural = jax.ShapeDtypeStruct((heads, GTOK, HD), BF)
        shapes += [jax.ShapeDtypeStruct((heads * ROWS, GTOK), BF), natural, natural]
        flops = 2 * GTOK * whole * heads * ROWS
    return pl.pallas_call(
        functools.partial(norm_kernel, mode, heads),
        grid_spec=pltpu.PrefetchScalarGridSpec(
            num_scalar_prefetch=1,
            grid=(BLOCKS,),
            in_specs=specs,
            out_specs=outs,
            scratch_shapes=[pltpu.VMEM((BLK, whole), BF)],
        ),
        out_shape=shapes,
        compiler_params=params(),
        cost_estimate=cost(flops + GTOK * whole * 6, GTOK * whole * 5),
    )(places, *operands)


def straighten(values, rank):
    count = values.shape[1]
    return jnp.stack([pick(values, j ^ rank, 1) for j in range(count)], 1)


def whole_spec(shape):
    return pl.BlockSpec(shape, lambda *i, n=len(shape): (0,) * n)


def cost(flops, bytes_accessed, transcendentals=0):
    return pl.CostEstimate(
        flops=int(flops), bytes_accessed=int(bytes_accessed), transcendentals=int(transcendentals)
    )


def params():
    return pltpu.CompilerParams(vmem_limit_bytes=VMEM_LIMIT)


def split_kernel(pairs, form, sub, *refs):
    keep, send = refs[2 * pairs :]
    total = mm(refs[0][...], refs[1][...], form)
    for p in range(1, pairs):
        total += mm(refs[2 * p][...], refs[2 * p + 1][...], form)
    low = total.astype(BF)
    for b in range(low.shape[0] // BLK):
        for k in range(8):
            target = send if k % 2 else keep
            start = b * BLK + k * sub
            target[k // 2, b * sub : (b + 1) * sub, :] = low[start : start + sub]


def split_product(pairs, form):
    width = pairs[0][1].shape[1]
    rows = pairs[0][0].shape[1 if form == TN else 0]
    depth = pairs[0][1].shape[0]
    tile = 512
    sub = BLK // 8
    specs, operands = [], []
    for left, right in pairs:
        specs += [whole_spec(left.shape), pl.BlockSpec((depth, tile), lambda j: (0, j))]
        operands += [left, right]
    shape = (4, rows // 8, width)
    return pl.pallas_call(
        functools.partial(split_kernel, len(pairs), form, sub),
        grid=(width // tile,),
        in_specs=specs,
        out_specs=[pl.BlockSpec((4, rows // 8, tile), lambda j: (0, 0, j))] * 2,
        out_shape=[jax.ShapeDtypeStruct(shape, BF)] * 2,
        compiler_params=params(),
        cost_estimate=cost(
            2 * rows * depth * width * len(pairs),
            2 * (rows * width + (rows + width) * depth * len(pairs)),
        ),
    )(*operands)


def mix_kernel(parts, sub, *refs):
    weight, keep, send = refs[parts:]
    at = 0
    for left in refs[:parts]:
        low = mm(left[...], weight[...]).astype(BF)
        for b in range(low.shape[0] // BLK):
            for k in range(8):
                target = send if k % 2 else keep
                start = b * BLK + k * sub
                target[k // 2, at : at + sub, :] = low[start : start + sub]
            at += sub


def mix_product(parts, weight):
    width = weight.shape[1]
    rows = sum(a.shape[0] for a in parts)
    tile = 256
    return pl.pallas_call(
        functools.partial(mix_kernel, len(parts), BLK // 8),
        grid=(width // tile,),
        in_specs=[whole_spec(a.shape) for a in parts]
        + [pl.BlockSpec((weight.shape[0], tile), lambda j: (0, j))],
        out_specs=[pl.BlockSpec((4, rows // 8, tile), lambda j: (0, 0, j))] * 2,
        out_shape=[jax.ShapeDtypeStruct((4, rows // 8, width), BF)] * 2,
        compiler_params=params(),
        cost_estimate=cost(2 * rows * weight.size, 2 * (rows * width + rows * weight.shape[0])),
    )(*parts, weight)


def join_rows(pieces, target):
    if len(pieces) == 1:
        target[...] = pieces[0][...]
        return
    blocks = target.shape[0] // BLK
    sub = BLK // 8
    for b in range(blocks):
        for k in range(8):
            start = b * BLK + k * sub
            source = ((k // 2) * blocks + b) * sub
            target[start : start + sub, :] = pieces[k % 2][source : source + sub, :]


def unit_kernel(count, *refs):
    pieces, (gates, ups, low, gate_out, up_out, hidden) = refs[:count], refs[count:]

    @pl.when(pl.program_id(0) == 0)
    def _():
        join_rows(pieces, low)

    rows = low[...]
    gate = mm(rows, gates[...], NT)
    up = mm(rows, ups[...], NT)
    gate_out[...] = gate.astype(BF)
    up_out[...] = up.astype(BF)
    hidden[...] = (gate * jax.nn.sigmoid(gate) * up).astype(BF)


def unit_products(pieces, gates, ups):
    rows = sum(p.shape[0] for p in pieces)
    units, depth = gates.shape
    tile = min(units, 256)
    weight = pl.BlockSpec((tile, depth), lambda j: (j, 0))
    result = pl.BlockSpec((rows, tile), lambda j: (0, j))
    return pl.pallas_call(
        functools.partial(unit_kernel, len(pieces)),
        grid=(units // tile,),
        in_specs=[whole_spec(p.shape) for p in pieces] + [weight, weight],
        out_specs=[whole_spec((rows, depth)), result, result, result],
        out_shape=[jax.ShapeDtypeStruct((rows, depth), BF)]
        + [jax.ShapeDtypeStruct((rows, units), BF)] * 3,
        compiler_params=params(),
        cost_estimate=cost(4 * rows * depth * units, 4 * depth * (rows + units), rows * units),
    )(*pieces, gates, ups)


def unit_grad_kernel(upstream, downs, gate_in, up_in, d_gate, d_up):
    d_hidden = mm(upstream[...], downs[...], NT)
    gate, up = gate_in[...].astype(F32), up_in[...].astype(F32)
    sigma = jax.nn.sigmoid(gate)
    silu = gate * sigma
    d_gate[...] = (d_hidden * up * (sigma + silu * (1.0 - sigma))).astype(BF)
    d_up[...] = (d_hidden * silu).astype(BF)


def unit_grads(upstream, first, rows, downs, gate, up):
    units, depth = downs.shape
    tile = min(units, 256)
    result = pl.BlockSpec((rows, tile), lambda j: (0, j))
    return pl.pallas_call(
        unit_grad_kernel,
        grid=(units // tile,),
        in_specs=[
            pl.BlockSpec((pl.Element(rows), pl.Element(depth)), lambda j: (first, 0)),
            pl.BlockSpec((tile, depth), lambda j: (j, 0)),
            result,
            result,
        ],
        out_specs=[result, result],
        out_shape=[jax.ShapeDtypeStruct((rows, units), BF)] * 2,
        compiler_params=params(),
        cost_estimate=cost(2 * rows * depth * units, 4 * depth * (rows + units), rows * units),
    )(upstream, downs, gate, up)


def head_kernel(count, *refs):
    pieces, (weight, joined, result) = refs[:count], refs[count:]
    join_rows(pieces, joined)
    result[...] = mm(weight[...], joined[...], NT).astype(BF)


def head_product(pieces, weight):
    depth = weight.shape[1]
    rows = sum(p.shape[0] for p in pieces)
    return pl.pallas_call(
        functools.partial(head_kernel, len(pieces)),
        out_shape=[
            jax.ShapeDtypeStruct((rows, depth), BF),
            jax.ShapeDtypeStruct((weight.shape[0], rows), BF),
        ],
        compiler_params=params(),
        cost_estimate=cost(2 * rows * depth * weight.shape[0], 4 * rows * depth),
    )(*pieces, weight)


def grad_kernel(parts, form, starts, *refs):
    rights = refs[parts:-1]
    total = None
    for p in range(parts):
        left = refs[p][...]
        if starts:
            count = left.shape[0]
            right = rights[0][starts[p] : starts[p] + count, :]
        else:
            right = rights[p][...]
        term = mm(left, right, form)
        total = term if total is None else total + term
    refs[-1][...] = total.astype(BF)


def grad_product(lefts, rights, form=TN, starts=()):
    rows = lefts[0].shape[1 if form == TN else 0]
    width = rights[0].shape[1]
    tile = 512
    tokens = sum(r.shape[0] for r in rights)
    return pl.pallas_call(
        functools.partial(grad_kernel, len(lefts), form, starts),
        grid=(width // tile,),
        in_specs=[whole_spec(a.shape) for a in lefts]
        + [pl.BlockSpec((b.shape[0], tile), lambda j: (0, j)) for b in rights],
        out_specs=pl.BlockSpec((rows, tile), lambda j: (0, j)),
        out_shape=jax.ShapeDtypeStruct((rows, width), BF),
        compiler_params=params(),
        cost_estimate=cost(2 * rows * width * tokens, 2 * tokens * (rows + width)),
    )(*lefts, *rights)


def last_kernel(places, d_qkv, weight, keep, send, whole):
    row, rank = places[1], places[2]
    sub = BLK // 8
    width = keep.shape[2]
    whole[...] = mm(d_qkv[...], weight[...], TN).astype(BF)
    for k in range(8):
        at = pl.ds(pl.multiple_of((rank ^ k) * sub, sub), sub)
        for j in range(4):
            target = send if j % 2 else keep
            source = pl.ds(pl.multiple_of((row ^ j) * width, width), width)
            target[j // 2, at, :] = whole[k * sub : (k + 1) * sub, source]


def last_product(places, d_qkv, weight):
    depth = weight.shape[1]
    per = BLOCKS // 2

    def out_map(i, places):
        return ((i // per) ^ places[0], i % per, 0)

    return pl.pallas_call(
        last_kernel,
        grid_spec=pltpu.PrefetchScalarGridSpec(
            num_scalar_prefetch=1,
            grid=(BLOCKS,),
            in_specs=[
                pl.BlockSpec((d_qkv.shape[0], BLK), lambda i, places: (0, i)),
                pl.BlockSpec(weight.shape, lambda i, places: (0, 0)),
            ],
            out_specs=[pl.BlockSpec((2, BLK, depth // 4), out_map)] * 2,
            scratch_shapes=[pltpu.VMEM((BLK, depth), BF)],
        ),
        out_shape=[jax.ShapeDtypeStruct((4, GTOK // 2, depth // 4), BF)] * 2,
        compiler_params=params(),
        cost_estimate=cost(2 * GTOK * depth * d_qkv.shape[0], 2 * GTOK * depth),
    )(places, d_qkv, weight)


def columns_of(values, count, width):
    return jnp.stack([values[..., k * width : (k + 1) * width] for k in range(count)])


def local(
    quick,
    hidden_in,
    gain_before,
    query_weight,
    key_weight,
    value_weight,
    output_weight,
    gain_middle,
    gate_weight,
    up_weight,
    down_weight,
    cotangent,
    branch_points,
    lengths,
):
    width = hidden_in.shape[1]
    depth = 4 * width
    head_width = query_weight.shape[1]
    heads = head_width // HD
    units = gate_weight.shape[1]
    local_tokens = hidden_in.shape[0]
    team = 4 * lax.axis_size("y")
    sub = BLK // team
    x, c = lax.axis_index("x"), lax.axis_index("c")
    z, y = lax.axis_index("z"), lax.axis_index("y")
    row = 2 * x + c
    rank = 4 * y + row
    order = rank if quick else jnp.int32(0)
    branch_row = pick(branch_points, z)
    length_row = pick(lengths, z)
    info = jnp.concatenate([branch_row, length_row, jnp.stack([order * sub])]).astype(jnp.int32)
    places = jnp.stack([y, row, rank]).astype(jnp.int32)

    def full_gather(share):
        blocks = share.shape[0] // sub
        got = lax.all_gather(share.reshape(blocks, sub, depth), TEAM, axis=1, tiled=False)
        return [got.reshape(-1, depth)]

    def full_scatter(partial):
        parts = partial.reshape(-1, team, sub, depth)
        parts = lax.psum_scatter(parts, TEAM, scatter_dimension=1, tiled=False)
        return parts.reshape(-1, depth).astype(F32)

    lines = Lines()
    tick = lines.tick

    joined = jnp.stack([query_weight.T, key_weight.T, value_weight.T, output_weight])
    if heads % 4 == 0:
        per = heads // 4
        pieces = joined.reshape(4, 4, per * HD, width).transpose(1, 0, 2, 3)
        if quick:
            from_y = flip(hidden_in, "y")
            lines.start("heads", spread_steps(pieces))
            tick(None, "heads")
            from_x = flip(after(hidden_in, lines.wanted["heads"][1][0][0]), "x")
            tick(None, "heads")
            pieces = lines.results["heads"]
        else:
            pieces = spread(pieces)
        pieces = jnp.concatenate([pieces[k] for k in range(4)], -1)
        pieces = pieces.reshape(4, per, HD, depth).transpose(1, 0, 2, 3).reshape(per, 4 * HD, depth)
        attend_weights = lax.all_gather(pieces, "z", axis=0, tiled=True)
    else:
        pieces = lax.all_gather(joined, "z", axis=0, tiled=False)
        pieces = spread(pieces).reshape(4, 4, heads, HD, width).transpose(2, 1, 3, 0, 4)
        attend_weights = pieces.reshape(heads, 4 * HD, depth)
    join_weight = attend_weights[:, :ROWS].reshape(heads * ROWS, depth)
    out_weight = attend_weights[:, ROWS:].reshape(heads * HD, depth)

    def unit_rows(weight):
        pieces = yield from spread_steps(weight.reshape(4, units // 4, width))
        pieces = jnp.concatenate([pieces[k] for k in range(4)], 1)
        if quick:
            lines.extra.append(pieces)
        return [lax.all_gather(pieces, "z", axis=0, tiled=True), pieces]

    gains = row_gather(after(jnp.stack([gain_before, gain_middle]), pieces))
    gains = gains.transpose(1, 0, 2).reshape(2, depth)
    gain_one, gain_two = gains[0], gains[1]

    ids = jnp.arange(GTOK, dtype=jnp.int32)
    slot_ids = (ids % BLK) ^ (order * sub)
    starts = jnp.concatenate([jnp.arange(PBLKS, dtype=jnp.int32) * BLK, branch_row])
    positions = jnp.repeat(starts, BLK) + slot_ids
    frequency = THETA ** (-2.0 * jnp.arange(HD // 2, dtype=F32) / HD)
    angles = positions.astype(F32)[None, :] * frequency[:, None]
    cosine, sine = jnp.cos(angles), jnp.sin(angles)

    steps = range(len(CHUNKS))
    ordered = sorted(steps, key=lambda k: CHUNKS[k][0])
    rows_of = [count * BLK for _, count in CHUNKS]
    shares = [slice(first * sub, (first + count) * sub) for first, count in CHUNKS]
    starts = tuple(first * BLK for first, _ in CHUNKS)
    conts = [k for k in ordered if CHUNKS[k][0] >= PBLKS]
    prompts = [k for k in ordered if CHUNKS[k][0] < PBLKS]
    attentions, middles, scales, norms, d_middles, notes = ({} for _ in range(6))
    attended, d_heads = {}, {}

    def to_middle(k, attention):
        middle = residual[shares[k]].astype(F32) + attention
        scale_two = lax.rsqrt(jnp.mean(middle * middle, -1, keepdims=True) + EPSILON)
        norm_two = middle * scale_two
        attentions[k], middles[k], scales[k], norms[k] = attention, middle, scale_two, norm_two
        return (norm_two * gain_two).astype(BF)

    def to_d_middle(k, d_two):
        notes[k] = jnp.sum(d_two * norms[k], 0)
        scaled_two = d_two * gain_two
        inner_two = jnp.mean(scaled_two * norms[k], -1, keepdims=True)
        d_middle = upstream[shares[k]].astype(F32) + scales[k] * (scaled_two - norms[k] * inner_two)
        d_middles[k] = d_middle
        return d_middle.astype(BF)

    def backward(parts, ties, before=None):
        d_out = jnp.concatenate([d_heads[k] for k in parts], 1)
        heads_out = jnp.concatenate([heads_parts[k] for k in ordered], 1)
        lse = jnp.concatenate([lse_parts[k] for k in ordered], 1)
        source = after(qkv, *ties) if ties else qkv
        operands = (source, keys, values, d_out, heads_out, lse, cosine, sine)
        return attend_backward(info, operands, heads, before)

    def total(grad):
        return lax.psum_scatter(grad, "z", scatter_dimension=0, tiled=True)

    def home_steps(part):
        part = yield from spread_steps(columns_of(part, 4, width))
        return part.reshape(-1, width)

    def outcome(mixed, join_grad):
        layer_out = (jnp.concatenate([middles[k] for k in ordered], 0) + mixed).astype(BF)
        here = jnp.arange(BLOCKS, dtype=jnp.int32)
        bound = jnp.where(here < PBLKS, BLK, jnp.take(length_row, jnp.maximum(here - PBLKS, 0)))
        slots = rank * sub + jnp.arange(sub, dtype=jnp.int32)
        valid = (slots[None, :] < bound[:, None]).astype(F32).reshape(-1)

        def square_sum(part, weights):
            return jnp.sum(weights * jnp.sum(part * part, -1))

        squares = jnp.stack(
            [square_sum(layer_out.astype(F32), valid)]
            + [
                sum(square_sum(parts[k], valid[shares[k]]) for k in steps)
                for parts in (attentions, d_middles)
            ]
        )
        before_local = jnp.sum(join_grad * join_weight.astype(F32), 0) / gain_one
        middle_local = sum(notes[k] for k in steps)
        return layer_out, jnp.concatenate([before_local, middle_local, squares])

    heads_parts, lse_parts, lows, gates, ups, hiddens = ([] for _ in range(6))
    gate_parts, up_parts = [], []
    if quick:
        former, latter = flip(halves(from_y)[0], "x"), flip(halves(from_x)[1], "y")
        corner = jnp.concatenate([former, latter], 0)
        four = [hidden_in, from_x, from_y, corner]
        hidden_pieces = [p for piece in four for p in (piece, flip(piece, "c"))]
        lines.start("gate", unit_rows(after(gate_weight, corner).T))
        lines.start("up", unit_rows(up_weight.T))
        lines.start("down", unit_rows(down_weight))
        lines.start("late", place_steps(after(cotangent, corner)))
        lines.launch("late")
        low_one, residual, qkv, keys, values = tick(
            lambda ties: assemble(
                places,
                after(hidden_pieces, *ties),
                gain_one,
                sub,
                (join_weight, cosine, sine),
                heads,
            ),
            "gate",
        )

        def forward_line(k, partial):
            low = to_middle(k, (yield from sum_steps(*partial)))
            return (yield from gather_steps(low))

        def attend(k, *names):
            def large(ties):
                return attend_forward(info, after(qkv, *ties), keys, heads, *CHUNKS[k])

            head_part, lse = tick(large, *names)
            heads_parts.append(head_part)
            lse_parts.append(lse)
            partial = split_product([(head_part, out_weight)], TN)
            lines.last = [partial[0]]
            lines.start(k, forward_line(k, partial))

        attend(0, "gate", "up")
        lines.land("late")
        attend(1, 0, "late")
        attend(2, 0, 1, "up", "late")
        attend(3, 0, 1, 2)
        gate_rows, up_rows = lines.results["gate"][0], lines.results["up"][0]
        upstream_rows, upstream = tick(
            lambda ties: assemble(places, after(lines.results["late"], *ties), None, sub), 0, 1, 3
        )

        def unit(k, *names):
            def large(ties):
                return unit_products(after(lines.results[k], *ties), gate_rows, up_rows)

            low, gate, up, hidden = tick(large, *names)
            lows.append(low)
            gates.append(gate)
            ups.append(up)
            hiddens.append(hidden)

        tick(None, 0, 2, "down")
        tick(None, 0, 1, 2, "down")
        down_rows = lines.results["down"][0]
        unit(0, 1, 3)
        tick(None, 1, 2)
        unit(1, 2, 3)
        tick(None, 2, 3)
        unit(2, 3)
        tick(None, 3)
        unit(3)
        down_grad = tick(lambda ties: grad_product(hiddens, [after(upstream_rows, *ties)], TN, starts))
        down_sum = total(down_grad)

        def backward_line(k, partial):
            low = to_d_middle(k, (yield from sum_steps(*partial)))
            pieces = yield from gather_steps(low)
            attended[k], d_heads[k] = head_product(pieces, out_weight)
            return d_heads[k]

        def unit_grad(k, first, second):
            def large(ties):
                source = after(gates[k], *ties)
                return unit_grads(upstream_rows, starts[k], rows_of[k], down_rows, source, ups[k])

            d_gate, d_up = tick(large, *first)
            gate_parts.append(d_gate)
            up_parts.append(d_up)

            def more(ties):
                return split_product([(after(d_gate, *ties), gate_rows), (d_up, up_rows)], NN)

            lines.start(k, backward_line(k, tick(more, *second)))

        unit_grad(0, (), ())
        unit_grad(1, (0,), (0,))
        unit_grad(2, (0, 1), (0, 1))
        unit_grad(3, (0, 1, 2), (0, 1, 2))
        def summed(values, axes):
            for axis in axes:
                (got,) = yield [(values, axis)]
                values = values + got
            return values

        gate_grad = tick(lambda ties: grad_product(after(gate_parts, *ties), lows), 1, 2, 3)
        gate_sum = total(gate_grad)
        mixed = tick(
            lambda ties: mix_product(after([hiddens[k] for k in ordered], *ties), down_rows),
            1,
            2,
            3,
        )
        lines.start("mixed", sum_steps(*mixed))
        before = tick(lambda ties: backward(conts, ties), 2, 3, "mixed")
        lines.start("down", home_steps(down_sum))
        up_grad = tick(lambda ties: grad_product(after(up_parts, *ties), lows), 2, 3, "down")
        up_sum = total(up_grad)
        tick(None, 3)
        tick(None, 3)
        lines.start("gate", home_steps(gate_sum))
        d_qkv, inner = tick(lambda ties: backward(prompts, ties, before), "mixed", "down", "gate")
        inner = straighten(inner[0].reshape(BLOCKS, team, sub), rank).reshape(GTOK)
        lines.start("inner", summed(inner, ("x", "c", "y")))
        lines.start("up", home_steps(up_sum))
        own, other = tick(
            lambda ties: last_product(places, after(d_qkv, *ties), join_weight),
            "mixed",
            "gate",
            "inner",
        )
        lines.start("last", sum_steps(own, other))
        join_grad = tick(lambda ties: mm(d_qkv, after(low_one, *ties)), "last", "up", "inner")
        join_sum = total(join_grad.astype(BF))
        mixed = lines.results["mixed"]
        layer_out, sums = outcome(mixed, join_grad)
        lines.start("sums", summed(sums, ("x", "y", "c", "z1", "z2")))
        tick(None, "sums")
        tick(None, "sums")
        out_grad = tick(
            lambda ties: grad_product(
                after([heads_parts[k] for k in ordered], *ties), [attended[k] for k in ordered], NN
            ),
            "last",
            "inner",
            "up",
        )
        tick(None, "last", "sums")
        tick(None, "sums")
        tick(None, "sums")
        d_one, inner, sums = (lines.results[n] for n in ("last", "inner", "sums"))
        gate_grad, up_grad, down_grad = (lines.results[n] for n in ("gate", "up", "down"))
    else:

        def full(values):
            values = lax.all_gather(values, "y", axis=0, tiled=True)
            return lax.all_gather(values, ROW, axis=1, tiled=True)

        def share_of(values):
            return pick(values.reshape(BLOCKS, team, sub, depth), rank, 1).reshape(-1, depth)

        gate_rows = complete(unit_rows(gate_weight.T))[0]
        up_rows = complete(unit_rows(up_weight.T))[0]
        down_rows = complete(unit_rows(down_weight))[0]
        hidden_rows = full(hidden_in)
        upstream_rows = full(cotangent)
        residual, upstream = share_of(hidden_rows), share_of(upstream_rows)
        wide = hidden_rows.astype(F32)
        scale = lax.rsqrt(jnp.mean(wide * wide, -1, keepdims=True) + EPSILON)
        low_one = (wide * scale * gain_one).astype(BF)
        qkv, keys, values = project(join_weight, low_one, cosine, sine, heads)
        for k in steps:
            head_part, lse = attend_forward(info, qkv, keys, heads, *CHUNKS[k])
            heads_parts.append(head_part)
            lse_parts.append(lse)
            low = to_middle(k, full_scatter(mm(head_part, out_weight, TN).astype(BF)))
            low, gate, up, hidden = unit_products(full_gather(low), gate_rows, up_rows)
            lows.append(low)
            hiddens.append(hidden)
            d_gate, d_up = unit_grads(upstream_rows, starts[k], rows_of[k], down_rows, gate, up)
            gate_parts.append(d_gate)
            up_parts.append(d_up)
            partial = (mm(d_gate, gate_rows) + mm(d_up, up_rows)).astype(BF)
            low = to_d_middle(k, full_scatter(partial))
            attended[k], d_heads[k] = head_product(full_gather(low), out_weight)
        gate_sum, up_sum = total(grad_product(gate_parts, lows)), total(grad_product(up_parts, lows))
        down_sum = total(grad_product(hiddens, [upstream_rows], TN, starts))
        mixed = full_scatter(
            jnp.concatenate([mm(hiddens[k], down_rows).astype(BF) for k in ordered], 0)
        )
        d_qkv, inner = backward(prompts, [], backward(conts, []))
        partial = mm(d_qkv, join_weight, TN).astype(BF)
        join_grad = mm(d_qkv, low_one)
        out_grad = grad_product([heads_parts[k] for k in ordered], [attended[k] for k in ordered], NN)
        layer_out, sums = outcome(mixed, join_grad)
        sums = lax.psum(sums, EVERY)
        gate_grad, up_grad, down_grad = (
            complete(home_steps(part)) for part in (gate_sum, up_sum, down_sum)
        )

    attended = [attended[k] for k in ordered]
    gate_grad, up_grad = gate_grad.T.astype(F32), up_grad.T.astype(F32)
    down_grad = down_grad.astype(F32)
    if heads % 4 == 0:
        part = join_sum if quick else total(join_grad.astype(BF))
        part = part.reshape(heads // 4, 3, HD, depth)
        out_part = total(out_grad).reshape(heads // 4, 1, HD, depth)
        part = jnp.concatenate([part, out_part], 1).transpose(1, 0, 2, 3)
        part = spread(columns_of(part.reshape(4, heads // 4 * HD, depth), 4, width))
        part = part.transpose(1, 0, 2, 3).reshape(4, head_width, width)
    else:
        part = jnp.concatenate(
            [join_grad.astype(BF).reshape(heads, 3, HD, depth), out_grad.reshape(heads, 1, HD, depth)], 1
        ).transpose(1, 0, 2, 3)
        part = spread(columns_of(part.reshape(4, heads * HD, depth), 4, width))
        part = lax.psum_scatter(part, "z", scatter_dimension=0, tiled=False)
    query_grad, key_grad, value_grad = (part[k].T.astype(F32) for k in range(3))
    output_grad = part[3].astype(F32)

    if quick:
        half = local_tokens
        inner = pick(inner.reshape(2, half), y)
        d_middle = jnp.concatenate(
            [lax.dynamic_slice_in_dim(a, row * width, width, 1) for a in attended], 0
        )
        d_middle = pick(d_middle.reshape(2, BLOCKS // 2, team, sub, width), y)
        d_middle = straighten(d_middle, rank).reshape(half, width).astype(F32)
        rows = half // team
        layer_out = jnp.stack(
            [
                layer_out[h * rows : (h + 1) * rows, k * width : (k + 1) * width]
                for h in range(2)
                for k in range(4)
            ]
        )
        layer_out = lax.all_to_all(layer_out, TEAM, 0, 0, tiled=True)
        layer_out = layer_out.reshape(team, BLOCKS // 2, sub, width).transpose(1, 0, 2, 3)
        layer_out = layer_out.reshape(half, width)
    else:
        d_one = lax.psum_scatter(partial, "y", scatter_dimension=0, tiled=True)
        d_one = lax.psum_scatter(d_one, ROW, scatter_dimension=1, tiled=True).astype(F32)
        inner = lax.psum(inner[0], TEAM)
        inner = lax.dynamic_slice(inner, (y * local_tokens,), (local_tokens,))
        corner = (y * local_tokens, row * width)
        d_middle = lax.dynamic_slice(
            jnp.concatenate(attended, 0), corner, (local_tokens, width)
        ).astype(F32)
        layer_out = lax.all_gather(
            layer_out.reshape(BLOCKS, sub, depth), TEAM, axis=1, tiled=False
        ).reshape(GTOK, depth)
        layer_out = lax.dynamic_slice(layer_out, corner, (local_tokens, width))
    wide = hidden_in.astype(F32)
    scale_one = lax.rsqrt(row_sum(jnp.sum(wide * wide, -1)) / depth + EPSILON)[:, None]
    norm_one = wide * scale_one
    input_grad = d_middle + scale_one * (d_one * gain_before - norm_one * (inner / depth)[:, None])

    before_grad = lax.dynamic_slice(sums, (row * width,), (width,))
    middle_grad = lax.dynamic_slice(sums, (depth + row * width,), (width,))
    valid_count = (lengths.shape[0] * PROMPT + jnp.sum(lengths)).astype(F32)
    rms_values = jnp.sqrt(sums[2 * depth :] / (valid_count * depth))
    return (
        layer_out,
        input_grad,
        before_grad,
        query_grad,
        key_grad,
        value_grad,
        output_grad,
        middle_grad,
        gate_grad,
        up_grad,
        down_grad,
        rms_values,
    )


def solution(mesh):
    split = mesh.shape["col"] // GROUPS
    grid = Mesh(mesh.devices.reshape(2, 2, GROUPS, split), ("x", "c", "z", "y"))
    row, col = ("x", "c"), ("z", "y")
    return jax.shard_map(
        functools.partial(local, split == 2),
        mesh=grid,
        in_specs=(
            P(col, row),
            P(row),
            P(row, col),
            P(row, col),
            P(row, col),
            P(col, row),
            P(row),
            P(row, col),
            P(row, col),
            P(col, row),
            P(col, row),
            P(),
            P(),
        ),
        out_specs=(
            P(col, row),
            P(col, row),
            P(row),
            P(row, col),
            P(row, col),
            P(row, col),
            P(col, row),
            P(row),
            P(row, col),
            P(row, col),
            P(col, row),
            P(),
        ),
        check_vma=False,
    )
```

```python
import functools
import jax
import jax.numpy as jnp
from jax import lax
from jax.experimental import pallas as pl
from jax.experimental.pallas import tpu as pltpu
from jax.sharding import Mesh
from jax.sharding import PartitionSpec as P

HD = 64
PROMPT = 2048
CLEN = 256
CONTS = 6
GTOK = 3584
BLK = 256
PBLKS = PROMPT // BLK
BLOCKS = GTOK // BLK
ROWS = 3 * HD
BF = jnp.bfloat16
F32 = jnp.float32
LOW = -1e30
LOG2E = 1.4426950408889634
FACTOR = HD ** (-0.5) * LOG2E
VMEM_LIMIT = 56 * 1024 * 1024

NN = (((1,), (0,)), ((), ()))
NT = (((1,), (1,)), ((), ()))
TN = (((0,), (0,)), ((), ()))


def mm(a, b, dims=NN):
    return lax.dot_general(a, b, dims, preferred_element_type=F32)


def block_plan(info, block):
    cont = jnp.maximum(block - PBLKS, 0)
    is_cont = block >= PBLKS
    reach = info[cont]
    full = jnp.where(is_cont, reach // BLK, block)
    rest = jnp.where(is_cont, reach - full * BLK, 0)
    limit = jnp.where(is_cont, info[CONTS + cont], BLK)
    masked = 1 + (rest > 0).astype(jnp.int32)
    return full, rest, limit, masked


def local_ids(info, shape, axis):
    return lax.broadcasted_iota(jnp.int32, shape, axis) ^ info[2 * CONTS]


def masked_step(info, block, full, rest, limit, index):
    own = index == 0
    target = jnp.where(own, block, full)
    query_ids = local_ids(info, (1, BLK), 1)
    bound = jnp.where(own, jnp.minimum(query_ids + 1, limit), rest)
    key_ids = local_ids(info, (BLK, BLK), 0)
    return target, key_ids < bound


def columns(block):
    return pl.ds(pl.multiple_of(block * BLK, BLK), BLK)


def forward_kernel(heads, first, info, qkv, knat, out, lse, acc, top, tot):
    block = pl.program_id(0) + first
    full, rest, limit, masked = block_plan(info, block)
    here = columns(block)
    acc[...] = jnp.zeros_like(acc)
    top[...] = jnp.full_like(top, LOW)
    tot[...] = jnp.zeros_like(tot)

    def step(target, allowed, wide=1):
        span = pl.ds(pl.multiple_of(target * BLK, BLK), wide * BLK)
        weights, shrinks = [], []
        scores = [
            mm(knat[h, span, :], qkv[h * ROWS : h * ROWS + HD, here]) for h in range(heads)
        ]
        for h in range(heads):
            score = scores[h] * FACTOR
            if allowed is not None:
                score = jnp.where(allowed, score, LOW)
            old = top[h : h + 1, :]
            new = jnp.maximum(old, jnp.max(score, 0, keepdims=True))
            weight = jnp.exp2(score - new)
            shrink = jnp.exp2(old - new)
            top[h : h + 1, :] = new
            tot[h : h + 1, :] = tot[h : h + 1, :] * shrink + jnp.sum(weight, 0, keepdims=True)
            weights.append(weight.astype(BF))
            shrinks.append(shrink)
        for h in range(heads):
            value = qkv[h * ROWS + 2 * HD : (h + 1) * ROWS, span]
            acc[h] = acc[h] * shrinks[h] + mm(value, weights[h])

    def full_step(index, carry):
        step(index, None)
        return carry

    def mask_step(index, carry):
        target, allowed = masked_step(info, block, full, rest, limit, index)
        step(target, allowed)
        return carry

    def wide_step(index, carry):
        step(index * 4, None, 4)
        return carry

    lax.fori_loop(0, full // 4, wide_step, 0)
    lax.fori_loop(full // 4 * 4, full, full_step, 0)
    lax.fori_loop(0, masked, mask_step, 0)
    for h in range(heads):
        total = tot[h : h + 1, :]
        out[h * HD : (h + 1) * HD, :] = (acc[h] / total).astype(BF)
        lse[h : h + 1, :] = top[h : h + 1, :] + jnp.log2(total)


def attend_forward(info, qkv, knat, heads, first, count):
    pad = max(8, heads)
    return pl.pallas_call(
        functools.partial(forward_kernel, heads, first),
        grid=(count,),
        in_specs=[
            pl.BlockSpec(memory_space=pltpu.SMEM),
            pl.BlockSpec(qkv.shape, lambda i: (0, 0)),
            pl.BlockSpec(knat.shape, lambda i: (0, 0, 0)),
        ],
        out_specs=[
            pl.BlockSpec((heads * HD, BLK), lambda i: (0, i)),
            pl.BlockSpec((pad, BLK), lambda i: (0, i)),
        ],
        out_shape=[
            jax.ShapeDtypeStruct((heads * HD, count * BLK), BF),
            jax.ShapeDtypeStruct((pad, count * BLK), F32),
        ],
        scratch_shapes=[
            pltpu.VMEM((heads, HD, BLK), F32),
            pltpu.VMEM((pad, BLK), F32),
            pltpu.VMEM((pad, BLK), F32),
        ],
        compiler_params=pltpu.CompilerParams(vmem_limit_bytes=VMEM_LIMIT),
        cost_estimate=pl.CostEstimate(
            flops=heads * count * 6 * BLK * BLK * 2560,
            bytes_accessed=16 << 20,
            transcendentals=heads * count * 6 * BLK * BLK,
        ),
    )(info, qkv, knat)


def turn(values, cosine, sine, at):
    half = HD // 2
    cos, sin = cosine[:, at], sine[:, at]
    former, latter = values[:half], values[half:]
    return former * cos + latter * sin, latter * cos - former * sin


def backward_kernel(heads, first, final, info, qkv, knat, vnat, d_out, heads_out, lse, cosine, sine, *refs):
    if final:
        d_old_keys, d_old_values, d_old_query, old_inner, d_qkv, inner, d_keys, d_values, d_query = refs
    else:
        d_keys, d_values, d_turned, share_out, d_query = refs
    block = pl.program_id(0) + first
    full, rest, limit, masked = block_plan(info, block)
    here = columns(block)
    there = columns(pl.program_id(0))

    @pl.when(pl.program_id(0) == 0)
    def _():
        if final:
            d_keys[...] = d_old_keys[...]
            d_values[...] = d_old_values[...]
            inner[...] = jnp.zeros_like(inner)
        else:
            d_keys[...] = jnp.zeros_like(d_keys)
            d_values[...] = jnp.zeros_like(d_values)

    d_query[...] = jnp.zeros_like(d_query)
    deltas = []
    for h in range(heads):
        rows = slice(h * HD, (h + 1) * HD)
        deltas.append(
            jnp.sum(d_out[rows, there].astype(F32) * heads_out[rows, here].astype(F32), 0, keepdims=True)
        )

    def step(target, allowed, wide=1):
        span = pl.ds(pl.multiple_of(target * BLK, BLK), wide * BLK)
        for first in range(0, heads, 4):
            team = range(first, min(first + 4, heads))
            scores = [
                mm(knat[h, span, :], qkv[h * ROWS : h * ROWS + HD, here]) for h in team
            ]
            d_probs = [
                mm(vnat[h, span, :], d_out[h * HD : (h + 1) * HD, there]) for h in team
            ]
            low_probs, d_scores = [], []
            for h, score, d_prob in zip(team, scores, d_probs):
                score = score * FACTOR - lse[h : h + 1, here]
                if allowed is not None:
                    score = jnp.where(allowed, score, LOW)
                probs = jnp.exp2(score)
                low_probs.append(probs.astype(BF))
                d_scores.append((probs * (d_prob - deltas[h])).astype(BF))
            for h, low, d_score in zip(team, low_probs, d_scores):
                rows = slice(h * HD, (h + 1) * HD)
                query = qkv[h * ROWS : h * ROWS + HD, here]
                key = qkv[h * ROWS + HD : h * ROWS + 2 * HD, span]
                d_query[h] += mm(key, d_score)
                d_keys[rows, span] += mm(query, d_score, NT)
                d_values[rows, span] += mm(d_out[rows, there], low, NT)

    def full_step(index, carry):
        step(index, None)
        return carry

    def mask_step(index, carry):
        target, allowed = masked_step(info, block, full, rest, limit, index)
        step(target, allowed)
        return carry

    def wide_step(index, carry):
        step(index * 2, None, 2)
        return carry

    lax.fori_loop(0, full // 2, wide_step, 0)
    lax.fori_loop(full // 2 * 2, full, full_step, 0)
    lax.fori_loop(0, masked, mask_step, 0)

    half = HD // 2
    share = jnp.zeros((1, BLK), F32)
    for h in range(heads):
        start = h * ROWS
        values = d_query[h] * HD ** (-0.5)
        share += jnp.sum(values * qkv[start : start + HD, here].astype(F32), 0, keepdims=True)
        low, high = turn(values, cosine, sine, here)
        if final:
            d_qkv[start : start + half, here] = low.astype(BF)
            d_qkv[start + half : start + HD, here] = high.astype(BF)
        else:
            d_turned[h * HD : h * HD + half, :] = low.astype(BF)
            d_turned[h * HD + half : (h + 1) * HD, :] = high.astype(BF)
    if not final:
        share_out[0:1, :] = share
        return
    inner[0:1, here] = share

    @pl.when(block == PBLKS - 1)
    def _():
        inner[:, PROMPT:] = old_inner[...]
        for h in range(heads):
            d_qkv[h * ROWS : h * ROWS + HD, PROMPT:] = d_old_query[h * HD : (h + 1) * HD, :]

        def finish(index, carry):
            at = columns(index)
            share = inner[0:1, at]
            for h in range(heads):
                start = h * ROWS + HD
                rows = slice(h * HD, (h + 1) * HD)
                values = d_keys[rows, at] * HD ** (-0.5)
                share += jnp.sum(values * qkv[start : start + HD, at].astype(F32), 0, keepdims=True)
                low, high = turn(values, cosine, sine, at)
                d_qkv[start : start + half, at] = low.astype(BF)
                d_qkv[start + half : start + HD, at] = high.astype(BF)
                start += HD
                values = d_values[rows, at]
                share += jnp.sum(values * qkv[start : start + HD, at].astype(F32), 0, keepdims=True)
                d_qkv[start : start + HD, at] = values.astype(BF)
            inner[0:1, at] = share
            return carry

        lax.fori_loop(0, BLOCKS, finish, 0)


def attend_backward(info, operands, heads, before=None):
    whole = lambda a: pl.BlockSpec(a.shape, lambda i, n=len(a.shape): (0,) * n)
    final = before is not None
    operands = tuple(operands) + (tuple(before) if final else ())
    sums = jax.ShapeDtypeStruct((heads * HD, GTOK), F32)
    rest = GTOK - PROMPT
    if final:
        shapes = [jax.ShapeDtypeStruct((heads * ROWS, GTOK), BF), jax.ShapeDtypeStruct((8, GTOK), F32)]
        specs = [whole(a) for a in shapes]
        scratch = [pltpu.VMEM(sums.shape, F32), pltpu.VMEM(sums.shape, F32)]
    else:
        shapes = [sums, sums, jax.ShapeDtypeStruct((heads * HD, rest), BF), jax.ShapeDtypeStruct((8, rest), F32)]
        specs = [whole(sums), whole(sums)]
        specs += [
            pl.BlockSpec((heads * HD, BLK), lambda i: (0, i)),
            pl.BlockSpec((8, BLK), lambda i: (0, i)),
        ]
        scratch = []
    return pl.pallas_call(
        functools.partial(backward_kernel, heads, 0 if final else PBLKS, final),
        grid=(PBLKS if final else CONTS,),
        in_specs=[pl.BlockSpec(memory_space=pltpu.SMEM)] + [whole(a) for a in operands],
        out_specs=specs,
        out_shape=shapes,
        scratch_shapes=scratch + [pltpu.VMEM((heads, HD, BLK), F32)],
        compiler_params=pltpu.CompilerParams(vmem_limit_bytes=VMEM_LIMIT),
        cost_estimate=pl.CostEstimate(
            flops=heads * BLOCKS * 3 * BLK * BLK * 4096,
            bytes_accessed=32 << 20,
            transcendentals=heads * BLOCKS * 3 * BLK * BLK,
        ),
    )(info, *operands)


def project_kernel(heads, weight, low, cosine, sine, qkv, knat, vnat):
    raw = mm(weight[...], low[...], NT)
    half = HD // 2
    cos, sin = cosine[...], sine[...]
    for h in range(heads):
        for part in range(2):
            start = h * ROWS + part * HD
            former, latter = raw[start : start + half], raw[start + half : start + HD]
            turned = jnp.concatenate(
                [former * cos - latter * sin, latter * cos + former * sin], 0
            )
            qkv[start : start + HD, :] = turned.astype(BF)
            if part:
                knat[h] = turned.T.astype(BF)
        start = h * ROWS + 2 * HD
        value = raw[start : start + HD]
        qkv[start : start + HD, :] = value.astype(BF)
        vnat[h] = value.T.astype(BF)


def project(weight, low, cosine, sine, heads):
    depth = weight.shape[1]
    natural = jax.ShapeDtypeStruct((heads, GTOK, HD), BF)
    return pl.pallas_call(
        functools.partial(project_kernel, heads),
        grid=(BLOCKS,),
        in_specs=[
            pl.BlockSpec(weight.shape, lambda i: (0, 0)),
            pl.BlockSpec((BLK, depth), lambda i: (i, 0)),
            pl.BlockSpec((HD // 2, BLK), lambda i: (0, i)),
            pl.BlockSpec((HD // 2, BLK), lambda i: (0, i)),
        ],
        out_specs=[pl.BlockSpec((heads * ROWS, BLK), lambda i: (0, i))]
        + [pl.BlockSpec((heads, BLK, HD), lambda i: (0, i, 0))] * 2,
        out_shape=[jax.ShapeDtypeStruct((heads * ROWS, GTOK), BF), natural, natural],
        compiler_params=pltpu.CompilerParams(vmem_limit_bytes=VMEM_LIMIT),
        cost_estimate=pl.CostEstimate(
            flops=2 * GTOK * depth * heads * ROWS, bytes_accessed=3 * GTOK * depth, transcendentals=0
        ),
    )(weight, low, cosine, sine)


EPSILON = 1e-05
THETA = 130000.0
GROUPS = 4
CHUNKS = ((8, 3), (11, 3), (0, 4), (4, 4))
ROW = ("x", "c")
TEAM = ("y", "x", "c")
EVERY = ("x", "c", "z", "y")


def after(values, *earlier):
    return lax.optimization_barrier((values, earlier))[0]


def flip(values, axis):
    return lax.ppermute(values, axis, [(0, 1), (1, 0)])


def send(values, axis):
    if axis == "z1":
        return lax.ppermute(values, "z", [(0, 1), (1, 0), (2, 3), (3, 2)])
    if axis == "z2":
        return lax.ppermute(values, "z", [(0, 2), (1, 3), (2, 0), (3, 1)])
    return flip(values, axis)


def pick(stack, index, axis=0):
    return lax.dynamic_index_in_dim(stack, index, axis, keepdims=False)


def in_order(mine, other, bit, axis):
    return jnp.where(
        bit == 0, jnp.stack([mine, other], axis), jnp.stack([other, mine], axis)
    )


def spread_steps(pieces):
    x, c = lax.axis_index("x"), lax.axis_index("c")
    pieces = pieces.reshape((2, 2) + pieces.shape[1:])
    (got,) = yield [(pick(pieces, 1 - x), "x")]
    pieces = in_order(pick(pieces, x), got, x, 0)
    (got,) = yield [(pick(pieces, 1 - c, 1), "c")]
    pieces = in_order(pick(pieces, c, 1), got, c, 1)
    return pieces.reshape((4,) + pieces.shape[2:])


def complete(steps):
    try:
        wanted = next(steps)
        while True:
            wanted = steps.send([flip(*w) for w in wanted])
    except StopIteration as end:
        return end.value


def spread(pieces):
    return complete(spread_steps(pieces))


class Lines:
    def __init__(self):
        self.wanted = {}
        self.flying = {}
        self.results = {}
        self.last = []
        self.extra = []

    def start(self, name, steps):
        self.wanted[name] = (steps, next(steps))

    def launch(self, name):
        steps, wanted = self.wanted.pop(name)
        wanted = [(after(v, *self.last) if self.last else v, axis) for v, axis in wanted]
        self.extra += [v for v, _ in wanted]
        self.flying[name] = (steps, [send(v, axis) for v, axis in wanted])

    def land(self, name):
        steps, got = self.flying.pop(name)
        self.proceed(name, steps, after(got, *self.last))

    def proceed(self, name, steps, got):
        try:
            self.wanted[name] = (steps, steps.send(got))
        except StopIteration as end:
            self.results[name] = end.value
            value = end.value[-1] if isinstance(end.value, list) else end.value
            if value is not None:
                self.extra.append(value)
            if name == "mixed":
                self.extra += list(got)

    def tick(self, large, *names):
        if large is None:
            for name in names:
                steps, wanted = self.wanted.pop(name)
                wanted = [(after(v, *self.last) if self.last else v, axis) for v, axis in wanted]
                self.proceed(name, steps, [send(*w) for w in wanted])
            return None
        sent = {}
        for name in names:
            steps, wanted = self.wanted.pop(name)
            sent[name] = (steps, [(after(v, *self.last) if self.last else v, axis) for v, axis in wanted])
        operands = [v for _, part in sent.values() for v, _ in part]
        done = large(self.last + self.extra + operands)
        self.extra = []
        self.last = [done[0] if isinstance(done, (tuple, list)) else done]
        for name, (steps, wanted) in sent.items():
            self.proceed(name, steps, after([send(*w) for w in wanted], *self.last))
        return done


def row_gather(values):
    x, c = lax.axis_index("x"), lax.axis_index("c")
    pair = in_order(values, flip(values, "x"), x, 0)
    four = in_order(pair, flip(pair, "c"), c, 1)
    return four.reshape((4,) + values.shape)


def row_sum(values):
    values = values + flip(values, "x")
    return values + flip(values, "c")


def halves(values):
    middle = values.shape[0] // 2
    return values[:middle], values[middle:]


def place_steps(own):
    from_x, from_y, from_c = yield [(own, "x"), (own, "y"), (own, "c")]
    former, latter, by_x, by_y = yield [
        (halves(from_y)[0], "x"),
        (halves(from_x)[1], "y"),
        (from_x, "c"),
        (from_y, "c"),
    ]
    corner = jnp.concatenate([former, latter], 0)
    (other,) = yield [(corner, "c")]
    return [own, from_c, from_x, by_x, from_y, by_y, corner, other]


def gather_steps(own):
    from_x, from_y = yield [(own, "x"), (own, "y")]
    former, latter = yield [(halves(from_y)[0], "x"), (halves(from_x)[1], "y")]
    four = jnp.concatenate([own, from_x, from_y, former, latter], 0)
    (other,) = yield [(four, "c")]
    return [four, other]


def sum_steps(keep, send):
    (got,) = yield [(send, "c")]
    sums = [halves(keep[k].astype(F32) + got[k].astype(F32)) for k in range(4)]
    to_x = jnp.stack([sums[1][0], sums[3][0]]).astype(BF)
    to_y = jnp.stack([sums[2][1], sums[3][1]]).astype(BF)
    by_x, by_y = yield [(to_x, "x"), (to_y, "y")]
    over_y = (sums[2][0] + by_x[1].astype(F32)).astype(BF)
    over_x = (sums[1][1] + by_y[1].astype(F32)).astype(BF)
    former = sums[0][0] + by_x[0].astype(F32)
    latter = sums[0][1] + by_y[0].astype(F32)
    by_y, by_x = yield [(over_y, "y"), (over_x, "x")]
    return jnp.concatenate([former + by_y.astype(F32), latter + by_x.astype(F32)], 0)


def norm_kernel(mode, heads, places, *refs):
    own, other, refs = refs[:4], refs[4:8], refs[8:]
    if mode:
        gain, weight, cosine, sine, low, share, qkv, knat, vnat, whole = refs
    else:
        low, share, whole = refs
    half, row, rank = places[0], places[1], places[2]
    mine = pl.program_id(0) // (BLOCKS // 2) == half
    width = own[0].shape[1]

    def place(sources):
        for k, source in enumerate(sources):
            at = pl.multiple_of((row ^ k) * width, width)
            whole[:, pl.ds(at, width)] = source[...]

    @pl.when(mine)
    def _():
        place(own)

    @pl.when(jnp.logical_not(mine))
    def _():
        place(other)

    sub = share.shape[0]
    for k in range(BLK // sub):
        at = pl.multiple_of((rank ^ k) * sub, sub)
        rows = whole[pl.ds(at, sub), :]
        if k == 0:
            share[...] = rows
        if not mode:
            low[k * sub : (k + 1) * sub, :] = rows
        else:
            wide = rows.astype(F32)
            scale = lax.rsqrt(jnp.sum(wide * wide, 1, keepdims=True) / wide.shape[1] + EPSILON)
            low[k * sub : (k + 1) * sub, :] = (wide * scale * gain[...]).astype(BF)
    if mode:
        project_kernel(heads, weight, low, cosine, sine, qkv, knat, vnat)


def assemble(places, pieces, gain, sub, projection=(), heads=0):
    per = BLOCKS // 2
    width = pieces[0].shape[1]
    whole = 4 * width
    mode = gain is not None

    def own_map(i, places):
        return jnp.where(i // per == places[0], i % per, 0), 0

    def other_map(i, places):
        return jnp.where(i // per == places[0], 0, i % per), 0

    operands = list(pieces)
    specs = [pl.BlockSpec((BLK, width), own_map)] * 4 + [pl.BlockSpec((BLK, width), other_map)] * 4
    outs = [pl.BlockSpec((BLK, whole), lambda i, p: (i, 0)), pl.BlockSpec((sub, whole), lambda i, p: (i, 0))]
    shapes = [jax.ShapeDtypeStruct((GTOK, whole), BF), jax.ShapeDtypeStruct((BLOCKS * sub, whole), BF)]
    flops = 0
    if mode:
        table = pl.BlockSpec((HD // 2, BLK), lambda i, p: (0, i))
        specs += [pl.BlockSpec((1, whole), lambda i, p: (0, 0))]
        specs += [pl.BlockSpec(projection[0].shape, lambda i, p: (0, 0)), table, table]
        operands += [gain.reshape(1, whole), *projection]
        outs += [pl.BlockSpec((heads * ROWS, BLK), lambda i, p: (0, i))]
        outs += [pl.BlockSpec((heads, BLK, HD), lambda i, p: (0, i, 0))] * 2
        natural = jax.ShapeDtypeStruct((heads, GTOK, HD), BF)
        shapes += [jax.ShapeDtypeStruct((heads * ROWS, GTOK), BF), natural, natural]
        flops = 2 * GTOK * whole * heads * ROWS
    return pl.pallas_call(
        functools.partial(norm_kernel, mode, heads),
        grid_spec=pltpu.PrefetchScalarGridSpec(
            num_scalar_prefetch=1,
            grid=(BLOCKS,),
            in_specs=specs,
            out_specs=outs,
            scratch_shapes=[pltpu.VMEM((BLK, whole), BF)],
        ),
        out_shape=shapes,
        compiler_params=params(),
        cost_estimate=cost(flops + GTOK * whole * 6, GTOK * whole * 5),
    )(places, *operands)


def straighten(values, rank):
    count = values.shape[1]
    return jnp.stack([pick(values, j ^ rank, 1) for j in range(count)], 1)


def whole_spec(shape):
    return pl.BlockSpec(shape, lambda *i, n=len(shape): (0,) * n)


def cost(flops, bytes_accessed, transcendentals=0):
    return pl.CostEstimate(
        flops=int(flops), bytes_accessed=int(bytes_accessed), transcendentals=int(transcendentals)
    )


def params():
    return pltpu.CompilerParams(vmem_limit_bytes=VMEM_LIMIT)


def split_kernel(pairs, form, sub, *refs):
    keep, send = refs[2 * pairs :]
    total = mm(refs[0][...], refs[1][...], form)
    for p in range(1, pairs):
        total += mm(refs[2 * p][...], refs[2 * p + 1][...], form)
    low = total.astype(BF)
    for b in range(low.shape[0] // BLK):
        for k in range(8):
            target = send if k % 2 else keep
            start = b * BLK + k * sub
            target[k // 2, b * sub : (b + 1) * sub, :] = low[start : start + sub]


def split_product(pairs, form):
    width = pairs[0][1].shape[1]
    rows = pairs[0][0].shape[1 if form == TN else 0]
    depth = pairs[0][1].shape[0]
    tile = 512
    sub = BLK // 8
    specs, operands = [], []
    for left, right in pairs:
        specs += [whole_spec(left.shape), pl.BlockSpec((depth, tile), lambda j: (0, j))]
        operands += [left, right]
    shape = (4, rows // 8, width)
    return pl.pallas_call(
        functools.partial(split_kernel, len(pairs), form, sub),
        grid=(width // tile,),
        in_specs=specs,
        out_specs=[pl.BlockSpec((4, rows // 8, tile), lambda j: (0, 0, j))] * 2,
        out_shape=[jax.ShapeDtypeStruct(shape, BF)] * 2,
        compiler_params=params(),
        cost_estimate=cost(
            2 * rows * depth * width * len(pairs),
            2 * (rows * width + (rows + width) * depth * len(pairs)),
        ),
    )(*operands)


def mix_kernel(parts, sub, *refs):
    weight, keep, send = refs[parts:]
    at = 0
    for left in refs[:parts]:
        low = mm(left[...], weight[...]).astype(BF)
        for b in range(low.shape[0] // BLK):
            for k in range(8):
                target = send if k % 2 else keep
                start = b * BLK + k * sub
                target[k // 2, at : at + sub, :] = low[start : start + sub]
            at += sub


def mix_product(parts, weight):
    width = weight.shape[1]
    rows = sum(a.shape[0] for a in parts)
    tile = 256
    return pl.pallas_call(
        functools.partial(mix_kernel, len(parts), BLK // 8),
        grid=(width // tile,),
        in_specs=[whole_spec(a.shape) for a in parts]
        + [pl.BlockSpec((weight.shape[0], tile), lambda j: (0, j))],
        out_specs=[pl.BlockSpec((4, rows // 8, tile), lambda j: (0, 0, j))] * 2,
        out_shape=[jax.ShapeDtypeStruct((4, rows // 8, width), BF)] * 2,
        compiler_params=params(),
        cost_estimate=cost(2 * rows * weight.size, 2 * (rows * width + rows * weight.shape[0])),
    )(*parts, weight)


def join_rows(pieces, target):
    if len(pieces) == 1:
        target[...] = pieces[0][...]
        return
    blocks = target.shape[0] // BLK
    sub = BLK // 8
    for b in range(blocks):
        for k in range(8):
            start = b * BLK + k * sub
            source = ((k // 2) * blocks + b) * sub
            target[start : start + sub, :] = pieces[k % 2][source : source + sub, :]


def unit_kernel(count, *refs):
    pieces, (gates, ups, low, gate_out, up_out, hidden) = refs[:count], refs[count:]

    @pl.when(pl.program_id(0) == 0)
    def _():
        join_rows(pieces, low)

    rows = low[...]
    gate = mm(rows, gates[...], NT)
    up = mm(rows, ups[...], NT)
    gate_out[...] = gate.astype(BF)
    up_out[...] = up.astype(BF)
    hidden[...] = (gate * jax.nn.sigmoid(gate) * up).astype(BF)


def unit_products(pieces, gates, ups):
    rows = sum(p.shape[0] for p in pieces)
    units, depth = gates.shape
    tile = min(units, 256)
    weight = pl.BlockSpec((tile, depth), lambda j: (j, 0))
    result = pl.BlockSpec((rows, tile), lambda j: (0, j))
    return pl.pallas_call(
        functools.partial(unit_kernel, len(pieces)),
        grid=(units // tile,),
        in_specs=[whole_spec(p.shape) for p in pieces] + [weight, weight],
        out_specs=[whole_spec((rows, depth)), result, result, result],
        out_shape=[jax.ShapeDtypeStruct((rows, depth), BF)]
        + [jax.ShapeDtypeStruct((rows, units), BF)] * 3,
        compiler_params=params(),
        cost_estimate=cost(4 * rows * depth * units, 4 * depth * (rows + units), rows * units),
    )(*pieces, gates, ups)


def unit_grad_kernel(upstream, downs, gate_in, up_in, d_gate, d_up):
    d_hidden = mm(upstream[...], downs[...], NT)
    gate, up = gate_in[...].astype(F32), up_in[...].astype(F32)
    sigma = jax.nn.sigmoid(gate)
    silu = gate * sigma
    d_gate[...] = (d_hidden * up * (sigma + silu * (1.0 - sigma))).astype(BF)
    d_up[...] = (d_hidden * silu).astype(BF)


def unit_grads(upstream, first, rows, downs, gate, up):
    units, depth = downs.shape
    tile = min(units, 256)
    result = pl.BlockSpec((rows, tile), lambda j: (0, j))
    return pl.pallas_call(
        unit_grad_kernel,
        grid=(units // tile,),
        in_specs=[
            pl.BlockSpec((pl.Element(rows), pl.Element(depth)), lambda j: (first, 0)),
            pl.BlockSpec((tile, depth), lambda j: (j, 0)),
            result,
            result,
        ],
        out_specs=[result, result],
        out_shape=[jax.ShapeDtypeStruct((rows, units), BF)] * 2,
        compiler_params=params(),
        cost_estimate=cost(2 * rows * depth * units, 4 * depth * (rows + units), rows * units),
    )(upstream, downs, gate, up)


def head_kernel(count, *refs):
    pieces, (weight, joined, result) = refs[:count], refs[count:]
    join_rows(pieces, joined)
    result[...] = mm(weight[...], joined[...], NT).astype(BF)


def head_product(pieces, weight):
    depth = weight.shape[1]
    rows = sum(p.shape[0] for p in pieces)
    return pl.pallas_call(
        functools.partial(head_kernel, len(pieces)),
        out_shape=[
            jax.ShapeDtypeStruct((rows, depth), BF),
            jax.ShapeDtypeStruct((weight.shape[0], rows), BF),
        ],
        compiler_params=params(),
        cost_estimate=cost(2 * rows * depth * weight.shape[0], 4 * rows * depth),
    )(*pieces, weight)


def grad_kernel(parts, form, starts, *refs):
    rights = refs[parts:-1]
    total = None
    for p in range(parts):
        left = refs[p][...]
        if starts:
            count = left.shape[0]
            right = rights[0][starts[p] : starts[p] + count, :]
        else:
            right = rights[p][...]
        term = mm(left, right, form)
        total = term if total is None else total + term
    refs[-1][...] = total.astype(BF)


def grad_product(lefts, rights, form=TN, starts=()):
    rows = lefts[0].shape[1 if form == TN else 0]
    width = rights[0].shape[1]
    tile = 512
    tokens = sum(r.shape[0] for r in rights)
    return pl.pallas_call(
        functools.partial(grad_kernel, len(lefts), form, starts),
        grid=(width // tile,),
        in_specs=[whole_spec(a.shape) for a in lefts]
        + [pl.BlockSpec((b.shape[0], tile), lambda j: (0, j)) for b in rights],
        out_specs=pl.BlockSpec((rows, tile), lambda j: (0, j)),
        out_shape=jax.ShapeDtypeStruct((rows, width), BF),
        compiler_params=params(),
        cost_estimate=cost(2 * rows * width * tokens, 2 * tokens * (rows + width)),
    )(*lefts, *rights)


def join_kernel(d_qkv, low, weight, grad, share):
    total = mm(d_qkv[...], low[...])
    grad[...] = total.astype(BF)
    sums = jnp.sum(total * weight[...].astype(F32), 0, keepdims=True)
    share[...] = jnp.broadcast_to(sums, share.shape)


def join_product(d_qkv, low, weight):
    rows, width = weight.shape
    tile = 512
    return pl.pallas_call(
        join_kernel,
        grid=(width // tile,),
        in_specs=[
            whole_spec(d_qkv.shape),
            pl.BlockSpec((low.shape[0], tile), lambda j: (0, j)),
            pl.BlockSpec((rows, tile), lambda j: (0, j)),
        ],
        out_specs=[
            pl.BlockSpec((rows, tile), lambda j: (0, j)),
            pl.BlockSpec((8, tile), lambda j: (0, j)),
        ],
        out_shape=[jax.ShapeDtypeStruct((rows, width), BF), jax.ShapeDtypeStruct((8, width), F32)],
        compiler_params=params(),
        cost_estimate=cost(2 * rows * width * low.shape[0], 2 * low.shape[0] * (rows + width)),
    )(d_qkv, low, weight)


def last_kernel(places, d_qkv, weight, keep, send, whole):
    row, rank = places[1], places[2]
    sub = BLK // 8
    width = keep.shape[2]
    whole[...] = mm(d_qkv[...], weight[...], TN).astype(BF)
    for k in range(8):
        at = pl.ds(pl.multiple_of((rank ^ k) * sub, sub), sub)
        for j in range(4):
            target = send if j % 2 else keep
            source = pl.ds(pl.multiple_of((row ^ j) * width, width), width)
            target[j // 2, at, :] = whole[k * sub : (k + 1) * sub, source]


def last_product(places, d_qkv, weight):
    depth = weight.shape[1]
    per = BLOCKS // 2

    def out_map(i, places):
        return ((i // per) ^ places[0], i % per, 0)

    return pl.pallas_call(
        last_kernel,
        grid_spec=pltpu.PrefetchScalarGridSpec(
            num_scalar_prefetch=1,
            grid=(BLOCKS,),
            in_specs=[
                pl.BlockSpec((d_qkv.shape[0], BLK), lambda i, places: (0, i)),
                pl.BlockSpec(weight.shape, lambda i, places: (0, 0)),
            ],
            out_specs=[pl.BlockSpec((2, BLK, depth // 4), out_map)] * 2,
            scratch_shapes=[pltpu.VMEM((BLK, depth), BF)],
        ),
        out_shape=[jax.ShapeDtypeStruct((4, GTOK // 2, depth // 4), BF)] * 2,
        compiler_params=params(),
        cost_estimate=cost(2 * GTOK * depth * d_qkv.shape[0], 2 * GTOK * depth),
    )(places, d_qkv, weight)


def columns_of(values, count, width):
    return jnp.stack([values[..., k * width : (k + 1) * width] for k in range(count)])


def local(
    quick,
    hidden_in,
    gain_before,
    query_weight,
    key_weight,
    value_weight,
    output_weight,
    gain_middle,
    gate_weight,
    up_weight,
    down_weight,
    cotangent,
    branch_points,
    lengths,
):
    width = hidden_in.shape[1]
    depth = 4 * width
    head_width = query_weight.shape[1]
    heads = head_width // HD
    units = gate_weight.shape[1]
    local_tokens = hidden_in.shape[0]
    team = 4 * lax.axis_size("y")
    sub = BLK // team
    x, c = lax.axis_index("x"), lax.axis_index("c")
    z, y = lax.axis_index("z"), lax.axis_index("y")
    row = 2 * x + c
    rank = 4 * y + row
    order = rank if quick else jnp.int32(0)
    branch_row = pick(branch_points, z)
    length_row = pick(lengths, z)
    info = jnp.concatenate([branch_row, length_row, jnp.stack([order * sub])]).astype(jnp.int32)
    places = jnp.stack([y, row, rank]).astype(jnp.int32)

    def full_gather(share):
        blocks = share.shape[0] // sub
        got = lax.all_gather(share.reshape(blocks, sub, depth), TEAM, axis=1, tiled=False)
        return [got.reshape(-1, depth)]

    def full_scatter(partial):
        parts = partial.reshape(-1, team, sub, depth)
        parts = lax.psum_scatter(parts, TEAM, scatter_dimension=1, tiled=False)
        return parts.reshape(-1, depth).astype(F32)

    lines = Lines()
    tick = lines.tick

    def unit_rows(weight):
        pieces = yield from spread_steps(weight.reshape(4, units // 4, width))
        pieces = jnp.concatenate([pieces[k] for k in range(4)], 1)
        if quick:
            lines.extra.append(pieces)
        return [lax.all_gather(pieces, "z", axis=0, tiled=True), pieces]

    joined = jnp.stack([query_weight.T, key_weight.T, value_weight.T, output_weight])
    if heads % 4 == 0:
        per = heads // 4
        pieces = joined.reshape(4, 4, per * HD, width).transpose(1, 0, 2, 3)
        if quick:
            from_y = flip(hidden_in, "y")
            lines.start("heads", spread_steps(pieces))
            tick(None, "heads")
            lines.start("gate", unit_rows(after(gate_weight, lines.wanted["heads"][1][0][0]).T))
            tick(None, "heads")
            tick(None, "gate")
            from_x = flip(after(hidden_in, lines.wanted["gate"][1][0][0]), "x")
            tick(None, "gate")
            pieces = lines.results["heads"]
        else:
            pieces = spread(pieces)
        pieces = jnp.concatenate([pieces[k] for k in range(4)], -1)
        pieces = pieces.reshape(4, per, HD, depth).transpose(1, 0, 2, 3).reshape(per, 4 * HD, depth)
        attend_weights = lax.all_gather(pieces, "z", axis=0, tiled=True)
    else:
        pieces = lax.all_gather(joined, "z", axis=0, tiled=False)
        pieces = spread(pieces).reshape(4, 4, heads, HD, width).transpose(2, 1, 3, 0, 4)
        attend_weights = pieces.reshape(heads, 4 * HD, depth)
    join_weight = attend_weights[:, :ROWS].reshape(heads * ROWS, depth)
    out_weight = attend_weights[:, ROWS:].reshape(heads * HD, depth)

    gains = row_gather(after(jnp.stack([gain_before, gain_middle]), pieces))
    gains = gains.transpose(1, 0, 2).reshape(2, depth)
    gain_one, gain_two = gains[0], gains[1]

    ids = jnp.arange(GTOK, dtype=jnp.int32)
    slot_ids = (ids % BLK) ^ (order * sub)
    starts = jnp.concatenate([jnp.arange(PBLKS, dtype=jnp.int32) * BLK, branch_row])
    positions = jnp.repeat(starts, BLK) + slot_ids
    frequency = THETA ** (-2.0 * jnp.arange(HD // 2, dtype=F32) / HD)
    angles = positions.astype(F32)[None, :] * frequency[:, None]
    cosine, sine = jnp.cos(angles), jnp.sin(angles)

    steps = range(len(CHUNKS))
    ordered = sorted(steps, key=lambda k: CHUNKS[k][0])
    rows_of = [count * BLK for _, count in CHUNKS]
    shares = [slice(first * sub, (first + count) * sub) for first, count in CHUNKS]
    starts = tuple(first * BLK for first, _ in CHUNKS)
    conts = [k for k in ordered if CHUNKS[k][0] >= PBLKS]
    prompts = [k for k in ordered if CHUNKS[k][0] < PBLKS]
    attentions, middles, scales, norms, d_middles, notes = ({} for _ in range(6))
    attended, d_heads = {}, {}

    def to_middle(k, attention):
        middle = residual[shares[k]].astype(F32) + attention
        scale_two = lax.rsqrt(jnp.mean(middle * middle, -1, keepdims=True) + EPSILON)
        norm_two = middle * scale_two
        attentions[k], middles[k], scales[k], norms[k] = attention, middle, scale_two, norm_two
        return (norm_two * gain_two).astype(BF)

    def to_d_middle(k, d_two):
        notes[k] = jnp.sum(d_two * norms[k], 0)
        scaled_two = d_two * gain_two
        inner_two = jnp.mean(scaled_two * norms[k], -1, keepdims=True)
        d_middle = upstream[shares[k]].astype(F32) + scales[k] * (scaled_two - norms[k] * inner_two)
        d_middles[k] = d_middle
        return d_middle.astype(BF)

    def backward(parts, ties, before=None):
        d_out = jnp.concatenate([d_heads[k] for k in parts], 1)
        heads_out = jnp.concatenate([heads_parts[k] for k in ordered], 1)
        lse = jnp.concatenate([lse_parts[k] for k in ordered], 1)
        source = after(qkv, *ties) if ties else qkv
        operands = (source, keys, values, d_out, heads_out, lse, cosine, sine)
        return attend_backward(info, operands, heads, before)

    def total(grad):
        return lax.psum_scatter(grad, "z", scatter_dimension=0, tiled=True)

    def home_steps(part):
        part = yield from spread_steps(columns_of(part, 4, width))
        return part.reshape(-1, width)

    def squares_one():
        wide = hidden_in.astype(F32)
        return jnp.sum(wide * wide, -1)

    def outcome(layer_out, share):
        here = jnp.arange(BLOCKS, dtype=jnp.int32)
        bound = jnp.where(here < PBLKS, BLK, jnp.take(length_row, jnp.maximum(here - PBLKS, 0)))
        slots = rank * sub + jnp.arange(sub, dtype=jnp.int32)
        valid = (slots[None, :] < bound[:, None]).astype(F32).reshape(-1)

        def square_sum(part, weights):
            return jnp.sum(weights * jnp.sum(part * part, -1))

        squares = jnp.stack(
            [square_sum(layer_out.astype(F32), valid)]
            + [
                sum(square_sum(parts[k], valid[shares[k]]) for k in steps)
                for parts in (attentions, d_middles)
            ]
        )
        before_local = share / gain_one
        middle_local = sum(notes[k] for k in steps)
        return jnp.concatenate([before_local, middle_local, squares])

    heads_parts, lse_parts, lows, gates, ups, hiddens = ([] for _ in range(6))
    gate_parts, up_parts = [], []
    if quick:
        former, latter = flip(halves(from_y)[0], "x"), flip(halves(from_x)[1], "y")
        corner = jnp.concatenate([former, latter], 0)
        four = [hidden_in, from_x, from_y, corner]
        hidden_pieces = [p for piece in four for p in (piece, flip(piece, "c"))]
        lines.start("up", unit_rows(up_weight.T))
        lines.start("down", unit_rows(down_weight))
        lines.start("late", place_steps(after(cotangent, corner)))
        lines.launch("late")
        low_one, residual, qkv, keys, values = tick(
            lambda ties: assemble(
                places,
                after(hidden_pieces, *ties),
                gain_one,
                sub,
                (join_weight, cosine, sine),
                heads,
            ),
            "up",
        )

        def forward_line(k, partial):
            low = to_middle(k, (yield from sum_steps(*partial)))
            return (yield from gather_steps(low))

        def attend(k, *names):
            def large(ties):
                return attend_forward(info, after(qkv, *ties), keys, heads, *CHUNKS[k])

            head_part, lse = tick(large, *names)
            heads_parts.append(head_part)
            lse_parts.append(lse)
            partial = split_product([(head_part, out_weight)], TN)
            lines.last = [partial[0]]
            lines.start(k, forward_line(k, partial))

        attend(0, "up")
        lines.land("late")
        attend(1, 0, "late")
        attend(2, 0, 1, "down", "late")
        attend(3, 0, 1, 2)
        gate_rows, up_rows = lines.results["gate"][0], lines.results["up"][0]
        upstream_rows, upstream = tick(
            lambda ties: assemble(places, after(lines.results["late"], *ties), None, sub), 0, 1, 3
        )

        def unit(k, *names):
            def large(ties):
                return unit_products(after(lines.results[k], *ties), gate_rows, up_rows)

            low, gate, up, hidden = tick(large, *names)
            lows.append(low)
            gates.append(gate)
            ups.append(up)
            hiddens.append(hidden)

        def gathered(k):
            lines.last = [lines.wanted[k][1][0][0]]
            tick(None, k)

        tick(None, 0, "down")
        down_rows = lines.results["down"][0]
        gathered(0)
        unit(0, 1, 2)
        tick(None, 1, 2)
        gathered(1)
        unit(1, 2, 3)
        tick(None, 2, 3)
        gathered(2)
        lines.extra.append(down_rows)
        unit(2, 3)
        tick(None, 3)
        gathered(3)
        unit(3)
        down_grad = tick(lambda ties: grad_product(hiddens, [after(upstream_rows, *ties)], TN, starts))
        down_sum = total(down_grad)

        def backward_line(k, partial):
            low = to_d_middle(k, (yield from sum_steps(*partial)))
            pieces = yield from gather_steps(low)
            attended[k], d_heads[k] = head_product(pieces, out_weight)
            return d_heads[k]

        def unit_grad(k, first, second):
            def large(ties):
                source = after(gates[k], *ties)
                return unit_grads(upstream_rows, starts[k], rows_of[k], down_rows, source, ups[k])

            d_gate, d_up = tick(large, *first)
            gate_parts.append(d_gate)
            up_parts.append(d_up)

            def more(ties):
                return split_product([(after(d_gate, *ties), gate_rows), (d_up, up_rows)], NN)

            lines.start(k, backward_line(k, tick(more, *second)))

        unit_grad(0, (), ())
        unit_grad(1, (0,), (0,))
        unit_grad(2, (0, 1), (0, 1))
        unit_grad(3, (0, 1, 2), (0, 1, 2))
        def summed(values, axes):
            for axis in axes:
                (got,) = yield [(values, axis)]
                values = values + got
            return values

        gate_grad = tick(lambda ties: grad_product(after(gate_parts, *ties), lows), 1, 2, 3)
        gate_sum = total(gate_grad)
        mixed = tick(
            lambda ties: mix_product(after([hiddens[k] for k in ordered], *ties), down_rows),
            1,
            2,
            3,
        )
        lines.start("mixed", sum_steps(*mixed))
        before = tick(lambda ties: backward(conts, ties), 2, 3, "mixed")
        lines.start("scale", summed(squares_one(), ("x", "c")))
        up_grad = tick(lambda ties: grad_product(after(up_parts, *ties), lows), 2, 3, "scale")
        up_sum = total(up_grad)
        tick(None, 3, "scale")
        tick(None, 3)
        lines.start("down", home_steps(down_sum))
        lines.start("gate", home_steps(gate_sum))
        d_qkv, inner = tick(lambda ties: backward(prompts, ties, before), "mixed", "down", "gate")
        inner = straighten(inner[0].reshape(BLOCKS, team, sub), rank).reshape(GTOK)
        lines.start("inner", summed(inner, ("x", "c", "y")))
        lines.start("up", home_steps(up_sum))
        own, other = tick(
            lambda ties: last_product(places, after(d_qkv, *ties), join_weight),
            "mixed",
            "down",
            "gate",
            "inner",
        )
        lines.start("last", sum_steps(own, other))
        mixed = lines.results["mixed"]
        layer_out = (jnp.concatenate([middles[k] for k in ordered], 0) + mixed).astype(BF)
        rows = local_tokens // team
        layer_pieces = jnp.stack(
            [
                layer_out[h * rows : (h + 1) * rows, k * width : (k + 1) * width]
                for h in range(2)
                for k in range(4)
            ]
        )
        lines.extra.append(layer_pieces)
        layer_pieces = lax.all_to_all(layer_pieces, TEAM, 0, 0, tiled=True)
        join_grad, share = tick(
            lambda ties: join_product(after(d_qkv, *ties), low_one, join_weight),
            "last",
            "up",
            "inner",
        )
        join_sum = total(join_grad)
        out_grad = tick(
            lambda ties: grad_product(
                after([heads_parts[k] for k in ordered], *ties), [attended[k] for k in ordered], NN
            ),
            "last",
            "inner",
            "up",
        )
        turned = lines.wanted["last"][1][0][0]
        sums = outcome(after(layer_out, out_grad), share[0])
        lines.start("sums", summed(after(sums, turned), ("c", "z1", "z2", "x", "y")))
        tick(None, "last")
        for _ in range(5):
            tick(None, "sums")
        d_one, inner, sums = (lines.results[n] for n in ("last", "inner", "sums"))
        join_sum, up_home = after((join_sum, lines.results["up"]), turned)
        lines.results["up"] = up_home
        lines.results["gate"], lines.results["down"], attended, layer_pieces, inner = after(
            (lines.results["gate"], lines.results["down"], attended, layer_pieces, inner), out_grad
        )
        gate_grad, up_grad, down_grad = (lines.results[n] for n in ("gate", "up", "down"))
    else:

        def full(values):
            values = lax.all_gather(values, "y", axis=0, tiled=True)
            return lax.all_gather(values, ROW, axis=1, tiled=True)

        def share_of(values):
            return pick(values.reshape(BLOCKS, team, sub, depth), rank, 1).reshape(-1, depth)

        gate_rows = complete(unit_rows(gate_weight.T))[0]
        up_rows = complete(unit_rows(up_weight.T))[0]
        down_rows = complete(unit_rows(down_weight))[0]
        hidden_rows = full(hidden_in)
        upstream_rows = full(cotangent)
        residual, upstream = share_of(hidden_rows), share_of(upstream_rows)
        wide = hidden_rows.astype(F32)
        scale = lax.rsqrt(jnp.mean(wide * wide, -1, keepdims=True) + EPSILON)
        low_one = (wide * scale * gain_one).astype(BF)
        qkv, keys, values = project(join_weight, low_one, cosine, sine, heads)
        for k in steps:
            head_part, lse = attend_forward(info, qkv, keys, heads, *CHUNKS[k])
            heads_parts.append(head_part)
            lse_parts.append(lse)
            low = to_middle(k, full_scatter(mm(head_part, out_weight, TN).astype(BF)))
            low, gate, up, hidden = unit_products(full_gather(low), gate_rows, up_rows)
            lows.append(low)
            hiddens.append(hidden)
            d_gate, d_up = unit_grads(upstream_rows, starts[k], rows_of[k], down_rows, gate, up)
            gate_parts.append(d_gate)
            up_parts.append(d_up)
            partial = (mm(d_gate, gate_rows) + mm(d_up, up_rows)).astype(BF)
            low = to_d_middle(k, full_scatter(partial))
            attended[k], d_heads[k] = head_product(full_gather(low), out_weight)
        gate_sum, up_sum = total(grad_product(gate_parts, lows)), total(grad_product(up_parts, lows))
        down_sum = total(grad_product(hiddens, [upstream_rows], TN, starts))
        mixed = full_scatter(
            jnp.concatenate([mm(hiddens[k], down_rows).astype(BF) for k in ordered], 0)
        )
        d_qkv, inner = backward(prompts, [], backward(conts, []))
        partial = mm(d_qkv, join_weight, TN).astype(BF)
        join_grad, share = join_product(d_qkv, low_one, join_weight)
        out_grad = grad_product([heads_parts[k] for k in ordered], [attended[k] for k in ordered], NN)
        layer_out = (jnp.concatenate([middles[k] for k in ordered], 0) + mixed).astype(BF)
        sums = lax.psum(outcome(layer_out, share[0]), EVERY)
        gate_grad, up_grad, down_grad = (
            complete(home_steps(part)) for part in (gate_sum, up_sum, down_sum)
        )

    attended = [attended[k] for k in ordered]
    gate_grad, up_grad = gate_grad.T.astype(F32), up_grad.T.astype(F32)
    down_grad = down_grad.astype(F32)
    if heads % 4 == 0:
        part = join_sum if quick else total(join_grad)
        part = part.reshape(heads // 4, 3, HD, depth).transpose(1, 0, 2, 3)
        part = spread(columns_of(part.reshape(3, heads // 4 * HD, depth), 4, width))
        part = part.transpose(1, 0, 2, 3).reshape(3, head_width, width)
        out_part = spread(columns_of(total(out_grad), 4, width)).reshape(1, head_width, width)
        part = jnp.concatenate([part, out_part], 0)
    else:
        part = jnp.concatenate(
            [join_grad.reshape(heads, 3, HD, depth), out_grad.reshape(heads, 1, HD, depth)], 1
        ).transpose(1, 0, 2, 3)
        part = spread(columns_of(part.reshape(4, heads * HD, depth), 4, width))
        part = lax.psum_scatter(part, "z", scatter_dimension=0, tiled=False)
    query_grad, key_grad, value_grad = (part[k].T.astype(F32) for k in range(3))
    output_grad = part[3].astype(F32)

    if quick:
        half = local_tokens
        inner = pick(inner.reshape(2, half), y)
        d_middle = jnp.concatenate(
            [lax.dynamic_slice_in_dim(a, row * width, width, 1) for a in attended], 0
        )
        d_middle = pick(d_middle.reshape(2, BLOCKS // 2, team, sub, width), y)
        d_middle = straighten(d_middle, rank).reshape(half, width).astype(F32)
        layer_out = layer_pieces.reshape(team, BLOCKS // 2, sub, width).transpose(1, 0, 2, 3)
        layer_out = layer_out.reshape(half, width)
    else:
        d_one = lax.psum_scatter(partial, "y", scatter_dimension=0, tiled=True)
        d_one = lax.psum_scatter(d_one, ROW, scatter_dimension=1, tiled=True).astype(F32)
        inner = lax.psum(inner[0], TEAM)
        inner = lax.dynamic_slice(inner, (y * local_tokens,), (local_tokens,))
        corner = (y * local_tokens, row * width)
        d_middle = lax.dynamic_slice(
            jnp.concatenate(attended, 0), corner, (local_tokens, width)
        ).astype(F32)
        layer_out = lax.all_gather(
            layer_out.reshape(BLOCKS, sub, depth), TEAM, axis=1, tiled=False
        ).reshape(GTOK, depth)
        layer_out = lax.dynamic_slice(layer_out, corner, (local_tokens, width))
    wide = hidden_in.astype(F32)
    row_squares = lines.results["scale"] if quick else row_sum(squares_one())
    scale_one = lax.rsqrt(row_squares / depth + EPSILON)[:, None]
    norm_one = wide * scale_one
    input_grad = d_middle + scale_one * (d_one * gain_before - norm_one * (inner / depth)[:, None])

    before_grad = lax.dynamic_slice(sums, (row * width,), (width,))
    middle_grad = lax.dynamic_slice(sums, (depth + row * width,), (width,))
    valid_count = (lengths.shape[0] * PROMPT + jnp.sum(lengths)).astype(F32)
    rms_values = jnp.sqrt(sums[2 * depth :] / (valid_count * depth))
    return (
        layer_out,
        input_grad,
        before_grad,
        query_grad,
        key_grad,
        value_grad,
        output_grad,
        middle_grad,
        gate_grad,
        up_grad,
        down_grad,
        rms_values,
    )


def solution(mesh):
    split = mesh.shape["col"] // GROUPS
    grid = Mesh(mesh.devices.reshape(2, 2, GROUPS, split), ("x", "c", "z", "y"))
    row, col = ("x", "c"), ("z", "y")
    return jax.shard_map(
        functools.partial(local, split == 2),
        mesh=grid,
        in_specs=(
            P(col, row),
            P(row),
            P(row, col),
            P(row, col),
            P(row, col),
            P(col, row),
            P(row),
            P(row, col),
            P(row, col),
            P(col, row),
            P(col, row),
            P(),
            P(),
        ),
        out_specs=(
            P(col, row),
            P(col, row),
            P(row),
            P(row, col),
            P(row, col),
            P(row, col),
            P(col, row),
            P(row),
            P(row, col),
            P(row, col),
            P(col, row),
            P(),
        ),
        check_vma=False,
    )
```

```python
import functools
import jax
import jax.numpy as jnp
from jax import lax
from jax.experimental import pallas as pl
from jax.experimental.pallas import tpu as pltpu
from jax.sharding import Mesh
from jax.sharding import PartitionSpec as P

HD = 64
PROMPT = 2048
CLEN = 256
CONTS = 6
GTOK = 3584
BLK = 256
PBLKS = PROMPT // BLK
BLOCKS = GTOK // BLK
ROWS = 3 * HD
BF = jnp.bfloat16
F32 = jnp.float32
LOW = -1e30
LOG2E = 1.4426950408889634
FACTOR = HD ** (-0.5) * LOG2E
VMEM_LIMIT = 56 * 1024 * 1024

NN = (((1,), (0,)), ((), ()))
NT = (((1,), (1,)), ((), ()))
TN = (((0,), (0,)), ((), ()))


def mm(a, b, dims=NN):
    return lax.dot_general(a, b, dims, preferred_element_type=F32)


def block_plan(info, block):
    cont = jnp.maximum(block - PBLKS, 0)
    is_cont = block >= PBLKS
    reach = info[cont]
    full = jnp.where(is_cont, reach // BLK, block)
    rest = jnp.where(is_cont, reach - full * BLK, 0)
    limit = jnp.where(is_cont, info[CONTS + cont], BLK)
    masked = 1 + (rest > 0).astype(jnp.int32)
    return full, rest, limit, masked


def local_ids(info, shape, axis):
    return lax.broadcasted_iota(jnp.int32, shape, axis) ^ info[2 * CONTS]


def masked_step(info, block, full, rest, limit, index):
    own = index == 0
    target = jnp.where(own, block, full)
    query_ids = local_ids(info, (1, BLK), 1)
    bound = jnp.where(own, jnp.minimum(query_ids + 1, limit), rest)
    key_ids = local_ids(info, (BLK, BLK), 0)
    return target, key_ids < bound


def columns(block):
    return pl.ds(pl.multiple_of(block * BLK, BLK), BLK)


def forward_kernel(heads, first, info, qkv, knat, out, lse, acc, top, tot):
    block = pl.program_id(0) + first
    full, rest, limit, masked = block_plan(info, block)
    here = columns(block)
    acc[...] = jnp.zeros_like(acc)
    top[...] = jnp.full_like(top, LOW)
    tot[...] = jnp.zeros_like(tot)

    def step(target, allowed, wide=1):
        span = pl.ds(pl.multiple_of(target * BLK, BLK), wide * BLK)
        weights, shrinks = [], []
        scores = [
            mm(knat[h, span, :], qkv[h * ROWS : h * ROWS + HD, here]) for h in range(heads)
        ]
        for h in range(heads):
            score = scores[h] * FACTOR
            if allowed is not None:
                score = jnp.where(allowed, score, LOW)
            old = top[h : h + 1, :]
            new = jnp.maximum(old, jnp.max(score, 0, keepdims=True))
            weight = jnp.exp2(score - new)
            shrink = jnp.exp2(old - new)
            top[h : h + 1, :] = new
            tot[h : h + 1, :] = tot[h : h + 1, :] * shrink + jnp.sum(weight, 0, keepdims=True)
            weights.append(weight.astype(BF))
            shrinks.append(shrink)
        for h in range(heads):
            value = qkv[h * ROWS + 2 * HD : (h + 1) * ROWS, span]
            acc[h] = acc[h] * shrinks[h] + mm(value, weights[h])

    def full_step(index, carry):
        step(index, None)
        return carry

    def mask_step(index, carry):
        target, allowed = masked_step(info, block, full, rest, limit, index)
        step(target, allowed)
        return carry

    def wide_step(index, carry):
        step(index * 4, None, 4)
        return carry

    lax.fori_loop(0, full // 4, wide_step, 0)

    @pl.when(full % 4 >= 2)
    def _():
        step(full // 4 * 4, None, 2)

    lax.fori_loop(full // 2 * 2, full, full_step, 0)
    lax.fori_loop(0, masked, mask_step, 0)
    for h in range(heads):
        total = tot[h : h + 1, :]
        out[h * HD : (h + 1) * HD, :] = (acc[h] / total).astype(BF)
        lse[h : h + 1, :] = top[h : h + 1, :] + jnp.log2(total)


def attend_forward(info, qkv, knat, heads, first, count):
    pad = max(8, heads)
    return pl.pallas_call(
        functools.partial(forward_kernel, heads, first),
        grid=(count,),
        in_specs=[
            pl.BlockSpec(memory_space=pltpu.SMEM),
            pl.BlockSpec(qkv.shape, lambda i: (0, 0)),
            pl.BlockSpec(knat.shape, lambda i: (0, 0, 0)),
        ],
        out_specs=[
            pl.BlockSpec((heads * HD, BLK), lambda i: (0, i)),
            pl.BlockSpec((pad, BLK), lambda i: (0, i)),
        ],
        out_shape=[
            jax.ShapeDtypeStruct((heads * HD, count * BLK), BF),
            jax.ShapeDtypeStruct((pad, count * BLK), F32),
        ],
        scratch_shapes=[
            pltpu.VMEM((heads, HD, BLK), F32),
            pltpu.VMEM((pad, BLK), F32),
            pltpu.VMEM((pad, BLK), F32),
        ],
        compiler_params=pltpu.CompilerParams(vmem_limit_bytes=VMEM_LIMIT),
        cost_estimate=pl.CostEstimate(
            flops=heads * count * 6 * BLK * BLK * 2560,
            bytes_accessed=16 << 20,
            transcendentals=heads * count * 6 * BLK * BLK,
        ),
    )(info, qkv, knat)


def turn(values, cosine, sine, at):
    half = HD // 2
    cos, sin = cosine[:, at], sine[:, at]
    former, latter = values[:half], values[half:]
    return former * cos + latter * sin, latter * cos - former * sin


def backward_kernel(heads, first, final, info, qkv, knat, vnat, d_out, heads_out, lse, cosine, sine, *refs):
    if final:
        d_old_keys, d_old_values, d_old_query, old_inner, d_qkv, inner, d_keys, d_values, d_query = refs
    else:
        d_keys, d_values, d_turned, share_out, d_query = refs
    block = pl.program_id(0) + first
    full, rest, limit, masked = block_plan(info, block)
    here = columns(block)
    there = columns(pl.program_id(0))

    @pl.when(pl.program_id(0) == 0)
    def _():
        if final:
            d_keys[...] = d_old_keys[...]
            d_values[...] = d_old_values[...]
            inner[...] = jnp.zeros_like(inner)
        else:
            d_keys[...] = jnp.zeros_like(d_keys)
            d_values[...] = jnp.zeros_like(d_values)

    d_query[...] = jnp.zeros_like(d_query)
    deltas = []
    for h in range(heads):
        rows = slice(h * HD, (h + 1) * HD)
        deltas.append(
            jnp.sum(d_out[rows, there].astype(F32) * heads_out[rows, here].astype(F32), 0, keepdims=True)
        )

    def step(target, allowed, wide=1):
        span = pl.ds(pl.multiple_of(target * BLK, BLK), wide * BLK)
        for first in range(0, heads, 4):
            team = range(first, min(first + 4, heads))
            scores = [
                mm(knat[h, span, :], qkv[h * ROWS : h * ROWS + HD, here]) for h in team
            ]
            d_probs = [
                mm(vnat[h, span, :], d_out[h * HD : (h + 1) * HD, there]) for h in team
            ]
            low_probs, d_scores = [], []
            for h, score, d_prob in zip(team, scores, d_probs):
                score = score * FACTOR - lse[h : h + 1, here]
                if allowed is not None:
                    score = jnp.where(allowed, score, LOW)
                probs = jnp.exp2(score)
                low_probs.append(probs.astype(BF))
                d_scores.append((probs * (d_prob - deltas[h])).astype(BF))
            for h, low, d_score in zip(team, low_probs, d_scores):
                rows = slice(h * HD, (h + 1) * HD)
                query = qkv[h * ROWS : h * ROWS + HD, here]
                key = qkv[h * ROWS + HD : h * ROWS + 2 * HD, span]
                d_query[h] += mm(key, d_score)
                d_keys[rows, span] += mm(query, d_score, NT)
                d_values[rows, span] += mm(d_out[rows, there], low, NT)

    def full_step(index, carry):
        step(index, None)
        return carry

    def mask_step(index, carry):
        target, allowed = masked_step(info, block, full, rest, limit, index)
        step(target, allowed)
        return carry

    def wide_step(index, carry):
        step(index * 2, None, 2)
        return carry

    lax.fori_loop(0, full // 2, wide_step, 0)
    lax.fori_loop(full // 2 * 2, full, full_step, 0)
    lax.fori_loop(0, masked, mask_step, 0)

    half = HD // 2
    share = jnp.zeros((1, BLK), F32)
    for h in range(heads):
        start = h * ROWS
        values = d_query[h] * HD ** (-0.5)
        share += jnp.sum(values * qkv[start : start + HD, here].astype(F32), 0, keepdims=True)
        low, high = turn(values, cosine, sine, here)
        if final:
            d_qkv[start : start + half, here] = low.astype(BF)
            d_qkv[start + half : start + HD, here] = high.astype(BF)
        else:
            d_turned[h * HD : h * HD + half, :] = low.astype(BF)
            d_turned[h * HD + half : (h + 1) * HD, :] = high.astype(BF)
    if not final:
        share_out[0:1, :] = share
        return
    inner[0:1, here] = share

    @pl.when(block == PBLKS - 1)
    def _():
        inner[:, PROMPT:] = old_inner[...]
        for h in range(heads):
            d_qkv[h * ROWS : h * ROWS + HD, PROMPT:] = d_old_query[h * HD : (h + 1) * HD, :]

        def finish(index, carry):
            at = columns(index)
            share = inner[0:1, at]
            for h in range(heads):
                start = h * ROWS + HD
                rows = slice(h * HD, (h + 1) * HD)
                values = d_keys[rows, at] * HD ** (-0.5)
                share += jnp.sum(values * qkv[start : start + HD, at].astype(F32), 0, keepdims=True)
                low, high = turn(values, cosine, sine, at)
                d_qkv[start : start + half, at] = low.astype(BF)
                d_qkv[start + half : start + HD, at] = high.astype(BF)
                start += HD
                values = d_values[rows, at]
                share += jnp.sum(values * qkv[start : start + HD, at].astype(F32), 0, keepdims=True)
                d_qkv[start : start + HD, at] = values.astype(BF)
            inner[0:1, at] = share
            return carry

        lax.fori_loop(0, BLOCKS, finish, 0)


def attend_backward(info, operands, heads, before=None):
    whole = lambda a: pl.BlockSpec(a.shape, lambda i, n=len(a.shape): (0,) * n)
    final = before is not None
    operands = tuple(operands) + (tuple(before) if final else ())
    sums = jax.ShapeDtypeStruct((heads * HD, GTOK), F32)
    rest = GTOK - PROMPT
    if final:
        shapes = [jax.ShapeDtypeStruct((heads * ROWS, GTOK), BF), jax.ShapeDtypeStruct((8, GTOK), F32)]
        specs = [whole(a) for a in shapes]
        scratch = [pltpu.VMEM(sums.shape, F32), pltpu.VMEM(sums.shape, F32)]
    else:
        shapes = [sums, sums, jax.ShapeDtypeStruct((heads * HD, rest), BF), jax.ShapeDtypeStruct((8, rest), F32)]
        specs = [whole(sums), whole(sums)]
        specs += [
            pl.BlockSpec((heads * HD, BLK), lambda i: (0, i)),
            pl.BlockSpec((8, BLK), lambda i: (0, i)),
        ]
        scratch = []
    return pl.pallas_call(
        functools.partial(backward_kernel, heads, 0 if final else PBLKS, final),
        grid=(PBLKS if final else CONTS,),
        in_specs=[pl.BlockSpec(memory_space=pltpu.SMEM)] + [whole(a) for a in operands],
        out_specs=specs,
        out_shape=shapes,
        scratch_shapes=scratch + [pltpu.VMEM((heads, HD, BLK), F32)],
        compiler_params=pltpu.CompilerParams(vmem_limit_bytes=VMEM_LIMIT),
        cost_estimate=pl.CostEstimate(
            flops=heads * BLOCKS * 3 * BLK * BLK * 4096,
            bytes_accessed=32 << 20,
            transcendentals=heads * BLOCKS * 3 * BLK * BLK,
        ),
    )(info, *operands)


def project_kernel(heads, weight, low, cosine, sine, qkv, knat, vnat):
    raw = mm(weight[...], low[...], NT)
    half = HD // 2
    cos, sin = cosine[...], sine[...]
    for h in range(heads):
        for part in range(2):
            start = h * ROWS + part * HD
            former, latter = raw[start : start + half], raw[start + half : start + HD]
            turned = jnp.concatenate(
                [former * cos - latter * sin, latter * cos + former * sin], 0
            )
            qkv[start : start + HD, :] = turned.astype(BF)
            if part:
                knat[h] = turned.T.astype(BF)
        start = h * ROWS + 2 * HD
        value = raw[start : start + HD]
        qkv[start : start + HD, :] = value.astype(BF)
        vnat[h] = value.T.astype(BF)


def project(weight, low, cosine, sine, heads):
    depth = weight.shape[1]
    natural = jax.ShapeDtypeStruct((heads, GTOK, HD), BF)
    return pl.pallas_call(
        functools.partial(project_kernel, heads),
        grid=(BLOCKS,),
        in_specs=[
            pl.BlockSpec(weight.shape, lambda i: (0, 0)),
            pl.BlockSpec((BLK, depth), lambda i: (i, 0)),
            pl.BlockSpec((HD // 2, BLK), lambda i: (0, i)),
            pl.BlockSpec((HD // 2, BLK), lambda i: (0, i)),
        ],
        out_specs=[pl.BlockSpec((heads * ROWS, BLK), lambda i: (0, i))]
        + [pl.BlockSpec((heads, BLK, HD), lambda i: (0, i, 0))] * 2,
        out_shape=[jax.ShapeDtypeStruct((heads * ROWS, GTOK), BF), natural, natural],
        compiler_params=pltpu.CompilerParams(vmem_limit_bytes=VMEM_LIMIT),
        cost_estimate=pl.CostEstimate(
            flops=2 * GTOK * depth * heads * ROWS, bytes_accessed=3 * GTOK * depth, transcendentals=0
        ),
    )(weight, low, cosine, sine)


EPSILON = 1e-05
THETA = 130000.0
GROUPS = 4
CHUNKS = ((8, 3), (11, 3), (0, 4), (4, 4))
ROW = ("x", "c")
TEAM = ("y", "x", "c")
EVERY = ("x", "c", "z", "y")


def after(values, *earlier):
    return lax.optimization_barrier((values, earlier))[0]


def flip(values, axis):
    return lax.ppermute(values, axis, [(0, 1), (1, 0)])


def send(values, axis):
    if axis == "z1":
        return lax.ppermute(values, "z", [(0, 1), (1, 0), (2, 3), (3, 2)])
    if axis == "z2":
        return lax.ppermute(values, "z", [(0, 2), (1, 3), (2, 0), (3, 1)])
    return flip(values, axis)


def pick(stack, index, axis=0):
    return lax.dynamic_index_in_dim(stack, index, axis, keepdims=False)


def in_order(mine, other, bit, axis):
    return jnp.where(
        bit == 0, jnp.stack([mine, other], axis), jnp.stack([other, mine], axis)
    )


def spread_steps(pieces):
    x, c = lax.axis_index("x"), lax.axis_index("c")
    pieces = pieces.reshape((2, 2) + pieces.shape[1:])
    (got,) = yield [(pick(pieces, 1 - x), "x")]
    pieces = in_order(pick(pieces, x), got, x, 0)
    (got,) = yield [(pick(pieces, 1 - c, 1), "c")]
    pieces = in_order(pick(pieces, c, 1), got, c, 1)
    return pieces.reshape((4,) + pieces.shape[2:])


def complete(steps):
    try:
        wanted = next(steps)
        while True:
            wanted = steps.send([flip(*w) for w in wanted])
    except StopIteration as end:
        return end.value


def spread(pieces):
    return complete(spread_steps(pieces))


class Lines:
    def __init__(self):
        self.wanted = {}
        self.flying = {}
        self.results = {}
        self.last = []
        self.extra = []

    def start(self, name, steps):
        self.wanted[name] = (steps, next(steps))

    def launch(self, name):
        steps, wanted = self.wanted.pop(name)
        wanted = [(after(v, *self.last) if self.last else v, axis) for v, axis in wanted]
        self.extra += [v for v, _ in wanted]
        self.flying[name] = (steps, [send(v, axis) for v, axis in wanted])

    def land(self, name):
        steps, got = self.flying.pop(name)
        self.proceed(name, steps, after(got, *self.last))

    def proceed(self, name, steps, got):
        try:
            self.wanted[name] = (steps, steps.send(got))
        except StopIteration as end:
            self.results[name] = end.value
            value = end.value[-1] if isinstance(end.value, list) else end.value
            if value is not None:
                self.extra.append(value)
            if name == "mixed":
                self.extra += list(got)

    def tick(self, large, *names):
        if large is None:
            for name in names:
                steps, wanted = self.wanted.pop(name)
                wanted = [(after(v, *self.last) if self.last else v, axis) for v, axis in wanted]
                self.proceed(name, steps, [send(*w) for w in wanted])
            return None
        sent = {}
        for name in names:
            steps, wanted = self.wanted.pop(name)
            sent[name] = (steps, [(after(v, *self.last) if self.last else v, axis) for v, axis in wanted])
        operands = [v for _, part in sent.values() for v, _ in part]
        done = large(self.last + self.extra + operands)
        self.extra = []
        self.last = [done[0] if isinstance(done, (tuple, list)) else done]
        for name, (steps, wanted) in sent.items():
            self.proceed(name, steps, after([send(*w) for w in wanted], *self.last))
        return done


def row_gather(values):
    x, c = lax.axis_index("x"), lax.axis_index("c")
    pair = in_order(values, flip(values, "x"), x, 0)
    four = in_order(pair, flip(pair, "c"), c, 1)
    return four.reshape((4,) + values.shape)


def row_sum(values):
    values = values + flip(values, "x")
    return values + flip(values, "c")


def halves(values):
    middle = values.shape[0] // 2
    return values[:middle], values[middle:]


def place_steps(own):
    from_x, from_y, from_c = yield [(own, "x"), (own, "y"), (own, "c")]
    former, latter, by_x, by_y = yield [
        (halves(from_y)[0], "x"),
        (halves(from_x)[1], "y"),
        (from_x, "c"),
        (from_y, "c"),
    ]
    corner = jnp.concatenate([former, latter], 0)
    (other,) = yield [(corner, "c")]
    return [own, from_c, from_x, by_x, from_y, by_y, corner, other]


def gather_steps(own):
    from_x, from_y = yield [(own, "x"), (own, "y")]
    former, latter = yield [(halves(from_y)[0], "x"), (halves(from_x)[1], "y")]
    four = jnp.concatenate([own, from_x, from_y, former, latter], 0)
    (other,) = yield [(four, "c")]
    return [four, other]


def sum_steps(keep, send):
    (got,) = yield [(send, "c")]
    sums = [halves((keep[k].astype(F32) + got[k].astype(F32)).astype(BF)) for k in range(4)]
    to_x = jnp.stack([sums[1][0], sums[3][0]])
    to_y = jnp.stack([sums[2][1], sums[3][1]])
    by_x, by_y = yield [(to_x, "x"), (to_y, "y")]
    over_y = (sums[2][0].astype(F32) + by_x[1].astype(F32)).astype(BF)
    over_x = (sums[1][1].astype(F32) + by_y[1].astype(F32)).astype(BF)
    former = sums[0][0].astype(F32) + by_x[0].astype(F32)
    latter = sums[0][1].astype(F32) + by_y[0].astype(F32)
    by_y, by_x = yield [(over_y, "y"), (over_x, "x")]
    return jnp.concatenate([former + by_y.astype(F32), latter + by_x.astype(F32)], 0)


def norm_kernel(mode, heads, places, *refs):
    own, other, refs = refs[:4], refs[4:8], refs[8:]
    if mode:
        gain, weight, cosine, sine, low, share, qkv, knat, vnat, whole = refs
    else:
        low, share, whole = refs
    half, row, rank = places[0], places[1], places[2]
    mine = pl.program_id(0) // (BLOCKS // 2) == half
    width = own[0].shape[1]

    def place(sources):
        for k, source in enumerate(sources):
            at = pl.multiple_of((row ^ k) * width, width)
            whole[:, pl.ds(at, width)] = source[...]

    @pl.when(mine)
    def _():
        place(own)

    @pl.when(jnp.logical_not(mine))
    def _():
        place(other)

    sub = share.shape[0]
    for k in range(BLK // sub):
        at = pl.multiple_of((rank ^ k) * sub, sub)
        rows = whole[pl.ds(at, sub), :]
        if k == 0:
            share[...] = rows
        if not mode:
            low[k * sub : (k + 1) * sub, :] = rows
        else:
            wide = rows.astype(F32)
            scale = lax.rsqrt(jnp.sum(wide * wide, 1, keepdims=True) / wide.shape[1] + EPSILON)
            low[k * sub : (k + 1) * sub, :] = (wide * scale * gain[...]).astype(BF)
    if mode:
        project_kernel(heads, weight, low, cosine, sine, qkv, knat, vnat)


def assemble(places, pieces, gain, sub, projection=(), heads=0):
    per = BLOCKS // 2
    width = pieces[0].shape[1]
    whole = 4 * width
    mode = gain is not None

    def own_map(i, places):
        return jnp.where(i // per == places[0], i % per, 0), 0

    def other_map(i, places):
        return jnp.where(i // per == places[0], 0, i % per), 0

    operands = list(pieces)
    specs = [pl.BlockSpec((BLK, width), own_map)] * 4 + [pl.BlockSpec((BLK, width), other_map)] * 4
    outs = [pl.BlockSpec((BLK, whole), lambda i, p: (i, 0)), pl.BlockSpec((sub, whole), lambda i, p: (i, 0))]
    shapes = [jax.ShapeDtypeStruct((GTOK, whole), BF), jax.ShapeDtypeStruct((BLOCKS * sub, whole), BF)]
    flops = 0
    if mode:
        table = pl.BlockSpec((HD // 2, BLK), lambda i, p: (0, i))
        specs += [pl.BlockSpec((1, whole), lambda i, p: (0, 0))]
        specs += [pl.BlockSpec(projection[0].shape, lambda i, p: (0, 0)), table, table]
        operands += [gain.reshape(1, whole), *projection]
        outs += [pl.BlockSpec((heads * ROWS, BLK), lambda i, p: (0, i))]
        outs += [pl.BlockSpec((heads, BLK, HD), lambda i, p: (0, i, 0))] * 2
        natural = jax.ShapeDtypeStruct((heads, GTOK, HD), BF)
        shapes += [jax.ShapeDtypeStruct((heads * ROWS, GTOK), BF), natural, natural]
        flops = 2 * GTOK * whole * heads * ROWS
    return pl.pallas_call(
        functools.partial(norm_kernel, mode, heads),
        grid_spec=pltpu.PrefetchScalarGridSpec(
            num_scalar_prefetch=1,
            grid=(BLOCKS,),
            in_specs=specs,
            out_specs=outs,
            scratch_shapes=[pltpu.VMEM((BLK, whole), BF)],
        ),
        out_shape=shapes,
        compiler_params=params(),
        cost_estimate=cost(flops + GTOK * whole * 6, GTOK * whole * 5),
    )(places, *operands)


def straighten(values, rank):
    count = values.shape[1]
    return jnp.stack([pick(values, j ^ rank, 1) for j in range(count)], 1)


def whole_spec(shape):
    return pl.BlockSpec(shape, lambda *i, n=len(shape): (0,) * n)


def cost(flops, bytes_accessed, transcendentals=0):
    return pl.CostEstimate(
        flops=int(flops), bytes_accessed=int(bytes_accessed), transcendentals=int(transcendentals)
    )


def params():
    return pltpu.CompilerParams(vmem_limit_bytes=VMEM_LIMIT)


def split_kernel(pairs, form, sub, *refs):
    keep, send = refs[2 * pairs :]
    total = mm(refs[0][...], refs[1][...], form)
    for p in range(1, pairs):
        total += mm(refs[2 * p][...], refs[2 * p + 1][...], form)
    low = total.astype(BF)
    for b in range(low.shape[0] // BLK):
        for k in range(8):
            target = send if k % 2 else keep
            start = b * BLK + k * sub
            target[k // 2, b * sub : (b + 1) * sub, :] = low[start : start + sub]


def split_product(pairs, form):
    width = pairs[0][1].shape[1]
    rows = pairs[0][0].shape[1 if form == TN else 0]
    depth = pairs[0][1].shape[0]
    tile = 512
    sub = BLK // 8
    specs, operands = [], []
    for left, right in pairs:
        specs += [whole_spec(left.shape), pl.BlockSpec((depth, tile), lambda j: (0, j))]
        operands += [left, right]
    shape = (4, rows // 8, width)
    return pl.pallas_call(
        functools.partial(split_kernel, len(pairs), form, sub),
        grid=(width // tile,),
        in_specs=specs,
        out_specs=[pl.BlockSpec((4, rows // 8, tile), lambda j: (0, 0, j))] * 2,
        out_shape=[jax.ShapeDtypeStruct(shape, BF)] * 2,
        compiler_params=params(),
        cost_estimate=cost(
            2 * rows * depth * width * len(pairs),
            2 * (rows * width + (rows + width) * depth * len(pairs)),
        ),
    )(*operands)


def mix_kernel(parts, sub, *refs):
    weight, keep, send = refs[parts:]
    at = 0
    for left in refs[:parts]:
        low = mm(left[...], weight[...]).astype(BF)
        for b in range(low.shape[0] // BLK):
            for k in range(8):
                target = send if k % 2 else keep
                start = b * BLK + k * sub
                target[k // 2, at : at + sub, :] = low[start : start + sub]
            at += sub


def mix_product(parts, weight):
    width = weight.shape[1]
    rows = sum(a.shape[0] for a in parts)
    tile = 256
    return pl.pallas_call(
        functools.partial(mix_kernel, len(parts), BLK // 8),
        grid=(width // tile,),
        in_specs=[whole_spec(a.shape) for a in parts]
        + [pl.BlockSpec((weight.shape[0], tile), lambda j: (0, j))],
        out_specs=[pl.BlockSpec((4, rows // 8, tile), lambda j: (0, 0, j))] * 2,
        out_shape=[jax.ShapeDtypeStruct((4, rows // 8, width), BF)] * 2,
        compiler_params=params(),
        cost_estimate=cost(2 * rows * weight.size, 2 * (rows * width + rows * weight.shape[0])),
    )(*parts, weight)


def join_rows(pieces, target):
    if len(pieces) == 1:
        target[...] = pieces[0][...]
        return
    blocks = target.shape[0] // BLK
    sub = BLK // 8
    for b in range(blocks):
        for k in range(8):
            start = b * BLK + k * sub
            source = ((k // 2) * blocks + b) * sub
            target[start : start + sub, :] = pieces[k % 2][source : source + sub, :]


def unit_kernel(count, *refs):
    pieces, (gates, ups, low, gate_out, up_out, hidden) = refs[:count], refs[count:]

    @pl.when(pl.program_id(0) == 0)
    def _():
        join_rows(pieces, low)

    rows = low[...]
    gate = mm(rows, gates[...], NT)
    up = mm(rows, ups[...], NT)
    gate_out[...] = gate.astype(BF)
    up_out[...] = up.astype(BF)
    hidden[...] = (gate * jax.nn.sigmoid(gate) * up).astype(BF)


def unit_products(pieces, gates, ups):
    rows = sum(p.shape[0] for p in pieces)
    units, depth = gates.shape
    tile = min(units, 256)
    weight = pl.BlockSpec((tile, depth), lambda j: (j, 0))
    result = pl.BlockSpec((rows, tile), lambda j: (0, j))
    return pl.pallas_call(
        functools.partial(unit_kernel, len(pieces)),
        grid=(units // tile,),
        in_specs=[whole_spec(p.shape) for p in pieces] + [weight, weight],
        out_specs=[whole_spec((rows, depth)), result, result, result],
        out_shape=[jax.ShapeDtypeStruct((rows, depth), BF)]
        + [jax.ShapeDtypeStruct((rows, units), BF)] * 3,
        compiler_params=params(),
        cost_estimate=cost(4 * rows * depth * units, 4 * depth * (rows + units), rows * units),
    )(*pieces, gates, ups)


def unit_grad_kernel(upstream, downs, gate_in, up_in, d_gate, d_up):
    d_hidden = mm(upstream[...], downs[...], NT)
    gate, up = gate_in[...].astype(F32), up_in[...].astype(F32)
    sigma = jax.nn.sigmoid(gate)
    silu = gate * sigma
    d_gate[...] = (d_hidden * up * (sigma + silu * (1.0 - sigma))).astype(BF)
    d_up[...] = (d_hidden * silu).astype(BF)


def unit_grads(upstream, first, rows, downs, gate, up):
    units, depth = downs.shape
    tile = min(units, 256)
    result = pl.BlockSpec((rows, tile), lambda j: (0, j))
    return pl.pallas_call(
        unit_grad_kernel,
        grid=(units // tile,),
        in_specs=[
            pl.BlockSpec((pl.Element(rows), pl.Element(depth)), lambda j: (first, 0)),
            pl.BlockSpec((tile, depth), lambda j: (j, 0)),
            result,
            result,
        ],
        out_specs=[result, result],
        out_shape=[jax.ShapeDtypeStruct((rows, units), BF)] * 2,
        compiler_params=params(),
        cost_estimate=cost(2 * rows * depth * units, 4 * depth * (rows + units), rows * units),
    )(upstream, downs, gate, up)


def head_kernel(count, *refs):
    pieces, (weight, joined, result) = refs[:count], refs[count:]
    join_rows(pieces, joined)
    result[...] = mm(weight[...], joined[...], NT).astype(BF)


def head_product(pieces, weight):
    depth = weight.shape[1]
    rows = sum(p.shape[0] for p in pieces)
    return pl.pallas_call(
        functools.partial(head_kernel, len(pieces)),
        out_shape=[
            jax.ShapeDtypeStruct((rows, depth), BF),
            jax.ShapeDtypeStruct((weight.shape[0], rows), BF),
        ],
        compiler_params=params(),
        cost_estimate=cost(2 * rows * depth * weight.shape[0], 4 * rows * depth),
    )(*pieces, weight)


def grad_kernel(parts, form, starts, *refs):
    rights = refs[parts:-1]
    total = None
    for p in range(parts):
        left = refs[p][...]
        if starts:
            count = left.shape[0]
            right = rights[0][starts[p] : starts[p] + count, :]
        else:
            right = rights[p][...]
        term = mm(left, right, form)
        total = term if total is None else total + term
    refs[-1][...] = total.astype(BF)


def grad_product(lefts, rights, form=TN, starts=()):
    rows = lefts[0].shape[1 if form == TN else 0]
    width = rights[0].shape[1]
    tile = 512
    tokens = sum(r.shape[0] for r in rights)
    return pl.pallas_call(
        functools.partial(grad_kernel, len(lefts), form, starts),
        grid=(width // tile,),
        in_specs=[whole_spec(a.shape) for a in lefts]
        + [pl.BlockSpec((b.shape[0], tile), lambda j: (0, j)) for b in rights],
        out_specs=pl.BlockSpec((rows, tile), lambda j: (0, j)),
        out_shape=jax.ShapeDtypeStruct((rows, width), BF),
        compiler_params=params(),
        cost_estimate=cost(2 * rows * width * tokens, 2 * tokens * (rows + width)),
    )(*lefts, *rights)


def join_kernel(d_qkv, low, weight, grad, share):
    total = mm(d_qkv[...], low[...])
    grad[...] = total.astype(BF)
    sums = jnp.sum(total * weight[...].astype(F32), 0, keepdims=True)
    share[...] = jnp.broadcast_to(sums, share.shape)


def join_product(d_qkv, low, weight):
    rows, width = weight.shape
    tile = 512
    return pl.pallas_call(
        join_kernel,
        grid=(width // tile,),
        in_specs=[
            whole_spec(d_qkv.shape),
            pl.BlockSpec((low.shape[0], tile), lambda j: (0, j)),
            pl.BlockSpec((rows, tile), lambda j: (0, j)),
        ],
        out_specs=[
            pl.BlockSpec((rows, tile), lambda j: (0, j)),
            pl.BlockSpec((8, tile), lambda j: (0, j)),
        ],
        out_shape=[jax.ShapeDtypeStruct((rows, width), BF), jax.ShapeDtypeStruct((8, width), F32)],
        compiler_params=params(),
        cost_estimate=cost(2 * rows * width * low.shape[0], 2 * low.shape[0] * (rows + width)),
    )(d_qkv, low, weight)


def last_kernel(places, d_qkv, weight, keep, send, whole):
    row, rank = places[1], places[2]
    sub = BLK // 8
    width = keep.shape[2]
    whole[...] = mm(d_qkv[...], weight[...], TN).astype(BF)
    for k in range(8):
        at = pl.ds(pl.multiple_of((rank ^ k) * sub, sub), sub)
        for j in range(4):
            target = send if j % 2 else keep
            source = pl.ds(pl.multiple_of((row ^ j) * width, width), width)
            target[j // 2, at, :] = whole[k * sub : (k + 1) * sub, source]


def last_product(places, d_qkv, weight):
    depth = weight.shape[1]
    per = BLOCKS // 2

    def out_map(i, places):
        return ((i // per) ^ places[0], i % per, 0)

    return pl.pallas_call(
        last_kernel,
        grid_spec=pltpu.PrefetchScalarGridSpec(
            num_scalar_prefetch=1,
            grid=(BLOCKS,),
            in_specs=[
                pl.BlockSpec((d_qkv.shape[0], BLK), lambda i, places: (0, i)),
                pl.BlockSpec(weight.shape, lambda i, places: (0, 0)),
            ],
            out_specs=[pl.BlockSpec((2, BLK, depth // 4), out_map)] * 2,
            scratch_shapes=[pltpu.VMEM((BLK, depth), BF)],
        ),
        out_shape=[jax.ShapeDtypeStruct((4, GTOK // 2, depth // 4), BF)] * 2,
        compiler_params=params(),
        cost_estimate=cost(2 * GTOK * depth * d_qkv.shape[0], 2 * GTOK * depth),
    )(places, d_qkv, weight)


def columns_of(values, count, width):
    return jnp.stack([values[..., k * width : (k + 1) * width] for k in range(count)])


def local(
    quick,
    hidden_in,
    gain_before,
    query_weight,
    key_weight,
    value_weight,
    output_weight,
    gain_middle,
    gate_weight,
    up_weight,
    down_weight,
    cotangent,
    branch_points,
    lengths,
):
    width = hidden_in.shape[1]
    depth = 4 * width
    head_width = query_weight.shape[1]
    heads = head_width // HD
    units = gate_weight.shape[1]
    local_tokens = hidden_in.shape[0]
    team = 4 * lax.axis_size("y")
    sub = BLK // team
    x, c = lax.axis_index("x"), lax.axis_index("c")
    z, y = lax.axis_index("z"), lax.axis_index("y")
    row = 2 * x + c
    rank = 4 * y + row
    order = rank if quick else jnp.int32(0)
    branch_row = pick(branch_points, z)
    length_row = pick(lengths, z)
    info = jnp.concatenate([branch_row, length_row, jnp.stack([order * sub])]).astype(jnp.int32)
    places = jnp.stack([y, row, rank]).astype(jnp.int32)

    def full_gather(share):
        blocks = share.shape[0] // sub
        got = lax.all_gather(share.reshape(blocks, sub, depth), TEAM, axis=1, tiled=False)
        return [got.reshape(-1, depth)]

    def full_scatter(partial):
        parts = partial.reshape(-1, team, sub, depth)
        parts = lax.psum_scatter(parts, TEAM, scatter_dimension=1, tiled=False)
        return parts.reshape(-1, depth).astype(F32)

    lines = Lines()
    tick = lines.tick

    def unit_rows(weight):
        pieces = yield from spread_steps(weight.reshape(4, units // 4, width))
        pieces = jnp.concatenate([pieces[k] for k in range(4)], 1)
        if quick:
            lines.extra.append(pieces)
        return [lax.all_gather(pieces, "z", axis=0, tiled=True), pieces]

    joined = jnp.stack([query_weight.T, key_weight.T, value_weight.T, output_weight])
    if heads % 4 == 0:
        per = heads // 4
        pieces = joined.reshape(4, 4, per * HD, width).transpose(1, 0, 2, 3)
        if quick:
            from_y = flip(hidden_in, "y")
            lines.start("heads", spread_steps(pieces))
            tick(None, "heads")
            lines.start("gate", unit_rows(after(gate_weight, lines.wanted["heads"][1][0][0]).T))
            tick(None, "heads")
            tick(None, "gate")
            from_x = flip(after(hidden_in, lines.wanted["gate"][1][0][0]), "x")
            tick(None, "gate")
            pieces = lines.results["heads"]
        else:
            pieces = spread(pieces)
        pieces = jnp.concatenate([pieces[k] for k in range(4)], -1)
        pieces = pieces.reshape(4, per, HD, depth).transpose(1, 0, 2, 3).reshape(per, 4 * HD, depth)
        attend_weights = lax.all_gather(pieces, "z", axis=0, tiled=True)
    else:
        pieces = lax.all_gather(joined, "z", axis=0, tiled=False)
        pieces = spread(pieces).reshape(4, 4, heads, HD, width).transpose(2, 1, 3, 0, 4)
        attend_weights = pieces.reshape(heads, 4 * HD, depth)
    join_weight = attend_weights[:, :ROWS].reshape(heads * ROWS, depth)
    out_weight = attend_weights[:, ROWS:].reshape(heads * HD, depth)

    gains = row_gather(after(jnp.stack([gain_before, gain_middle]), pieces))
    gains = gains.transpose(1, 0, 2).reshape(2, depth)
    gain_one, gain_two = gains[0], gains[1]

    ids = jnp.arange(GTOK, dtype=jnp.int32)
    slot_ids = (ids % BLK) ^ (order * sub)
    starts = jnp.concatenate([jnp.arange(PBLKS, dtype=jnp.int32) * BLK, branch_row])
    positions = jnp.repeat(starts, BLK) + slot_ids
    frequency = THETA ** (-2.0 * jnp.arange(HD // 2, dtype=F32) / HD)
    angles = positions.astype(F32)[None, :] * frequency[:, None]
    cosine, sine = jnp.cos(angles), jnp.sin(angles)

    steps = range(len(CHUNKS))
    ordered = sorted(steps, key=lambda k: CHUNKS[k][0])
    rows_of = [count * BLK for _, count in CHUNKS]
    shares = [slice(first * sub, (first + count) * sub) for first, count in CHUNKS]
    starts = tuple(first * BLK for first, _ in CHUNKS)
    conts = [k for k in ordered if CHUNKS[k][0] >= PBLKS]
    prompts = [k for k in ordered if CHUNKS[k][0] < PBLKS]
    attentions, middles, scales, norms, d_middles, notes = ({} for _ in range(6))
    attended, d_heads = {}, {}

    def to_middle(k, attention):
        middle = residual[shares[k]].astype(F32) + attention
        scale_two = lax.rsqrt(jnp.mean(middle * middle, -1, keepdims=True) + EPSILON)
        norm_two = middle * scale_two
        attentions[k], middles[k], scales[k], norms[k] = attention, middle, scale_two, norm_two
        return (norm_two * gain_two).astype(BF)

    def to_d_middle(k, d_two):
        notes[k] = jnp.sum(d_two * norms[k], 0)
        scaled_two = d_two * gain_two
        inner_two = jnp.mean(scaled_two * norms[k], -1, keepdims=True)
        d_middle = upstream[shares[k]].astype(F32) + scales[k] * (scaled_two - norms[k] * inner_two)
        d_middles[k] = d_middle
        return d_middle.astype(BF)

    def backward(parts, ties, before=None):
        d_out = jnp.concatenate([d_heads[k] for k in parts], 1)
        heads_out = jnp.concatenate([heads_parts[k] for k in ordered], 1)
        lse = jnp.concatenate([lse_parts[k] for k in ordered], 1)
        source = after(qkv, *ties) if ties else qkv
        operands = (source, keys, values, d_out, heads_out, lse, cosine, sine)
        return attend_backward(info, operands, heads, before)

    def total(grad):
        return lax.psum_scatter(grad, "z", scatter_dimension=0, tiled=True)

    def home_steps(part):
        part = yield from spread_steps(columns_of(part, 4, width))
        return part.reshape(-1, width)

    def squares_one():
        wide = hidden_in.astype(F32)
        return jnp.sum(wide * wide, -1)

    def outcome(layer_out, share):
        here = jnp.arange(BLOCKS, dtype=jnp.int32)
        bound = jnp.where(here < PBLKS, BLK, jnp.take(length_row, jnp.maximum(here - PBLKS, 0)))
        slots = rank * sub + jnp.arange(sub, dtype=jnp.int32)
        valid = (slots[None, :] < bound[:, None]).astype(F32).reshape(-1)

        def square_sum(part, weights):
            return jnp.sum(weights * jnp.sum(part * part, -1))

        squares = jnp.stack(
            [square_sum(layer_out.astype(F32), valid)]
            + [
                sum(square_sum(parts[k], valid[shares[k]]) for k in steps)
                for parts in (attentions, d_middles)
            ]
        )
        before_local = share / gain_one
        middle_local = sum(notes[k] for k in steps)
        return jnp.concatenate([before_local, middle_local, squares])

    heads_parts, lse_parts, lows, gates, ups, hiddens = ([] for _ in range(6))
    gate_parts, up_parts = [], []
    if quick:
        former, latter = flip(halves(from_y)[0], "x"), flip(halves(from_x)[1], "y")
        corner = jnp.concatenate([former, latter], 0)
        four = [hidden_in, from_x, from_y, corner]
        hidden_pieces = [p for piece in four for p in (piece, flip(piece, "c"))]
        lines.start("up", unit_rows(up_weight.T))
        lines.start("down", unit_rows(down_weight))
        lines.start("late", place_steps(after(cotangent, corner)))
        lines.launch("late")
        low_one, residual, qkv, keys, values = tick(
            lambda ties: assemble(
                places,
                after(hidden_pieces, *ties),
                gain_one,
                sub,
                (join_weight, cosine, sine),
                heads,
            ),
            "up",
        )

        def forward_line(k, partial):
            low = to_middle(k, (yield from sum_steps(*partial)))
            return (yield from gather_steps(low))

        def attend(k, *names):
            def large(ties):
                return attend_forward(info, after(qkv, *ties), keys, heads, *CHUNKS[k])

            head_part, lse = tick(large, *names)
            heads_parts.append(head_part)
            lse_parts.append(lse)
            partial = split_product([(head_part, out_weight)], TN)
            lines.last = [partial[0]]
            lines.start(k, forward_line(k, partial))

        attend(0, "up")
        lines.land("late")
        attend(1, 0, "late")
        attend(2, 0, 1, "down", "late")
        attend(3, 0, 1, 2)
        gate_rows, up_rows = lines.results["gate"][0], lines.results["up"][0]
        upstream_rows, upstream = tick(
            lambda ties: assemble(places, after(lines.results["late"], *ties), None, sub), 0, 1, 3
        )

        def unit(k, *names):
            def large(ties):
                return unit_products(after(lines.results[k], *ties), gate_rows, up_rows)

            low, gate, up, hidden = tick(large, *names)
            lows.append(low)
            gates.append(gate)
            ups.append(up)
            hiddens.append(hidden)

        def gathered(k):
            lines.last = [lines.wanted[k][1][0][0]]
            tick(None, k)

        tick(None, 0, "down")
        down_rows = lines.results["down"][0]
        gathered(0)
        unit(0, 1, 2)
        tick(None, 1, 2)
        gathered(1)
        unit(1, 2, 3)
        tick(None, 2, 3)
        gathered(2)
        lines.extra.append(down_rows)
        unit(2, 3)
        tick(None, 3)
        gathered(3)
        unit(3)
        down_grad = tick(lambda ties: grad_product(hiddens, [after(upstream_rows, *ties)], TN, starts))
        down_sum = total(down_grad)

        def backward_line(k, partial):
            low = to_d_middle(k, (yield from sum_steps(*partial)))
            pieces = yield from gather_steps(low)
            attended[k], d_heads[k] = head_product(pieces, out_weight)
            return d_heads[k]

        def unit_grad(k, first, second):
            def large(ties):
                source = after(gates[k], *ties)
                return unit_grads(upstream_rows, starts[k], rows_of[k], down_rows, source, ups[k])

            d_gate, d_up = tick(large, *first)
            gate_parts.append(d_gate)
            up_parts.append(d_up)

            def more(ties):
                return split_product([(after(d_gate, *ties), gate_rows), (d_up, up_rows)], NN)

            lines.start(k, backward_line(k, tick(more, *second)))

        unit_grad(0, (), ())
        unit_grad(1, (0,), (0,))
        unit_grad(2, (0, 1), (0, 1))
        unit_grad(3, (0, 1, 2), (0, 1, 2))
        def summed(values, axes):
            for axis in axes:
                (got,) = yield [(values, axis)]
                values = values + got
            return values

        gate_grad = tick(lambda ties: grad_product(after(gate_parts, *ties), lows), 1, 2, 3)
        gate_sum = total(gate_grad)
        mixed = tick(
            lambda ties: mix_product(after([hiddens[k] for k in ordered], *ties), down_rows),
            1,
            2,
            3,
        )
        lines.start("mixed", sum_steps(*mixed))
        before = tick(lambda ties: backward(conts, ties), 2, 3, "mixed")
        lines.start("scale", summed(squares_one(), ("x", "c")))
        up_grad = tick(lambda ties: grad_product(after(up_parts, *ties), lows), 2, 3, "scale")
        up_sum = total(up_grad)
        tick(None, 3, "scale")
        tick(None, 3)
        lines.start("down", home_steps(down_sum))
        lines.start("gate", home_steps(gate_sum))
        d_qkv, inner = tick(lambda ties: backward(prompts, ties, before), "mixed", "down", "gate")
        inner = straighten(inner[0].reshape(BLOCKS, team, sub), rank).reshape(GTOK)
        lines.start("inner", summed(inner, ("x", "c", "y")))
        lines.start("up", home_steps(up_sum))
        own, other = tick(
            lambda ties: last_product(places, after(d_qkv, *ties), join_weight),
            "mixed",
            "down",
            "gate",
            "inner",
        )
        lines.start("last", sum_steps(own, other))
        mixed = lines.results["mixed"]
        layer_out = (jnp.concatenate([middles[k] for k in ordered], 0) + mixed).astype(BF)
        rows = local_tokens // team
        layer_pieces = jnp.stack(
            [
                layer_out[h * rows : (h + 1) * rows, k * width : (k + 1) * width]
                for h in range(2)
                for k in range(4)
            ]
        )
        lines.extra.append(layer_pieces)
        layer_pieces = lax.all_to_all(layer_pieces, TEAM, 0, 0, tiled=True)
        join_grad, share = tick(
            lambda ties: join_product(after(d_qkv, *ties), low_one, join_weight),
            "last",
            "up",
            "inner",
        )
        join_sum = total(join_grad)
        out_grad = tick(
            lambda ties: grad_product(
                after([heads_parts[k] for k in ordered], *ties), [attended[k] for k in ordered], NN
            ),
            "last",
            "inner",
            "up",
        )
        turned = lines.wanted["last"][1][0][0]
        sums = outcome(after(layer_out, out_grad), share[0])
        lines.start("sums", summed(after(sums, turned), ("c", "z1", "z2", "x", "y")))
        tick(None, "last")
        for _ in range(5):
            tick(None, "sums")
        d_one, inner, sums = (lines.results[n] for n in ("last", "inner", "sums"))
        join_sum, up_home = after((join_sum, lines.results["up"]), turned)
        lines.results["up"] = up_home
        lines.results["gate"], lines.results["down"], attended, layer_pieces, inner = after(
            (lines.results["gate"], lines.results["down"], attended, layer_pieces, inner), out_grad
        )
        gate_grad, up_grad, down_grad = (lines.results[n] for n in ("gate", "up", "down"))
    else:

        def full(values):
            values = lax.all_gather(values, "y", axis=0, tiled=True)
            return lax.all_gather(values, ROW, axis=1, tiled=True)

        def share_of(values):
            return pick(values.reshape(BLOCKS, team, sub, depth), rank, 1).reshape(-1, depth)

        gate_rows = complete(unit_rows(gate_weight.T))[0]
        up_rows = complete(unit_rows(up_weight.T))[0]
        down_rows = complete(unit_rows(down_weight))[0]
        hidden_rows = full(hidden_in)
        upstream_rows = full(cotangent)
        residual, upstream = share_of(hidden_rows), share_of(upstream_rows)
        wide = hidden_rows.astype(F32)
        scale = lax.rsqrt(jnp.mean(wide * wide, -1, keepdims=True) + EPSILON)
        low_one = (wide * scale * gain_one).astype(BF)
        qkv, keys, values = project(join_weight, low_one, cosine, sine, heads)
        for k in steps:
            head_part, lse = attend_forward(info, qkv, keys, heads, *CHUNKS[k])
            heads_parts.append(head_part)
            lse_parts.append(lse)
            low = to_middle(k, full_scatter(mm(head_part, out_weight, TN).astype(BF)))
            low, gate, up, hidden = unit_products(full_gather(low), gate_rows, up_rows)
            lows.append(low)
            hiddens.append(hidden)
            d_gate, d_up = unit_grads(upstream_rows, starts[k], rows_of[k], down_rows, gate, up)
            gate_parts.append(d_gate)
            up_parts.append(d_up)
            partial = (mm(d_gate, gate_rows) + mm(d_up, up_rows)).astype(BF)
            low = to_d_middle(k, full_scatter(partial))
            attended[k], d_heads[k] = head_product(full_gather(low), out_weight)
        gate_sum, up_sum = total(grad_product(gate_parts, lows)), total(grad_product(up_parts, lows))
        down_sum = total(grad_product(hiddens, [upstream_rows], TN, starts))
        mixed = full_scatter(
            jnp.concatenate([mm(hiddens[k], down_rows).astype(BF) for k in ordered], 0)
        )
        d_qkv, inner = backward(prompts, [], backward(conts, []))
        partial = mm(d_qkv, join_weight, TN).astype(BF)
        join_grad, share = join_product(d_qkv, low_one, join_weight)
        out_grad = grad_product([heads_parts[k] for k in ordered], [attended[k] for k in ordered], NN)
        layer_out = (jnp.concatenate([middles[k] for k in ordered], 0) + mixed).astype(BF)
        sums = lax.psum(outcome(layer_out, share[0]), EVERY)
        gate_grad, up_grad, down_grad = (
            complete(home_steps(part)) for part in (gate_sum, up_sum, down_sum)
        )

    attended = [attended[k] for k in ordered]
    gate_grad, up_grad = gate_grad.T.astype(F32), up_grad.T.astype(F32)
    down_grad = down_grad.astype(F32)
    if heads % 4 == 0:
        part = join_sum if quick else total(join_grad)
        part = part.reshape(heads // 4, 3, HD, depth).transpose(1, 0, 2, 3)
        part = spread(columns_of(part.reshape(3, heads // 4 * HD, depth), 4, width))
        part = part.transpose(1, 0, 2, 3).reshape(3, head_width, width)
        out_part = spread(columns_of(total(out_grad), 4, width)).reshape(1, head_width, width)
        part = jnp.concatenate([part, out_part], 0)
    else:
        part = jnp.concatenate(
            [join_grad.reshape(heads, 3, HD, depth), out_grad.reshape(heads, 1, HD, depth)], 1
        ).transpose(1, 0, 2, 3)
        part = spread(columns_of(part.reshape(4, heads * HD, depth), 4, width))
        part = lax.psum_scatter(part, "z", scatter_dimension=0, tiled=False)
    query_grad, key_grad, value_grad = (part[k].T.astype(F32) for k in range(3))
    output_grad = part[3].astype(F32)

    if quick:
        half = local_tokens
        inner = pick(inner.reshape(2, half), y)
        d_middle = jnp.concatenate(
            [lax.dynamic_slice_in_dim(a, row * width, width, 1) for a in attended], 0
        )
        d_middle = pick(d_middle.reshape(2, BLOCKS // 2, team, sub, width), y)
        d_middle = straighten(d_middle, rank).reshape(half, width).astype(F32)
        layer_out = layer_pieces.reshape(team, BLOCKS // 2, sub, width).transpose(1, 0, 2, 3)
        layer_out = layer_out.reshape(half, width)
    else:
        d_one = lax.psum_scatter(partial, "y", scatter_dimension=0, tiled=True)
        d_one = lax.psum_scatter(d_one, ROW, scatter_dimension=1, tiled=True).astype(F32)
        inner = lax.psum(inner[0], TEAM)
        inner = lax.dynamic_slice(inner, (y * local_tokens,), (local_tokens,))
        corner = (y * local_tokens, row * width)
        d_middle = lax.dynamic_slice(
            jnp.concatenate(attended, 0), corner, (local_tokens, width)
        ).astype(F32)
        layer_out = lax.all_gather(
            layer_out.reshape(BLOCKS, sub, depth), TEAM, axis=1, tiled=False
        ).reshape(GTOK, depth)
        layer_out = lax.dynamic_slice(layer_out, corner, (local_tokens, width))
    wide = hidden_in.astype(F32)
    row_squares = lines.results["scale"] if quick else row_sum(squares_one())
    scale_one = lax.rsqrt(row_squares / depth + EPSILON)[:, None]
    norm_one = wide * scale_one
    input_grad = d_middle + scale_one * (d_one * gain_before - norm_one * (inner / depth)[:, None])

    before_grad = lax.dynamic_slice(sums, (row * width,), (width,))
    middle_grad = lax.dynamic_slice(sums, (depth + row * width,), (width,))
    valid_count = (lengths.shape[0] * PROMPT + jnp.sum(lengths)).astype(F32)
    rms_values = jnp.sqrt(sums[2 * depth :] / (valid_count * depth))
    return (
        layer_out,
        input_grad,
        before_grad,
        query_grad,
        key_grad,
        value_grad,
        output_grad,
        middle_grad,
        gate_grad,
        up_grad,
        down_grad,
        rms_values,
    )


def solution(mesh):
    split = mesh.shape["col"] // GROUPS
    grid = Mesh(mesh.devices.reshape(2, 2, GROUPS, split), ("x", "c", "z", "y"))
    row, col = ("x", "c"), ("z", "y")
    return jax.shard_map(
        functools.partial(local, split == 2),
        mesh=grid,
        in_specs=(
            P(col, row),
            P(row),
            P(row, col),
            P(row, col),
            P(row, col),
            P(col, row),
            P(row),
            P(row, col),
            P(row, col),
            P(col, row),
            P(col, row),
            P(),
            P(),
        ),
        out_specs=(
            P(col, row),
            P(col, row),
            P(row),
            P(row, col),
            P(row, col),
            P(row, col),
            P(col, row),
            P(row),
            P(row, col),
            P(row, col),
            P(col, row),
            P(),
        ),
        check_vma=False,
    )
```

```python
import functools
import jax
import jax.numpy as jnp
from jax import lax
from jax.experimental import pallas as pl
from jax.experimental.pallas import tpu as pltpu
from jax.sharding import Mesh
from jax.sharding import PartitionSpec as P

HD = 64
PROMPT = 2048
CLEN = 256
CONTS = 6
GTOK = 3584
BLK = 256
PBLKS = PROMPT // BLK
BLOCKS = GTOK // BLK
ROWS = 3 * HD
BF = jnp.bfloat16
F32 = jnp.float32
LOW = -1e30
LOG2E = 1.4426950408889634
FACTOR = HD ** (-0.5) * LOG2E
VMEM_LIMIT = 56 * 1024 * 1024

NN = (((1,), (0,)), ((), ()))
NT = (((1,), (1,)), ((), ()))
TN = (((0,), (0,)), ((), ()))


def mm(a, b, dims=NN):
    return lax.dot_general(a, b, dims, preferred_element_type=F32)


def block_plan(info, block):
    cont = jnp.maximum(block - PBLKS, 0)
    is_cont = block >= PBLKS
    reach = info[cont]
    full = jnp.where(is_cont, reach // BLK, block)
    rest = jnp.where(is_cont, reach - full * BLK, 0)
    limit = jnp.where(is_cont, info[CONTS + cont], BLK)
    masked = 1 + (rest > 0).astype(jnp.int32)
    return full, rest, limit, masked


def local_ids(info, shape, axis):
    return lax.broadcasted_iota(jnp.int32, shape, axis) ^ info[2 * CONTS]


def masked_step(info, block, full, rest, limit, index):
    own = index == 0
    target = jnp.where(own, block, full)
    query_ids = local_ids(info, (1, BLK), 1)
    bound = jnp.where(own, jnp.minimum(query_ids + 1, limit), rest)
    key_ids = local_ids(info, (BLK, BLK), 0)
    return target, key_ids < bound


def columns(block):
    return pl.ds(pl.multiple_of(block * BLK, BLK), BLK)


def forward_kernel(heads, first, info, qkv, knat, out, lse, acc, top, tot):
    block = pl.program_id(0) + first
    full, rest, limit, masked = block_plan(info, block)
    here = columns(block)
    acc[...] = jnp.zeros_like(acc)
    top[...] = jnp.full_like(top, LOW)
    tot[...] = jnp.zeros_like(tot)

    def step(target, allowed, wide=1):
        span = pl.ds(pl.multiple_of(target * BLK, BLK), wide * BLK)
        weights, shrinks = [], []
        scores = [
            mm(knat[h, span, :], qkv[h * ROWS : h * ROWS + HD, here]) for h in range(heads)
        ]
        for h in range(heads):
            score = scores[h] * FACTOR
            if allowed is not None:
                score = jnp.where(allowed, score, LOW)
            old = top[h : h + 1, :]
            new = jnp.maximum(old, jnp.max(score, 0, keepdims=True))
            weight = jnp.exp2(score - new)
            shrink = jnp.exp2(old - new)
            top[h : h + 1, :] = new
            tot[h : h + 1, :] = tot[h : h + 1, :] * shrink + jnp.sum(weight, 0, keepdims=True)
            weights.append(weight.astype(BF))
            shrinks.append(shrink)
        for h in range(heads):
            value = qkv[h * ROWS + 2 * HD : (h + 1) * ROWS, span]
            acc[h] = acc[h] * shrinks[h] + mm(value, weights[h])

    def full_step(index, carry):
        step(index, None)
        return carry

    def mask_step(index, carry):
        target, allowed = masked_step(info, block, full, rest, limit, index)
        step(target, allowed)
        return carry

    def wide_step(index, carry):
        step(index * 4, None, 4)
        return carry

    lax.fori_loop(0, full // 4, wide_step, 0)

    @pl.when(full % 4 >= 2)
    def _():
        step(full // 4 * 4, None, 2)

    lax.fori_loop(full // 2 * 2, full, full_step, 0)
    lax.fori_loop(0, masked, mask_step, 0)
    for h in range(heads):
        total = tot[h : h + 1, :]
        out[h * HD : (h + 1) * HD, :] = (acc[h] / total).astype(BF)
        lse[h : h + 1, :] = top[h : h + 1, :] + jnp.log2(total)


def attend_forward(info, qkv, knat, heads, first, count):
    pad = max(8, heads)
    return pl.pallas_call(
        functools.partial(forward_kernel, heads, first),
        grid=(count,),
        in_specs=[
            pl.BlockSpec(memory_space=pltpu.SMEM),
            pl.BlockSpec(qkv.shape, lambda i: (0, 0)),
            pl.BlockSpec(knat.shape, lambda i: (0, 0, 0)),
        ],
        out_specs=[
            pl.BlockSpec((heads * HD, BLK), lambda i: (0, i)),
            pl.BlockSpec((pad, BLK), lambda i: (0, i)),
        ],
        out_shape=[
            jax.ShapeDtypeStruct((heads * HD, count * BLK), BF),
            jax.ShapeDtypeStruct((pad, count * BLK), F32),
        ],
        scratch_shapes=[
            pltpu.VMEM((heads, HD, BLK), F32),
            pltpu.VMEM((pad, BLK), F32),
            pltpu.VMEM((pad, BLK), F32),
        ],
        compiler_params=pltpu.CompilerParams(vmem_limit_bytes=VMEM_LIMIT),
        cost_estimate=pl.CostEstimate(
            flops=heads * count * 6 * BLK * BLK * 2560,
            bytes_accessed=16 << 20,
            transcendentals=heads * count * 6 * BLK * BLK,
        ),
    )(info, qkv, knat)


def turn(values, cosine, sine, at):
    half = HD // 2
    cos, sin = cosine[:, at], sine[:, at]
    former, latter = values[:half], values[half:]
    return former * cos + latter * sin, latter * cos - former * sin


def backward_kernel(heads, first, final, info, qkv, knat, vnat, d_out, heads_out, lse, cosine, sine, *refs):
    if final:
        d_old_keys, d_old_values, d_old_query, old_inner, d_qkv, inner, d_keys, d_values, d_query = refs
    else:
        d_keys, d_values, d_turned, share_out, d_query = refs
    block = pl.program_id(0) + first
    full, rest, limit, masked = block_plan(info, block)
    here = columns(block)
    there = columns(pl.program_id(0))

    @pl.when(pl.program_id(0) == 0)
    def _():
        if final:
            d_keys[...] = d_old_keys[...]
            d_values[...] = d_old_values[...]
            inner[...] = jnp.zeros_like(inner)
        else:
            d_keys[...] = jnp.zeros_like(d_keys)
            d_values[...] = jnp.zeros_like(d_values)

    d_query[...] = jnp.zeros_like(d_query)
    deltas = []
    for h in range(heads):
        rows = slice(h * HD, (h + 1) * HD)
        deltas.append(
            jnp.sum(d_out[rows, there].astype(F32) * heads_out[rows, here].astype(F32), 0, keepdims=True)
        )

    def step(target, allowed, wide=1):
        span = pl.ds(pl.multiple_of(target * BLK, BLK), wide * BLK)
        for first in range(0, heads, 4):
            team = range(first, min(first + 4, heads))
            scores = [
                mm(knat[h, span, :], qkv[h * ROWS : h * ROWS + HD, here]) for h in team
            ]
            d_probs = [
                mm(vnat[h, span, :], d_out[h * HD : (h + 1) * HD, there]) for h in team
            ]
            low_probs, d_scores = [], []
            for h, score, d_prob in zip(team, scores, d_probs):
                score = score * FACTOR - lse[h : h + 1, here]
                if allowed is not None:
                    score = jnp.where(allowed, score, LOW)
                probs = jnp.exp2(score)
                low_probs.append(probs.astype(BF))
                d_scores.append((probs * (d_prob - deltas[h])).astype(BF))
            for h, low, d_score in zip(team, low_probs, d_scores):
                rows = slice(h * HD, (h + 1) * HD)
                query = qkv[h * ROWS : h * ROWS + HD, here]
                key = qkv[h * ROWS + HD : h * ROWS + 2 * HD, span]
                d_query[h] += mm(key, d_score)
                d_keys[rows, span] += mm(query, d_score, NT)
                d_values[rows, span] += mm(d_out[rows, there], low, NT)

    def full_step(index, carry):
        step(index, None)
        return carry

    def mask_step(index, carry):
        target, allowed = masked_step(info, block, full, rest, limit, index)
        step(target, allowed)
        return carry

    def wide_step(index, carry):
        step(index * 2, None, 2)
        return carry

    lax.fori_loop(0, full // 2, wide_step, 0)
    lax.fori_loop(full // 2 * 2, full, full_step, 0)
    lax.fori_loop(0, masked, mask_step, 0)

    half = HD // 2
    share = jnp.zeros((1, BLK), F32)
    for h in range(heads):
        start = h * ROWS
        values = d_query[h] * HD ** (-0.5)
        share += jnp.sum(values * qkv[start : start + HD, here].astype(F32), 0, keepdims=True)
        low, high = turn(values, cosine, sine, here)
        if final:
            d_qkv[start : start + half, here] = low.astype(BF)
            d_qkv[start + half : start + HD, here] = high.astype(BF)
        else:
            d_turned[h * HD : h * HD + half, :] = low.astype(BF)
            d_turned[h * HD + half : (h + 1) * HD, :] = high.astype(BF)
    if not final:
        share_out[0:1, :] = share
        return
    inner[0:1, here] = share

    @pl.when(block == PBLKS - 1)
    def _():
        inner[:, PROMPT:] = old_inner[...]
        for h in range(heads):
            d_qkv[h * ROWS : h * ROWS + HD, PROMPT:] = d_old_query[h * HD : (h + 1) * HD, :]

        def finish(index, carry):
            at = columns(index)
            share = inner[0:1, at]
            for h in range(heads):
                start = h * ROWS + HD
                rows = slice(h * HD, (h + 1) * HD)
                values = d_keys[rows, at] * HD ** (-0.5)
                share += jnp.sum(values * qkv[start : start + HD, at].astype(F32), 0, keepdims=True)
                low, high = turn(values, cosine, sine, at)
                d_qkv[start : start + half, at] = low.astype(BF)
                d_qkv[start + half : start + HD, at] = high.astype(BF)
                start += HD
                values = d_values[rows, at]
                share += jnp.sum(values * qkv[start : start + HD, at].astype(F32), 0, keepdims=True)
                d_qkv[start : start + HD, at] = values.astype(BF)
            inner[0:1, at] = share
            return carry

        lax.fori_loop(0, BLOCKS, finish, 0)


def attend_backward(info, operands, heads, before=None):
    whole = lambda a: pl.BlockSpec(a.shape, lambda i, n=len(a.shape): (0,) * n)
    final = before is not None
    operands = tuple(operands) + (tuple(before) if final else ())
    sums = jax.ShapeDtypeStruct((heads * HD, GTOK), F32)
    rest = GTOK - PROMPT
    if final:
        shapes = [jax.ShapeDtypeStruct((heads * ROWS, GTOK), BF), jax.ShapeDtypeStruct((8, GTOK), F32)]
        specs = [whole(a) for a in shapes]
        scratch = [pltpu.VMEM(sums.shape, F32), pltpu.VMEM(sums.shape, F32)]
    else:
        shapes = [sums, sums, jax.ShapeDtypeStruct((heads * HD, rest), BF), jax.ShapeDtypeStruct((8, rest), F32)]
        specs = [whole(sums), whole(sums)]
        specs += [
            pl.BlockSpec((heads * HD, BLK), lambda i: (0, i)),
            pl.BlockSpec((8, BLK), lambda i: (0, i)),
        ]
        scratch = []
    return pl.pallas_call(
        functools.partial(backward_kernel, heads, 0 if final else PBLKS, final),
        grid=(PBLKS if final else CONTS,),
        in_specs=[pl.BlockSpec(memory_space=pltpu.SMEM)] + [whole(a) for a in operands],
        out_specs=specs,
        out_shape=shapes,
        scratch_shapes=scratch + [pltpu.VMEM((heads, HD, BLK), F32)],
        compiler_params=pltpu.CompilerParams(vmem_limit_bytes=VMEM_LIMIT),
        cost_estimate=pl.CostEstimate(
            flops=heads * BLOCKS * 3 * BLK * BLK * 4096,
            bytes_accessed=32 << 20,
            transcendentals=heads * BLOCKS * 3 * BLK * BLK,
        ),
    )(info, *operands)


def project_kernel(heads, weight, low, cosine, sine, qkv, knat, vnat):
    raw = mm(weight[...], low[...], NT)
    half = HD // 2
    cos, sin = cosine[...], sine[...]
    for h in range(heads):
        for part in range(2):
            start = h * ROWS + part * HD
            former, latter = raw[start : start + half], raw[start + half : start + HD]
            turned = jnp.concatenate(
                [former * cos - latter * sin, latter * cos + former * sin], 0
            )
            qkv[start : start + HD, :] = turned.astype(BF)
            if part:
                knat[h] = turned.T.astype(BF)
        start = h * ROWS + 2 * HD
        value = raw[start : start + HD]
        qkv[start : start + HD, :] = value.astype(BF)
        vnat[h] = value.T.astype(BF)


def project(weight, low, cosine, sine, heads):
    depth = weight.shape[1]
    natural = jax.ShapeDtypeStruct((heads, GTOK, HD), BF)
    return pl.pallas_call(
        functools.partial(project_kernel, heads),
        grid=(BLOCKS,),
        in_specs=[
            pl.BlockSpec(weight.shape, lambda i: (0, 0)),
            pl.BlockSpec((BLK, depth), lambda i: (i, 0)),
            pl.BlockSpec((HD // 2, BLK), lambda i: (0, i)),
            pl.BlockSpec((HD // 2, BLK), lambda i: (0, i)),
        ],
        out_specs=[pl.BlockSpec((heads * ROWS, BLK), lambda i: (0, i))]
        + [pl.BlockSpec((heads, BLK, HD), lambda i: (0, i, 0))] * 2,
        out_shape=[jax.ShapeDtypeStruct((heads * ROWS, GTOK), BF), natural, natural],
        compiler_params=pltpu.CompilerParams(vmem_limit_bytes=VMEM_LIMIT),
        cost_estimate=pl.CostEstimate(
            flops=2 * GTOK * depth * heads * ROWS, bytes_accessed=3 * GTOK * depth, transcendentals=0
        ),
    )(weight, low, cosine, sine)


EPSILON = 1e-05
THETA = 130000.0
GROUPS = 4
CHUNKS = ((8, 3), (11, 3), (0, 4), (4, 4))
ROW = ("x", "c")
TEAM = ("y", "x", "c")
EVERY = ("x", "c", "z", "y")


def after(values, *earlier):
    return lax.optimization_barrier((values, earlier))[0]


def flip(values, axis):
    return lax.ppermute(values, axis, [(0, 1), (1, 0)])


def send(values, axis):
    if axis == "z1":
        return lax.ppermute(values, "z", [(0, 1), (1, 0), (2, 3), (3, 2)])
    if axis == "z2":
        return lax.ppermute(values, "z", [(0, 2), (1, 3), (2, 0), (3, 1)])
    return flip(values, axis)


def pick(stack, index, axis=0):
    return lax.dynamic_index_in_dim(stack, index, axis, keepdims=False)


def in_order(mine, other, bit, axis):
    return jnp.where(
        bit == 0, jnp.stack([mine, other], axis), jnp.stack([other, mine], axis)
    )


def spread_steps(pieces):
    x, c = lax.axis_index("x"), lax.axis_index("c")
    pieces = pieces.reshape((2, 2) + pieces.shape[1:])
    (got,) = yield [(pick(pieces, 1 - x), "x")]
    pieces = in_order(pick(pieces, x), got, x, 0)
    (got,) = yield [(pick(pieces, 1 - c, 1), "c")]
    pieces = in_order(pick(pieces, c, 1), got, c, 1)
    return pieces.reshape((4,) + pieces.shape[2:])


def complete(steps):
    try:
        wanted = next(steps)
        while True:
            wanted = steps.send([flip(*w) for w in wanted])
    except StopIteration as end:
        return end.value


def spread(pieces):
    return complete(spread_steps(pieces))


class Lines:
    def __init__(self):
        self.wanted = {}
        self.flying = {}
        self.results = {}
        self.last = []
        self.extra = []

    def start(self, name, steps):
        self.wanted[name] = (steps, next(steps))

    def launch(self, name):
        steps, wanted = self.wanted.pop(name)
        wanted = [(after(v, *self.last) if self.last else v, axis) for v, axis in wanted]
        self.extra += [v for v, _ in wanted]
        self.flying[name] = (steps, [send(v, axis) for v, axis in wanted])

    def land(self, name):
        steps, got = self.flying.pop(name)
        self.proceed(name, steps, after(got, *self.last))

    def proceed(self, name, steps, got):
        try:
            self.wanted[name] = (steps, steps.send(got))
        except StopIteration as end:
            self.results[name] = end.value
            value = end.value[-1] if isinstance(end.value, list) else end.value
            if value is not None:
                self.extra.append(value)
            if name == "mixed":
                self.extra += list(got)

    def tick(self, large, *names):
        if large is None:
            for name in names:
                steps, wanted = self.wanted.pop(name)
                wanted = [(after(v, *self.last) if self.last else v, axis) for v, axis in wanted]
                self.proceed(name, steps, [send(*w) for w in wanted])
            return None
        sent = {}
        for name in names:
            steps, wanted = self.wanted.pop(name)
            sent[name] = (steps, [(after(v, *self.last) if self.last else v, axis) for v, axis in wanted])
        operands = [v for _, part in sent.values() for v, _ in part]
        done = large(self.last + self.extra + operands)
        self.extra = []
        self.last = [done[0] if isinstance(done, (tuple, list)) else done]
        for name, (steps, wanted) in sent.items():
            self.proceed(name, steps, after([send(*w) for w in wanted], *self.last))
        return done


def row_gather(values):
    x, c = lax.axis_index("x"), lax.axis_index("c")
    pair = in_order(values, flip(values, "x"), x, 0)
    four = in_order(pair, flip(pair, "c"), c, 1)
    return four.reshape((4,) + values.shape)


def row_sum(values):
    values = values + flip(values, "x")
    return values + flip(values, "c")


def halves(values):
    middle = values.shape[0] // 2
    return values[:middle], values[middle:]


def place_steps(own):
    from_x, from_y, from_c = yield [(own, "x"), (own, "y"), (own, "c")]
    former, latter, by_x, by_y = yield [
        (halves(from_y)[0], "x"),
        (halves(from_x)[1], "y"),
        (from_x, "c"),
        (from_y, "c"),
    ]
    corner = jnp.concatenate([former, latter], 0)
    (other,) = yield [(corner, "c")]
    return [own, from_c, from_x, by_x, from_y, by_y, corner, other]


def gather_steps(own):
    from_x, from_y = yield [(own, "x"), (own, "y")]
    former, latter = yield [(halves(from_y)[0], "x"), (halves(from_x)[1], "y")]
    four = jnp.concatenate([own, from_x, from_y, former, latter], 0)
    (other,) = yield [(four, "c")]
    return [four, other]


def sum_steps(keep, send):
    shape = (4, 2, keep.shape[1] // 2, keep.shape[2])

    def pair(*values):
        first, second = (v.reshape(shape) for v in values)
        return lambda *at: first[at].astype(F32) + second[at].astype(F32)

    (got,) = yield [(send, "c")]
    part = pair(keep, got)
    to_x = part(slice(1, 4, 2), 0).astype(BF)
    to_y = part(slice(2, 4), 1).astype(BF)
    by_x, by_y = yield [(to_x, "x"), (to_y, "y")]
    keep, got = after((keep, got), by_x, by_y)
    part = pair(keep, got)
    over_y = (part(2, 0) + by_x[1].astype(F32)).astype(BF)
    over_x = (part(1, 1) + by_y[1].astype(F32)).astype(BF)
    last_y, last_x = yield [(over_y, "y"), (over_x, "x")]
    keep, got = after((keep, got), last_y, last_x)
    part = pair(keep, got)
    former = part(0, 0) + by_x[0].astype(F32) + last_y.astype(F32)
    latter = part(0, 1) + by_y[0].astype(F32) + last_x.astype(F32)
    return jnp.concatenate([former, latter], 0)


def norm_kernel(mode, heads, places, *refs):
    own, other, refs = refs[:4], refs[4:8], refs[8:]
    if mode:
        gain, weight, cosine, sine, low, share, qkv, knat, vnat, whole = refs
    else:
        low, share, whole = refs
    half, row, rank = places[0], places[1], places[2]
    mine = pl.program_id(0) // (BLOCKS // 2) == half
    width = own[0].shape[1]

    def place(sources):
        for k, source in enumerate(sources):
            at = pl.multiple_of((row ^ k) * width, width)
            whole[:, pl.ds(at, width)] = source[...]

    @pl.when(mine)
    def _():
        place(own)

    @pl.when(jnp.logical_not(mine))
    def _():
        place(other)

    sub = share.shape[0]
    for k in range(BLK // sub):
        at = pl.multiple_of((rank ^ k) * sub, sub)
        rows = whole[pl.ds(at, sub), :]
        if k == 0:
            share[...] = rows
        if not mode:
            low[k * sub : (k + 1) * sub, :] = rows
        else:
            wide = rows.astype(F32)
            scale = lax.rsqrt(jnp.sum(wide * wide, 1, keepdims=True) / wide.shape[1] + EPSILON)
            low[k * sub : (k + 1) * sub, :] = (wide * scale * gain[...]).astype(BF)
    if mode:
        project_kernel(heads, weight, low, cosine, sine, qkv, knat, vnat)


def assemble(places, pieces, gain, sub, projection=(), heads=0):
    per = BLOCKS // 2
    width = pieces[0].shape[1]
    whole = 4 * width
    mode = gain is not None

    def own_map(i, places):
        return jnp.where(i // per == places[0], i % per, 0), 0

    def other_map(i, places):
        return jnp.where(i // per == places[0], 0, i % per), 0

    operands = list(pieces)
    specs = [pl.BlockSpec((BLK, width), own_map)] * 4 + [pl.BlockSpec((BLK, width), other_map)] * 4
    outs = [pl.BlockSpec((BLK, whole), lambda i, p: (i, 0)), pl.BlockSpec((sub, whole), lambda i, p: (i, 0))]
    shapes = [jax.ShapeDtypeStruct((GTOK, whole), BF), jax.ShapeDtypeStruct((BLOCKS * sub, whole), BF)]
    flops = 0
    if mode:
        table = pl.BlockSpec((HD // 2, BLK), lambda i, p: (0, i))
        specs += [pl.BlockSpec((1, whole), lambda i, p: (0, 0))]
        specs += [pl.BlockSpec(projection[0].shape, lambda i, p: (0, 0)), table, table]
        operands += [gain.reshape(1, whole), *projection]
        outs += [pl.BlockSpec((heads * ROWS, BLK), lambda i, p: (0, i))]
        outs += [pl.BlockSpec((heads, BLK, HD), lambda i, p: (0, i, 0))] * 2
        natural = jax.ShapeDtypeStruct((heads, GTOK, HD), BF)
        shapes += [jax.ShapeDtypeStruct((heads * ROWS, GTOK), BF), natural, natural]
        flops = 2 * GTOK * whole * heads * ROWS
    return pl.pallas_call(
        functools.partial(norm_kernel, mode, heads),
        grid_spec=pltpu.PrefetchScalarGridSpec(
            num_scalar_prefetch=1,
            grid=(BLOCKS,),
            in_specs=specs,
            out_specs=outs,
            scratch_shapes=[pltpu.VMEM((BLK, whole), BF)],
        ),
        out_shape=shapes,
        compiler_params=params(),
        cost_estimate=cost(flops + GTOK * whole * 6, GTOK * whole * 5),
    )(places, *operands)


def straighten(values, rank):
    count = values.shape[1]
    return jnp.stack([pick(values, j ^ rank, 1) for j in range(count)], 1)


def whole_spec(shape):
    return pl.BlockSpec(shape, lambda *i, n=len(shape): (0,) * n)


def cost(flops, bytes_accessed, transcendentals=0):
    return pl.CostEstimate(
        flops=int(flops), bytes_accessed=int(bytes_accessed), transcendentals=int(transcendentals)
    )


def params():
    return pltpu.CompilerParams(vmem_limit_bytes=VMEM_LIMIT)


def split_kernel(pairs, form, sub, *refs):
    keep, send = refs[2 * pairs :]
    total = mm(refs[0][...], refs[1][...], form)
    for p in range(1, pairs):
        total += mm(refs[2 * p][...], refs[2 * p + 1][...], form)
    low = total.astype(BF)
    for b in range(low.shape[0] // BLK):
        for k in range(8):
            target = send if k % 2 else keep
            start = b * BLK + k * sub
            target[k // 2, b * sub : (b + 1) * sub, :] = low[start : start + sub]


def split_product(pairs, form):
    width = pairs[0][1].shape[1]
    rows = pairs[0][0].shape[1 if form == TN else 0]
    depth = pairs[0][1].shape[0]
    tile = 512
    sub = BLK // 8
    specs, operands = [], []
    for left, right in pairs:
        specs += [whole_spec(left.shape), pl.BlockSpec((depth, tile), lambda j: (0, j))]
        operands += [left, right]
    shape = (4, rows // 8, width)
    return pl.pallas_call(
        functools.partial(split_kernel, len(pairs), form, sub),
        grid=(width // tile,),
        in_specs=specs,
        out_specs=[pl.BlockSpec((4, rows // 8, tile), lambda j: (0, 0, j))] * 2,
        out_shape=[jax.ShapeDtypeStruct(shape, BF)] * 2,
        compiler_params=params(),
        cost_estimate=cost(
            2 * rows * depth * width * len(pairs),
            2 * (rows * width + (rows + width) * depth * len(pairs)),
        ),
    )(*operands)


def mix_kernel(parts, sub, *refs):
    weight, keep, send = refs[parts:]
    at = 0
    for left in refs[:parts]:
        low = mm(left[...], weight[...]).astype(BF)
        for b in range(low.shape[0] // BLK):
            for k in range(8):
                target = send if k % 2 else keep
                start = b * BLK + k * sub
                target[k // 2, at : at + sub, :] = low[start : start + sub]
            at += sub


def mix_product(parts, weight):
    width = weight.shape[1]
    rows = sum(a.shape[0] for a in parts)
    tile = 256
    return pl.pallas_call(
        functools.partial(mix_kernel, len(parts), BLK // 8),
        grid=(width // tile,),
        in_specs=[whole_spec(a.shape) for a in parts]
        + [pl.BlockSpec((weight.shape[0], tile), lambda j: (0, j))],
        out_specs=[pl.BlockSpec((4, rows // 8, tile), lambda j: (0, 0, j))] * 2,
        out_shape=[jax.ShapeDtypeStruct((4, rows // 8, width), BF)] * 2,
        compiler_params=params(),
        cost_estimate=cost(2 * rows * weight.size, 2 * (rows * width + rows * weight.shape[0])),
    )(*parts, weight)


def join_rows(pieces, target):
    if len(pieces) == 1:
        target[...] = pieces[0][...]
        return
    blocks = target.shape[0] // BLK
    sub = BLK // 8
    for b in range(blocks):
        for k in range(8):
            start = b * BLK + k * sub
            source = ((k // 2) * blocks + b) * sub
            target[start : start + sub, :] = pieces[k % 2][source : source + sub, :]


def unit_kernel(count, *refs):
    pieces, (gates, ups, low, gate_out, up_out, hidden) = refs[:count], refs[count:]

    @pl.when(pl.program_id(0) == 0)
    def _():
        join_rows(pieces, low)

    rows = low[...]
    gate = mm(rows, gates[...], NT)
    up = mm(rows, ups[...], NT)
    gate_out[...] = gate.astype(BF)
    up_out[...] = up.astype(BF)
    hidden[...] = (gate * jax.nn.sigmoid(gate) * up).astype(BF)


def unit_products(pieces, gates, ups):
    rows = sum(p.shape[0] for p in pieces)
    units, depth = gates.shape
    tile = min(units, 256)
    weight = pl.BlockSpec((tile, depth), lambda j: (j, 0))
    result = pl.BlockSpec((rows, tile), lambda j: (0, j))
    return pl.pallas_call(
        functools.partial(unit_kernel, len(pieces)),
        grid=(units // tile,),
        in_specs=[whole_spec(p.shape) for p in pieces] + [weight, weight],
        out_specs=[whole_spec((rows, depth)), result, result, result],
        out_shape=[jax.ShapeDtypeStruct((rows, depth), BF)]
        + [jax.ShapeDtypeStruct((rows, units), BF)] * 3,
        compiler_params=params(),
        cost_estimate=cost(4 * rows * depth * units, 4 * depth * (rows + units), rows * units),
    )(*pieces, gates, ups)


def unit_grad_kernel(upstream, downs, gate_in, up_in, d_gate, d_up):
    d_hidden = mm(upstream[...], downs[...], NT)
    gate, up = gate_in[...].astype(F32), up_in[...].astype(F32)
    sigma = jax.nn.sigmoid(gate)
    silu = gate * sigma
    d_gate[...] = (d_hidden * up * (sigma + silu * (1.0 - sigma))).astype(BF)
    d_up[...] = (d_hidden * silu).astype(BF)


def unit_grads(upstream, first, rows, downs, gate, up):
    units, depth = downs.shape
    tile = min(units, 256)
    result = pl.BlockSpec((rows, tile), lambda j: (0, j))
    return pl.pallas_call(
        unit_grad_kernel,
        grid=(units // tile,),
        in_specs=[
            pl.BlockSpec((pl.Element(rows), pl.Element(depth)), lambda j: (first, 0)),
            pl.BlockSpec((tile, depth), lambda j: (j, 0)),
            result,
            result,
        ],
        out_specs=[result, result],
        out_shape=[jax.ShapeDtypeStruct((rows, units), BF)] * 2,
        compiler_params=params(),
        cost_estimate=cost(2 * rows * depth * units, 4 * depth * (rows + units), rows * units),
    )(upstream, downs, gate, up)


def head_kernel(count, *refs):
    pieces, (weight, joined, result) = refs[:count], refs[count:]
    join_rows(pieces, joined)
    result[...] = mm(weight[...], joined[...], NT).astype(BF)


def head_product(pieces, weight):
    depth = weight.shape[1]
    rows = sum(p.shape[0] for p in pieces)
    return pl.pallas_call(
        functools.partial(head_kernel, len(pieces)),
        out_shape=[
            jax.ShapeDtypeStruct((rows, depth), BF),
            jax.ShapeDtypeStruct((weight.shape[0], rows), BF),
        ],
        compiler_params=params(),
        cost_estimate=cost(2 * rows * depth * weight.shape[0], 4 * rows * depth),
    )(*pieces, weight)


def grad_kernel(parts, form, starts, *refs):
    rights = refs[parts:-1]
    total = None
    for p in range(parts):
        left = refs[p][...]
        if starts:
            count = left.shape[0]
            right = rights[0][starts[p] : starts[p] + count, :]
        else:
            right = rights[p][...]
        term = mm(left, right, form)
        total = term if total is None else total + term
    refs[-1][...] = total.astype(BF)


def grad_product(lefts, rights, form=TN, starts=()):
    rows = lefts[0].shape[1 if form == TN else 0]
    width = rights[0].shape[1]
    tile = 512
    tokens = sum(r.shape[0] for r in rights)
    return pl.pallas_call(
        functools.partial(grad_kernel, len(lefts), form, starts),
        grid=(width // tile,),
        in_specs=[whole_spec(a.shape) for a in lefts]
        + [pl.BlockSpec((b.shape[0], tile), lambda j: (0, j)) for b in rights],
        out_specs=pl.BlockSpec((rows, tile), lambda j: (0, j)),
        out_shape=jax.ShapeDtypeStruct((rows, width), BF),
        compiler_params=params(),
        cost_estimate=cost(2 * rows * width * tokens, 2 * tokens * (rows + width)),
    )(*lefts, *rights)


def join_kernel(d_qkv, low, weight, grad, share):
    total = mm(d_qkv[...], low[...])
    grad[...] = total.astype(BF)
    sums = jnp.sum(total * weight[...].astype(F32), 0, keepdims=True)
    share[...] = jnp.broadcast_to(sums, share.shape)


def join_product(d_qkv, low, weight):
    rows, width = weight.shape
    tile = 512
    return pl.pallas_call(
        join_kernel,
        grid=(width // tile,),
        in_specs=[
            whole_spec(d_qkv.shape),
            pl.BlockSpec((low.shape[0], tile), lambda j: (0, j)),
            pl.BlockSpec((rows, tile), lambda j: (0, j)),
        ],
        out_specs=[
            pl.BlockSpec((rows, tile), lambda j: (0, j)),
            pl.BlockSpec((8, tile), lambda j: (0, j)),
        ],
        out_shape=[jax.ShapeDtypeStruct((rows, width), BF), jax.ShapeDtypeStruct((8, width), F32)],
        compiler_params=params(),
        cost_estimate=cost(2 * rows * width * low.shape[0], 2 * low.shape[0] * (rows + width)),
    )(d_qkv, low, weight)


def last_kernel(places, d_qkv, weight, keep, send, whole):
    row, rank = places[1], places[2]
    sub = BLK // 8
    width = keep.shape[2]
    whole[...] = mm(d_qkv[...], weight[...], TN).astype(BF)
    for k in range(8):
        at = pl.ds(pl.multiple_of((rank ^ k) * sub, sub), sub)
        for j in range(4):
            target = send if j % 2 else keep
            source = pl.ds(pl.multiple_of((row ^ j) * width, width), width)
            target[j // 2, at, :] = whole[k * sub : (k + 1) * sub, source]


def last_product(places, d_qkv, weight):
    depth = weight.shape[1]
    per = BLOCKS // 2

    def out_map(i, places):
        return ((i // per) ^ places[0], i % per, 0)

    return pl.pallas_call(
        last_kernel,
        grid_spec=pltpu.PrefetchScalarGridSpec(
            num_scalar_prefetch=1,
            grid=(BLOCKS,),
            in_specs=[
                pl.BlockSpec((d_qkv.shape[0], BLK), lambda i, places: (0, i)),
                pl.BlockSpec(weight.shape, lambda i, places: (0, 0)),
            ],
            out_specs=[pl.BlockSpec((2, BLK, depth // 4), out_map)] * 2,
            scratch_shapes=[pltpu.VMEM((BLK, depth), BF)],
        ),
        out_shape=[jax.ShapeDtypeStruct((4, GTOK // 2, depth // 4), BF)] * 2,
        compiler_params=params(),
        cost_estimate=cost(2 * GTOK * depth * d_qkv.shape[0], 2 * GTOK * depth),
    )(places, d_qkv, weight)


def columns_of(values, count, width):
    return jnp.stack([values[..., k * width : (k + 1) * width] for k in range(count)])


def local(
    quick,
    hidden_in,
    gain_before,
    query_weight,
    key_weight,
    value_weight,
    output_weight,
    gain_middle,
    gate_weight,
    up_weight,
    down_weight,
    cotangent,
    branch_points,
    lengths,
):
    width = hidden_in.shape[1]
    depth = 4 * width
    head_width = query_weight.shape[1]
    heads = head_width // HD
    units = gate_weight.shape[1]
    local_tokens = hidden_in.shape[0]
    team = 4 * lax.axis_size("y")
    sub = BLK // team
    x, c = lax.axis_index("x"), lax.axis_index("c")
    z, y = lax.axis_index("z"), lax.axis_index("y")
    row = 2 * x + c
    rank = 4 * y + row
    order = rank if quick else jnp.int32(0)
    branch_row = pick(branch_points, z)
    length_row = pick(lengths, z)
    info = jnp.concatenate([branch_row, length_row, jnp.stack([order * sub])]).astype(jnp.int32)
    places = jnp.stack([y, row, rank]).astype(jnp.int32)

    def full_gather(share):
        blocks = share.shape[0] // sub
        got = lax.all_gather(share.reshape(blocks, sub, depth), TEAM, axis=1, tiled=False)
        return [got.reshape(-1, depth)]

    def full_scatter(partial):
        parts = partial.reshape(-1, team, sub, depth)
        parts = lax.psum_scatter(parts, TEAM, scatter_dimension=1, tiled=False)
        return parts.reshape(-1, depth).astype(F32)

    lines = Lines()
    tick = lines.tick

    def unit_rows(weight):
        pieces = yield from spread_steps(weight.reshape(4, units // 4, width))
        pieces = jnp.concatenate([pieces[k] for k in range(4)], 1)
        if quick:
            lines.extra.append(pieces)
        return [lax.all_gather(pieces, "z", axis=0, tiled=True), pieces]

    joined = jnp.stack([query_weight.T, key_weight.T, value_weight.T, output_weight])
    if heads % 4 == 0:
        per = heads // 4
        pieces = joined.reshape(4, 4, per * HD, width).transpose(1, 0, 2, 3)
        if quick:
            from_y = flip(hidden_in, "y")
            lines.start("heads", spread_steps(pieces))
            tick(None, "heads")
            lines.start("gate", unit_rows(after(gate_weight, lines.wanted["heads"][1][0][0]).T))
            tick(None, "heads")
            tick(None, "gate")
            from_x = flip(after(hidden_in, lines.wanted["gate"][1][0][0]), "x")
            tick(None, "gate")
            pieces = lines.results["heads"]
        else:
            pieces = spread(pieces)
        pieces = jnp.concatenate([pieces[k] for k in range(4)], -1)
        pieces = pieces.reshape(4, per, HD, depth).transpose(1, 0, 2, 3).reshape(per, 4 * HD, depth)
        attend_weights = lax.all_gather(pieces, "z", axis=0, tiled=True)
    else:
        pieces = lax.all_gather(joined, "z", axis=0, tiled=False)
        pieces = spread(pieces).reshape(4, 4, heads, HD, width).transpose(2, 1, 3, 0, 4)
        attend_weights = pieces.reshape(heads, 4 * HD, depth)
    join_weight = attend_weights[:, :ROWS].reshape(heads * ROWS, depth)
    out_weight = attend_weights[:, ROWS:].reshape(heads * HD, depth)

    gains = row_gather(after(jnp.stack([gain_before, gain_middle]), pieces))
    gains = gains.transpose(1, 0, 2).reshape(2, depth)
    gain_one, gain_two = gains[0], gains[1]

    ids = jnp.arange(GTOK, dtype=jnp.int32)
    slot_ids = (ids % BLK) ^ (order * sub)
    starts = jnp.concatenate([jnp.arange(PBLKS, dtype=jnp.int32) * BLK, branch_row])
    positions = jnp.repeat(starts, BLK) + slot_ids
    frequency = THETA ** (-2.0 * jnp.arange(HD // 2, dtype=F32) / HD)
    angles = positions.astype(F32)[None, :] * frequency[:, None]
    cosine, sine = jnp.cos(angles), jnp.sin(angles)

    steps = range(len(CHUNKS))
    ordered = sorted(steps, key=lambda k: CHUNKS[k][0])
    rows_of = [count * BLK for _, count in CHUNKS]
    shares = [slice(first * sub, (first + count) * sub) for first, count in CHUNKS]
    starts = tuple(first * BLK for first, _ in CHUNKS)
    conts = [k for k in ordered if CHUNKS[k][0] >= PBLKS]
    prompts = [k for k in ordered if CHUNKS[k][0] < PBLKS]
    attentions, middles, scales, norms, d_middles, notes = ({} for _ in range(6))
    attended, d_heads = {}, {}

    def to_middle(k, attention):
        middle = residual[shares[k]].astype(F32) + attention
        scale_two = lax.rsqrt(jnp.mean(middle * middle, -1, keepdims=True) + EPSILON)
        norm_two = middle * scale_two
        attentions[k], middles[k], scales[k], norms[k] = attention, middle, scale_two, norm_two
        return (norm_two * gain_two).astype(BF)

    def to_d_middle(k, d_two):
        notes[k] = jnp.sum(d_two * norms[k], 0)
        scaled_two = d_two * gain_two
        inner_two = jnp.mean(scaled_two * norms[k], -1, keepdims=True)
        d_middle = upstream[shares[k]].astype(F32) + scales[k] * (scaled_two - norms[k] * inner_two)
        d_middles[k] = d_middle
        return d_middle.astype(BF)

    def backward(parts, ties, before=None):
        d_out = jnp.concatenate([d_heads[k] for k in parts], 1)
        heads_out = jnp.concatenate([heads_parts[k] for k in ordered], 1)
        lse = jnp.concatenate([lse_parts[k] for k in ordered], 1)
        source = after(qkv, *ties) if ties else qkv
        operands = (source, keys, values, d_out, heads_out, lse, cosine, sine)
        return attend_backward(info, operands, heads, before)

    def total(grad):
        return lax.psum_scatter(grad, "z", scatter_dimension=0, tiled=True)

    def home_steps(part):
        part = yield from spread_steps(columns_of(part, 4, width))
        return part.reshape(-1, width)

    def squares_one():
        wide = hidden_in.astype(F32)
        return jnp.sum(wide * wide, -1)

    def outcome(layer_out, share):
        here = jnp.arange(BLOCKS, dtype=jnp.int32)
        bound = jnp.where(here < PBLKS, BLK, jnp.take(length_row, jnp.maximum(here - PBLKS, 0)))
        slots = rank * sub + jnp.arange(sub, dtype=jnp.int32)
        valid = (slots[None, :] < bound[:, None]).astype(F32).reshape(-1)

        def square_sum(part, weights):
            return jnp.sum(weights * jnp.sum(part * part, -1))

        squares = jnp.stack(
            [square_sum(layer_out.astype(F32), valid)]
            + [
                sum(square_sum(parts[k], valid[shares[k]]) for k in steps)
                for parts in (attentions, d_middles)
            ]
        )
        before_local = share / gain_one
        middle_local = sum(notes[k] for k in steps)
        return jnp.concatenate([before_local, middle_local, squares])

    heads_parts, lse_parts, lows, gates, ups, hiddens = ([] for _ in range(6))
    gate_parts, up_parts = [], []
    if quick:
        former, latter = flip(halves(from_y)[0], "x"), flip(halves(from_x)[1], "y")
        corner = jnp.concatenate([former, latter], 0)
        four = [hidden_in, from_x, from_y, corner]
        hidden_pieces = [p for piece in four for p in (piece, flip(piece, "c"))]
        lines.start("up", unit_rows(up_weight.T))
        lines.start("down", unit_rows(down_weight))
        lines.start("late", place_steps(after(cotangent, corner)))
        lines.launch("late")
        low_one, residual, qkv, keys, values = tick(
            lambda ties: assemble(
                places,
                after(hidden_pieces, *ties),
                gain_one,
                sub,
                (join_weight, cosine, sine),
                heads,
            ),
            "up",
        )

        def forward_line(k, partial):
            low = to_middle(k, (yield from sum_steps(*partial)))
            return (yield from gather_steps(low))

        def attend(k, *names):
            def large(ties):
                return attend_forward(info, after(qkv, *ties), keys, heads, *CHUNKS[k])

            head_part, lse = tick(large, *names)
            heads_parts.append(head_part)
            lse_parts.append(lse)
            partial = split_product([(head_part, out_weight)], TN)
            lines.last = [partial[0]]
            lines.start(k, forward_line(k, partial))

        attend(0, "up")
        lines.land("late")
        attend(1, 0, "late")
        attend(2, 0, 1, "down", "late")
        attend(3, 0, 1, 2)
        gate_rows, up_rows = lines.results["gate"][0], lines.results["up"][0]
        upstream_rows, upstream = tick(
            lambda ties: assemble(places, after(lines.results["late"], *ties), None, sub), 0, 1, 3
        )

        def unit(k, *names):
            def large(ties):
                return unit_products(after(lines.results[k], *ties), gate_rows, up_rows)

            low, gate, up, hidden = tick(large, *names)
            lows.append(low)
            gates.append(gate)
            ups.append(up)
            hiddens.append(hidden)

        def gathered(k):
            lines.last = [lines.wanted[k][1][0][0]]
            tick(None, k)

        tick(None, 0, "down")
        down_rows = lines.results["down"][0]
        gathered(0)
        unit(0, 1, 2)
        tick(None, 1, 2)
        gathered(1)
        unit(1, 2, 3)
        tick(None, 2, 3)
        gathered(2)
        lines.extra.append(down_rows)
        unit(2, 3)
        tick(None, 3)
        gathered(3)
        unit(3)
        down_grad = tick(lambda ties: grad_product(hiddens, [after(upstream_rows, *ties)], TN, starts))
        down_sum = total(down_grad)

        def backward_line(k, partial):
            low = to_d_middle(k, (yield from sum_steps(*partial)))
            pieces = yield from gather_steps(low)
            attended[k], d_heads[k] = head_product(pieces, out_weight)
            return d_heads[k]

        def unit_grad(k, first, second):
            def large(ties):
                source = after(gates[k], *ties)
                return unit_grads(upstream_rows, starts[k], rows_of[k], down_rows, source, ups[k])

            d_gate, d_up = tick(large, *first)
            gate_parts.append(d_gate)
            up_parts.append(d_up)

            def more(ties):
                return split_product([(after(d_gate, *ties), gate_rows), (d_up, up_rows)], NN)

            lines.start(k, backward_line(k, tick(more, *second)))

        unit_grad(0, (), ())
        unit_grad(1, (0,), (0,))
        unit_grad(2, (0, 1), (0, 1))
        unit_grad(3, (0, 1, 2), (0, 1, 2))
        def summed(values, axes):
            for axis in axes:
                (got,) = yield [(values, axis)]
                values = values + got
            return values

        gate_grad = tick(lambda ties: grad_product(after(gate_parts, *ties), lows), 1, 2, 3)
        gate_sum = total(gate_grad)
        mixed = tick(
            lambda ties: mix_product(after([hiddens[k] for k in ordered], *ties), down_rows),
            1,
            2,
            3,
        )
        lines.start("mixed", sum_steps(*mixed))
        before = tick(lambda ties: backward(conts, ties), 2, 3, "mixed")
        lines.start("scale", summed(squares_one(), ("x", "c")))
        up_grad = tick(lambda ties: grad_product(after(up_parts, *ties), lows), 2, 3, "scale")
        up_sum = total(up_grad)
        tick(None, 3, "scale")
        tick(None, 3)
        lines.start("down", home_steps(down_sum))
        lines.start("gate", home_steps(gate_sum))
        d_qkv, inner = tick(lambda ties: backward(prompts, ties, before), "mixed", "down", "gate")
        inner = straighten(inner[0].reshape(BLOCKS, team, sub), rank).reshape(GTOK)
        lines.start("inner", summed(inner, ("x", "c", "y")))
        lines.start("up", home_steps(up_sum))
        own, other = tick(
            lambda ties: last_product(places, after(d_qkv, *ties), join_weight),
            "mixed",
            "down",
            "gate",
            "inner",
        )
        lines.start("last", sum_steps(own, other))
        mixed = lines.results["mixed"]
        layer_out = (jnp.concatenate([middles[k] for k in ordered], 0) + mixed).astype(BF)
        rows = local_tokens // team
        layer_pieces = jnp.stack(
            [
                layer_out[h * rows : (h + 1) * rows, k * width : (k + 1) * width]
                for h in range(2)
                for k in range(4)
            ]
        )
        lines.extra.append(layer_pieces)
        layer_pieces = lax.all_to_all(layer_pieces, TEAM, 0, 0, tiled=True)
        join_grad, share = tick(
            lambda ties: join_product(after(d_qkv, *ties), low_one, join_weight),
            "last",
            "up",
            "inner",
        )
        join_sum = total(join_grad)
        out_grad = tick(
            lambda ties: grad_product(
                after([heads_parts[k] for k in ordered], *ties), [attended[k] for k in ordered], NN
            ),
            "last",
            "inner",
            "up",
        )
        turned = lines.wanted["last"][1][0][0]
        sums = outcome(after(layer_out, out_grad), share[0])
        lines.start("sums", summed(sums, ("c", "z1", "z2", "x", "y")))
        for _ in range(3):
            tick(None, "sums")
        tick(None, "last")
        lines.last = [lines.results["last"]]
        for _ in range(2):
            tick(None, "sums")
        d_one, inner, sums = (lines.results[n] for n in ("last", "inner", "sums"))
        join_sum, out_sum = after((join_sum, total(out_grad)), d_one)
        lines.results["up"] = after(lines.results["up"], turned)
        lines.results["gate"], lines.results["down"], attended, layer_pieces, inner = after(
            (lines.results["gate"], lines.results["down"], attended, layer_pieces, inner), out_grad
        )
        gate_grad, up_grad, down_grad = (lines.results[n] for n in ("gate", "up", "down"))
    else:

        def full(values):
            values = lax.all_gather(values, "y", axis=0, tiled=True)
            return lax.all_gather(values, ROW, axis=1, tiled=True)

        def share_of(values):
            return pick(values.reshape(BLOCKS, team, sub, depth), rank, 1).reshape(-1, depth)

        gate_rows = complete(unit_rows(gate_weight.T))[0]
        up_rows = complete(unit_rows(up_weight.T))[0]
        down_rows = complete(unit_rows(down_weight))[0]
        hidden_rows = full(hidden_in)
        upstream_rows = full(cotangent)
        residual, upstream = share_of(hidden_rows), share_of(upstream_rows)
        wide = hidden_rows.astype(F32)
        scale = lax.rsqrt(jnp.mean(wide * wide, -1, keepdims=True) + EPSILON)
        low_one = (wide * scale * gain_one).astype(BF)
        qkv, keys, values = project(join_weight, low_one, cosine, sine, heads)
        for k in steps:
            head_part, lse = attend_forward(info, qkv, keys, heads, *CHUNKS[k])
            heads_parts.append(head_part)
            lse_parts.append(lse)
            low = to_middle(k, full_scatter(mm(head_part, out_weight, TN).astype(BF)))
            low, gate, up, hidden = unit_products(full_gather(low), gate_rows, up_rows)
            lows.append(low)
            hiddens.append(hidden)
            d_gate, d_up = unit_grads(upstream_rows, starts[k], rows_of[k], down_rows, gate, up)
            gate_parts.append(d_gate)
            up_parts.append(d_up)
            partial = (mm(d_gate, gate_rows) + mm(d_up, up_rows)).astype(BF)
            low = to_d_middle(k, full_scatter(partial))
            attended[k], d_heads[k] = head_product(full_gather(low), out_weight)
        gate_sum, up_sum = total(grad_product(gate_parts, lows)), total(grad_product(up_parts, lows))
        down_sum = total(grad_product(hiddens, [upstream_rows], TN, starts))
        mixed = full_scatter(
            jnp.concatenate([mm(hiddens[k], down_rows).astype(BF) for k in ordered], 0)
        )
        d_qkv, inner = backward(prompts, [], backward(conts, []))
        partial = mm(d_qkv, join_weight, TN).astype(BF)
        join_grad, share = join_product(d_qkv, low_one, join_weight)
        out_grad = grad_product([heads_parts[k] for k in ordered], [attended[k] for k in ordered], NN)
        layer_out = (jnp.concatenate([middles[k] for k in ordered], 0) + mixed).astype(BF)
        sums = lax.psum(outcome(layer_out, share[0]), EVERY)
        gate_grad, up_grad, down_grad = (
            complete(home_steps(part)) for part in (gate_sum, up_sum, down_sum)
        )

    attended = [attended[k] for k in ordered]
    gate_grad, up_grad = gate_grad.T.astype(F32), up_grad.T.astype(F32)
    down_grad = down_grad.astype(F32)
    if heads % 4 == 0:
        part = join_sum if quick else total(join_grad)
        part = part.reshape(heads // 4, 3, HD, depth).transpose(1, 0, 2, 3)
        part = spread(columns_of(part.reshape(3, heads // 4 * HD, depth), 4, width))
        part = part.transpose(1, 0, 2, 3).reshape(3, head_width, width)
        out_part = spread(columns_of(out_sum if quick else total(out_grad), 4, width)).reshape(1, head_width, width)
        part = jnp.concatenate([part, out_part], 0)
    else:
        part = jnp.concatenate(
            [join_grad.reshape(heads, 3, HD, depth), out_grad.reshape(heads, 1, HD, depth)], 1
        ).transpose(1, 0, 2, 3)
        part = spread(columns_of(part.reshape(4, heads * HD, depth), 4, width))
        part = lax.psum_scatter(part, "z", scatter_dimension=0, tiled=False)
    query_grad, key_grad, value_grad = (part[k].T.astype(F32) for k in range(3))
    output_grad = part[3].astype(F32)

    if quick:
        half = local_tokens
        inner = pick(inner.reshape(2, half), y)
        d_middle = jnp.concatenate(
            [lax.dynamic_slice_in_dim(a, row * width, width, 1) for a in attended], 0
        )
        d_middle = pick(d_middle.reshape(2, BLOCKS // 2, team, sub, width), y)
        d_middle = straighten(d_middle, rank).reshape(half, width).astype(F32)
        layer_out = layer_pieces.reshape(team, BLOCKS // 2, sub, width).transpose(1, 0, 2, 3)
        layer_out = layer_out.reshape(half, width)
    else:
        d_one = lax.psum_scatter(partial, "y", scatter_dimension=0, tiled=True)
        d_one = lax.psum_scatter(d_one, ROW, scatter_dimension=1, tiled=True).astype(F32)
        inner = lax.psum(inner[0], TEAM)
        inner = lax.dynamic_slice(inner, (y * local_tokens,), (local_tokens,))
        corner = (y * local_tokens, row * width)
        d_middle = lax.dynamic_slice(
            jnp.concatenate(attended, 0), corner, (local_tokens, width)
        ).astype(F32)
        layer_out = lax.all_gather(
            layer_out.reshape(BLOCKS, sub, depth), TEAM, axis=1, tiled=False
        ).reshape(GTOK, depth)
        layer_out = lax.dynamic_slice(layer_out, corner, (local_tokens, width))
    wide = hidden_in.astype(F32)
    row_squares = lines.results["scale"] if quick else row_sum(squares_one())
    scale_one = lax.rsqrt(row_squares / depth + EPSILON)[:, None]
    norm_one = wide * scale_one
    input_grad = d_middle + scale_one * (d_one * gain_before - norm_one * (inner / depth)[:, None])

    before_grad = lax.dynamic_slice(sums, (row * width,), (width,))
    middle_grad = lax.dynamic_slice(sums, (depth + row * width,), (width,))
    valid_count = (lengths.shape[0] * PROMPT + jnp.sum(lengths)).astype(F32)
    rms_values = jnp.sqrt(sums[2 * depth :] / (valid_count * depth))
    return (
        layer_out,
        input_grad,
        before_grad,
        query_grad,
        key_grad,
        value_grad,
        output_grad,
        middle_grad,
        gate_grad,
        up_grad,
        down_grad,
        rms_values,
    )


def solution(mesh):
    split = mesh.shape["col"] // GROUPS
    grid = Mesh(mesh.devices.reshape(2, 2, GROUPS, split), ("x", "c", "z", "y"))
    row, col = ("x", "c"), ("z", "y")
    return jax.shard_map(
        functools.partial(local, split == 2),
        mesh=grid,
        in_specs=(
            P(col, row),
            P(row),
            P(row, col),
            P(row, col),
            P(row, col),
            P(col, row),
            P(row),
            P(row, col),
            P(row, col),
            P(col, row),
            P(col, row),
            P(),
            P(),
        ),
        out_specs=(
            P(col, row),
            P(col, row),
            P(row),
            P(row, col),
            P(row, col),
            P(row, col),
            P(col, row),
            P(row),
            P(row, col),
            P(row, col),
            P(col, row),
            P(),
        ),
        check_vma=False,
    )
```

```python
import functools
import jax
import jax.numpy as jnp
from jax import lax
from jax.experimental import pallas as pl
from jax.experimental.pallas import tpu as pltpu
from jax.sharding import Mesh
from jax.sharding import PartitionSpec as P

HD = 64
PROMPT = 2048
CLEN = 256
CONTS = 6
GTOK = 3584
BLK = 256
PBLKS = PROMPT // BLK
BLOCKS = GTOK // BLK
ROWS = 3 * HD
BF = jnp.bfloat16
F32 = jnp.float32
LOW = -1e30
LOG2E = 1.4426950408889634
FACTOR = HD ** (-0.5) * LOG2E
VMEM_LIMIT = 56 * 1024 * 1024

NN = (((1,), (0,)), ((), ()))
NT = (((1,), (1,)), ((), ()))
TN = (((0,), (0,)), ((), ()))


def mm(a, b, dims=NN):
    return lax.dot_general(a, b, dims, preferred_element_type=F32)


def block_plan(info, block):
    cont = jnp.maximum(block - PBLKS, 0)
    is_cont = block >= PBLKS
    reach = info[cont]
    full = jnp.where(is_cont, reach // BLK, block)
    rest = jnp.where(is_cont, reach - full * BLK, 0)
    limit = jnp.where(is_cont, info[CONTS + cont], BLK)
    masked = 1 + (rest > 0).astype(jnp.int32)
    return full, rest, limit, masked


def local_ids(info, shape, axis):
    return lax.broadcasted_iota(jnp.int32, shape, axis) ^ info[2 * CONTS]


def masked_step(info, block, full, rest, limit, index):
    own = index == 0
    target = jnp.where(own, block, full)
    query_ids = local_ids(info, (1, BLK), 1)
    bound = jnp.where(own, jnp.minimum(query_ids + 1, limit), rest)
    key_ids = local_ids(info, (BLK, BLK), 0)
    return target, key_ids < bound


def columns(block):
    return pl.ds(pl.multiple_of(block * BLK, BLK), BLK)


def forward_kernel(heads, first, info, qkv, knat, out, lse, acc, top, tot):
    block = pl.program_id(0) + first
    full, rest, limit, masked = block_plan(info, block)
    here = columns(block)
    acc[...] = jnp.zeros_like(acc)
    top[...] = jnp.full_like(top, LOW)
    tot[...] = jnp.zeros_like(tot)

    def step(target, allowed, wide=1):
        span = pl.ds(pl.multiple_of(target * BLK, BLK), wide * BLK)
        weights, shrinks = [], []
        scores = [
            mm(knat[h, span, :], qkv[h * ROWS : h * ROWS + HD, here]) for h in range(heads)
        ]
        for h in range(heads):
            score = scores[h] * FACTOR
            if allowed is not None:
                score = jnp.where(allowed, score, LOW)
            old = top[h : h + 1, :]
            new = jnp.maximum(old, jnp.max(score, 0, keepdims=True))
            weight = jnp.exp2(score - new)
            shrink = jnp.exp2(old - new)
            top[h : h + 1, :] = new
            tot[h : h + 1, :] = tot[h : h + 1, :] * shrink + jnp.sum(weight, 0, keepdims=True)
            weights.append(weight.astype(BF))
            shrinks.append(shrink)
        for h in range(heads):
            value = qkv[h * ROWS + 2 * HD : (h + 1) * ROWS, span]
            acc[h] = acc[h] * shrinks[h] + mm(value, weights[h])

    def full_step(index, carry):
        step(index, None)
        return carry

    def mask_step(index, carry):
        target, allowed = masked_step(info, block, full, rest, limit, index)
        step(target, allowed)
        return carry

    def wide_step(index, carry):
        step(index * 4, None, 4)
        return carry

    lax.fori_loop(0, full // 4, wide_step, 0)

    @pl.when(full % 4 >= 2)
    def _():
        step(full // 4 * 4, None, 2)

    lax.fori_loop(full // 2 * 2, full, full_step, 0)
    lax.fori_loop(0, masked, mask_step, 0)
    for h in range(heads):
        total = tot[h : h + 1, :]
        out[h * HD : (h + 1) * HD, :] = (acc[h] / total).astype(BF)
        lse[h : h + 1, :] = top[h : h + 1, :] + jnp.log2(total)


def attend_forward(info, qkv, knat, heads, first, count):
    pad = max(8, heads)
    return pl.pallas_call(
        functools.partial(forward_kernel, heads, first),
        grid=(count,),
        in_specs=[
            pl.BlockSpec(memory_space=pltpu.SMEM),
            pl.BlockSpec(qkv.shape, lambda i: (0, 0)),
            pl.BlockSpec(knat.shape, lambda i: (0, 0, 0)),
        ],
        out_specs=[
            pl.BlockSpec((heads * HD, BLK), lambda i: (0, i)),
            pl.BlockSpec((pad, BLK), lambda i: (0, i)),
        ],
        out_shape=[
            jax.ShapeDtypeStruct((heads * HD, count * BLK), BF),
            jax.ShapeDtypeStruct((pad, count * BLK), F32),
        ],
        scratch_shapes=[
            pltpu.VMEM((heads, HD, BLK), F32),
            pltpu.VMEM((pad, BLK), F32),
            pltpu.VMEM((pad, BLK), F32),
        ],
        compiler_params=pltpu.CompilerParams(vmem_limit_bytes=VMEM_LIMIT),
        cost_estimate=pl.CostEstimate(
            flops=heads * count * 6 * BLK * BLK * 2560,
            bytes_accessed=16 << 20,
            transcendentals=heads * count * 6 * BLK * BLK,
        ),
    )(info, qkv, knat)


def turn(values, cosine, sine, at):
    half = HD // 2
    cos, sin = cosine[:, at], sine[:, at]
    former, latter = values[:half], values[half:]
    return former * cos + latter * sin, latter * cos - former * sin


def backward_kernel(heads, first, final, info, qkv, knat, vnat, d_out, heads_out, lse, cosine, sine, *refs):
    if final:
        d_old_keys, d_old_values, d_old_query, old_inner, d_qkv, inner, d_keys, d_values, d_query = refs
    else:
        d_keys, d_values, d_turned, share_out, d_query = refs
    block = pl.program_id(0) + first
    full, rest, limit, masked = block_plan(info, block)
    here = columns(block)
    there = columns(pl.program_id(0))

    @pl.when(pl.program_id(0) == 0)
    def _():
        if final:
            d_keys[...] = d_old_keys[...]
            d_values[...] = d_old_values[...]
            inner[...] = jnp.zeros_like(inner)
        else:
            d_keys[...] = jnp.zeros_like(d_keys)
            d_values[...] = jnp.zeros_like(d_values)

    d_query[...] = jnp.zeros_like(d_query)
    deltas = []
    for h in range(heads):
        rows = slice(h * HD, (h + 1) * HD)
        deltas.append(
            jnp.sum(d_out[rows, there].astype(F32) * heads_out[rows, here].astype(F32), 0, keepdims=True)
        )

    def step(target, allowed, wide=1):
        span = pl.ds(pl.multiple_of(target * BLK, BLK), wide * BLK)
        for first in range(0, heads, 4):
            team = range(first, min(first + 4, heads))
            scores = [
                mm(knat[h, span, :], qkv[h * ROWS : h * ROWS + HD, here]) for h in team
            ]
            d_probs = [
                mm(vnat[h, span, :], d_out[h * HD : (h + 1) * HD, there]) for h in team
            ]
            low_probs, d_scores = [], []
            for h, score, d_prob in zip(team, scores, d_probs):
                score = score * FACTOR - lse[h : h + 1, here]
                if allowed is not None:
                    score = jnp.where(allowed, score, LOW)
                probs = jnp.exp2(score)
                low_probs.append(probs.astype(BF))
                d_scores.append((probs * (d_prob - deltas[h])).astype(BF))
            for h, low, d_score in zip(team, low_probs, d_scores):
                rows = slice(h * HD, (h + 1) * HD)
                query = qkv[h * ROWS : h * ROWS + HD, here]
                key = qkv[h * ROWS + HD : h * ROWS + 2 * HD, span]
                d_query[h] += mm(key, d_score)
                d_keys[rows, span] += mm(query, d_score, NT)
                d_values[rows, span] += mm(d_out[rows, there], low, NT)

    def full_step(index, carry):
        step(index, None)
        return carry

    def mask_step(index, carry):
        target, allowed = masked_step(info, block, full, rest, limit, index)
        step(target, allowed)
        return carry

    def wide_step(index, carry):
        step(index * 2, None, 2)
        return carry

    lax.fori_loop(0, full // 2, wide_step, 0)
    lax.fori_loop(full // 2 * 2, full, full_step, 0)
    lax.fori_loop(0, masked, mask_step, 0)

    half = HD // 2
    share = jnp.zeros((1, BLK), F32)
    for h in range(heads):
        start = h * ROWS
        values = d_query[h] * HD ** (-0.5)
        share += jnp.sum(values * qkv[start : start + HD, here].astype(F32), 0, keepdims=True)
        low, high = turn(values, cosine, sine, here)
        if final:
            d_qkv[start : start + half, here] = low.astype(BF)
            d_qkv[start + half : start + HD, here] = high.astype(BF)
        else:
            d_turned[h * HD : h * HD + half, :] = low.astype(BF)
            d_turned[h * HD + half : (h + 1) * HD, :] = high.astype(BF)
    if not final:
        share_out[0:1, :] = share
        return
    inner[0:1, here] = share

    @pl.when(block == PBLKS - 1)
    def _():
        inner[:, PROMPT:] = old_inner[...]
        for h in range(heads):
            d_qkv[h * ROWS : h * ROWS + HD, PROMPT:] = d_old_query[h * HD : (h + 1) * HD, :]

        def finish(index, carry):
            at = columns(index)
            share = inner[0:1, at]
            for h in range(heads):
                start = h * ROWS + HD
                rows = slice(h * HD, (h + 1) * HD)
                values = d_keys[rows, at] * HD ** (-0.5)
                share += jnp.sum(values * qkv[start : start + HD, at].astype(F32), 0, keepdims=True)
                low, high = turn(values, cosine, sine, at)
                d_qkv[start : start + half, at] = low.astype(BF)
                d_qkv[start + half : start + HD, at] = high.astype(BF)
                start += HD
                values = d_values[rows, at]
                share += jnp.sum(values * qkv[start : start + HD, at].astype(F32), 0, keepdims=True)
                d_qkv[start : start + HD, at] = values.astype(BF)
            inner[0:1, at] = share
            return carry

        lax.fori_loop(0, BLOCKS, finish, 0)


def attend_backward(info, operands, heads, before=None):
    whole = lambda a: pl.BlockSpec(a.shape, lambda i, n=len(a.shape): (0,) * n)
    final = before is not None
    operands = tuple(operands) + (tuple(before) if final else ())
    sums = jax.ShapeDtypeStruct((heads * HD, GTOK), F32)
    rest = GTOK - PROMPT
    if final:
        shapes = [jax.ShapeDtypeStruct((heads * ROWS, GTOK), BF), jax.ShapeDtypeStruct((8, GTOK), F32)]
        specs = [whole(a) for a in shapes]
        scratch = [pltpu.VMEM(sums.shape, F32), pltpu.VMEM(sums.shape, F32)]
    else:
        shapes = [sums, sums, jax.ShapeDtypeStruct((heads * HD, rest), BF), jax.ShapeDtypeStruct((8, rest), F32)]
        specs = [whole(sums), whole(sums)]
        specs += [
            pl.BlockSpec((heads * HD, BLK), lambda i: (0, i)),
            pl.BlockSpec((8, BLK), lambda i: (0, i)),
        ]
        scratch = []
    return pl.pallas_call(
        functools.partial(backward_kernel, heads, 0 if final else PBLKS, final),
        grid=(PBLKS if final else CONTS,),
        in_specs=[pl.BlockSpec(memory_space=pltpu.SMEM)] + [whole(a) for a in operands],
        out_specs=specs,
        out_shape=shapes,
        scratch_shapes=scratch + [pltpu.VMEM((heads, HD, BLK), F32)],
        compiler_params=pltpu.CompilerParams(vmem_limit_bytes=VMEM_LIMIT),
        cost_estimate=pl.CostEstimate(
            flops=heads * BLOCKS * 3 * BLK * BLK * 4096,
            bytes_accessed=32 << 20,
            transcendentals=heads * BLOCKS * 3 * BLK * BLK,
        ),
    )(info, *operands)


def project_kernel(heads, weight, low, cosine, sine, qkv, knat, vnat):
    raw = mm(weight[...], low[...], NT)
    half = HD // 2
    cos, sin = cosine[...], sine[...]
    for h in range(heads):
        for part in range(2):
            start = h * ROWS + part * HD
            former, latter = raw[start : start + half], raw[start + half : start + HD]
            turned = jnp.concatenate(
                [former * cos - latter * sin, latter * cos + former * sin], 0
            )
            qkv[start : start + HD, :] = turned.astype(BF)
            if part:
                knat[h] = turned.T.astype(BF)
        start = h * ROWS + 2 * HD
        value = raw[start : start + HD]
        qkv[start : start + HD, :] = value.astype(BF)
        vnat[h] = value.T.astype(BF)


def project(weight, low, cosine, sine, heads):
    depth = weight.shape[1]
    natural = jax.ShapeDtypeStruct((heads, GTOK, HD), BF)
    return pl.pallas_call(
        functools.partial(project_kernel, heads),
        grid=(BLOCKS,),
        in_specs=[
            pl.BlockSpec(weight.shape, lambda i: (0, 0)),
            pl.BlockSpec((BLK, depth), lambda i: (i, 0)),
            pl.BlockSpec((HD // 2, BLK), lambda i: (0, i)),
            pl.BlockSpec((HD // 2, BLK), lambda i: (0, i)),
        ],
        out_specs=[pl.BlockSpec((heads * ROWS, BLK), lambda i: (0, i))]
        + [pl.BlockSpec((heads, BLK, HD), lambda i: (0, i, 0))] * 2,
        out_shape=[jax.ShapeDtypeStruct((heads * ROWS, GTOK), BF), natural, natural],
        compiler_params=pltpu.CompilerParams(vmem_limit_bytes=VMEM_LIMIT),
        cost_estimate=pl.CostEstimate(
            flops=2 * GTOK * depth * heads * ROWS, bytes_accessed=3 * GTOK * depth, transcendentals=0
        ),
    )(weight, low, cosine, sine)


EPSILON = 1e-05
THETA = 130000.0
GROUPS = 4
CHUNKS = ((8, 3), (11, 3), (0, 4), (4, 4))
ROW = ("x", "c")
TEAM = ("y", "x", "c")
EVERY = ("x", "c", "z", "y")


def after(values, *earlier):
    return lax.optimization_barrier((values, earlier))[0]


def flip(values, axis):
    return lax.ppermute(values, axis, [(0, 1), (1, 0)])


def send(values, axis):
    if axis == "z1":
        return lax.ppermute(values, "z", [(0, 1), (1, 0), (2, 3), (3, 2)])
    if axis == "z2":
        return lax.ppermute(values, "z", [(0, 2), (1, 3), (2, 0), (3, 1)])
    return flip(values, axis)


def pick(stack, index, axis=0):
    return lax.dynamic_index_in_dim(stack, index, axis, keepdims=False)


def in_order(mine, other, bit, axis):
    return jnp.where(
        bit == 0, jnp.stack([mine, other], axis), jnp.stack([other, mine], axis)
    )


def spread_steps(pieces):
    x, c = lax.axis_index("x"), lax.axis_index("c")
    pieces = pieces.reshape((2, 2) + pieces.shape[1:])
    (got,) = yield [(pick(pieces, 1 - x), "x")]
    pieces = in_order(pick(pieces, x), got, x, 0)
    (got,) = yield [(pick(pieces, 1 - c, 1), "c")]
    pieces = in_order(pick(pieces, c, 1), got, c, 1)
    return pieces.reshape((4,) + pieces.shape[2:])


def complete(steps):
    try:
        wanted = next(steps)
        while True:
            wanted = steps.send([flip(*w) for w in wanted])
    except StopIteration as end:
        return end.value


def spread(pieces):
    return complete(spread_steps(pieces))


class Lines:
    def __init__(self):
        self.wanted = {}
        self.flying = {}
        self.results = {}
        self.last = []
        self.extra = []

    def start(self, name, steps):
        self.wanted[name] = (steps, next(steps))

    def launch(self, name):
        steps, wanted = self.wanted.pop(name)
        wanted = [(after(v, *self.last) if self.last else v, axis) for v, axis in wanted]
        self.extra += [v for v, _ in wanted]
        self.flying[name] = (steps, [send(v, axis) for v, axis in wanted])

    def land(self, name):
        steps, got = self.flying.pop(name)
        self.proceed(name, steps, after(got, *self.last))

    def proceed(self, name, steps, got):
        try:
            self.wanted[name] = (steps, steps.send(got))
        except StopIteration as end:
            self.results[name] = end.value
            value = end.value[-1] if isinstance(end.value, list) else end.value
            if value is not None:
                self.extra.append(value)
            if name == "mixed":
                self.extra += list(got)

    def tick(self, large, *names):
        if large is None:
            for name in names:
                steps, wanted = self.wanted.pop(name)
                wanted = [(after(v, *self.last) if self.last else v, axis) for v, axis in wanted]
                self.proceed(name, steps, [send(*w) for w in wanted])
            return None
        sent = {}
        for name in names:
            steps, wanted = self.wanted.pop(name)
            sent[name] = (steps, [(after(v, *self.last) if self.last else v, axis) for v, axis in wanted])
        operands = [v for _, part in sent.values() for v, _ in part]
        done = large(self.last + self.extra + operands)
        self.extra = []
        self.last = [done[0] if isinstance(done, (tuple, list)) else done]
        for name, (steps, wanted) in sent.items():
            self.proceed(name, steps, after([send(*w) for w in wanted], *self.last))
        return done


def row_gather(values):
    x, c = lax.axis_index("x"), lax.axis_index("c")
    pair = in_order(values, flip(values, "x"), x, 0)
    four = in_order(pair, flip(pair, "c"), c, 1)
    return four.reshape((4,) + values.shape)


def row_sum(values):
    values = values + flip(values, "x")
    return values + flip(values, "c")


def halves(values):
    middle = values.shape[0] // 2
    return values[:middle], values[middle:]


def place_steps(own):
    from_x, from_y, from_c = yield [(own, "x"), (own, "y"), (own, "c")]
    former, latter, by_x, by_y = yield [
        (halves(from_y)[0], "x"),
        (halves(from_x)[1], "y"),
        (from_x, "c"),
        (from_y, "c"),
    ]
    corner = jnp.concatenate([former, latter], 0)
    (other,) = yield [(corner, "c")]
    return [own, from_c, from_x, by_x, from_y, by_y, corner, other]


def gather_steps(own):
    from_x, from_y = yield [(own, "x"), (own, "y")]
    former, latter = yield [(halves(from_y)[0], "x"), (halves(from_x)[1], "y")]
    four = jnp.concatenate([own, from_x, from_y, former, latter], 0)
    (other,) = yield [(four, "c")]
    return [four, other]


def sum_steps(keep, send):
    shape = (4, 2, keep.shape[1] // 2, keep.shape[2])

    def pair(*values):
        first, second = (v.reshape(shape) for v in values)
        return lambda *at: first[at].astype(F32) + second[at].astype(F32)

    (got,) = yield [(send, "c")]
    part = pair(keep, got)
    to_x = part(slice(1, 4, 2), 0).astype(BF)
    to_y = part(slice(2, 4), 1).astype(BF)
    by_x, by_y = yield [(to_x, "x"), (to_y, "y")]
    keep, got = after((keep, got), by_x, by_y)
    part = pair(keep, got)
    over_y = (part(2, 0) + by_x[1].astype(F32)).astype(BF)
    over_x = (part(1, 1) + by_y[1].astype(F32)).astype(BF)
    last_y, last_x = yield [(over_y, "y"), (over_x, "x")]
    keep, got = after((keep, got), last_y, last_x)
    part = pair(keep, got)
    former = part(0, 0) + by_x[0].astype(F32) + last_y.astype(F32)
    latter = part(0, 1) + by_y[0].astype(F32) + last_x.astype(F32)
    return jnp.concatenate([former, latter], 0)


def norm_kernel(mode, heads, places, *refs):
    own, other, refs = refs[:4], refs[4:8], refs[8:]
    if mode:
        gain, weight, cosine, sine, low, share, qkv, knat, vnat, whole = refs
    else:
        low, share, whole = refs
    half, row, rank = places[0], places[1], places[2]
    mine = pl.program_id(0) // (BLOCKS // 2) == half
    width = own[0].shape[1]

    def place(sources):
        for k, source in enumerate(sources):
            at = pl.multiple_of((row ^ k) * width, width)
            whole[:, pl.ds(at, width)] = source[...]

    @pl.when(mine)
    def _():
        place(own)

    @pl.when(jnp.logical_not(mine))
    def _():
        place(other)

    sub = share.shape[0]
    for k in range(BLK // sub):
        at = pl.multiple_of((rank ^ k) * sub, sub)
        rows = whole[pl.ds(at, sub), :]
        if k == 0:
            share[...] = rows
        if not mode:
            low[k * sub : (k + 1) * sub, :] = rows
        else:
            wide = rows.astype(F32)
            scale = lax.rsqrt(jnp.sum(wide * wide, 1, keepdims=True) / wide.shape[1] + EPSILON)
            low[k * sub : (k + 1) * sub, :] = (wide * scale * gain[...]).astype(BF)
    if mode:
        project_kernel(heads, weight, low, cosine, sine, qkv, knat, vnat)


def assemble(places, pieces, gain, sub, projection=(), heads=0):
    per = BLOCKS // 2
    width = pieces[0].shape[1]
    whole = 4 * width
    mode = gain is not None

    def own_map(i, places):
        return jnp.where(i // per == places[0], i % per, 0), 0

    def other_map(i, places):
        return jnp.where(i // per == places[0], 0, i % per), 0

    operands = list(pieces)
    specs = [pl.BlockSpec((BLK, width), own_map)] * 4 + [pl.BlockSpec((BLK, width), other_map)] * 4
    outs = [pl.BlockSpec((BLK, whole), lambda i, p: (i, 0)), pl.BlockSpec((sub, whole), lambda i, p: (i, 0))]
    shapes = [jax.ShapeDtypeStruct((GTOK, whole), BF), jax.ShapeDtypeStruct((BLOCKS * sub, whole), BF)]
    flops = 0
    if mode:
        table = pl.BlockSpec((HD // 2, BLK), lambda i, p: (0, i))
        specs += [pl.BlockSpec((1, whole), lambda i, p: (0, 0))]
        specs += [pl.BlockSpec(projection[0].shape, lambda i, p: (0, 0)), table, table]
        operands += [gain.reshape(1, whole), *projection]
        outs += [pl.BlockSpec((heads * ROWS, BLK), lambda i, p: (0, i))]
        outs += [pl.BlockSpec((heads, BLK, HD), lambda i, p: (0, i, 0))] * 2
        natural = jax.ShapeDtypeStruct((heads, GTOK, HD), BF)
        shapes += [jax.ShapeDtypeStruct((heads * ROWS, GTOK), BF), natural, natural]
        flops = 2 * GTOK * whole * heads * ROWS
    return pl.pallas_call(
        functools.partial(norm_kernel, mode, heads),
        grid_spec=pltpu.PrefetchScalarGridSpec(
            num_scalar_prefetch=1,
            grid=(BLOCKS,),
            in_specs=specs,
            out_specs=outs,
            scratch_shapes=[pltpu.VMEM((BLK, whole), BF)],
        ),
        out_shape=shapes,
        compiler_params=params(),
        cost_estimate=cost(flops + GTOK * whole * 6, GTOK * whole * 5),
    )(places, *operands)


def straighten(values, rank):
    count = values.shape[1]
    return jnp.stack([pick(values, j ^ rank, 1) for j in range(count)], 1)


def whole_spec(shape):
    return pl.BlockSpec(shape, lambda *i, n=len(shape): (0,) * n)


def cost(flops, bytes_accessed, transcendentals=0):
    return pl.CostEstimate(
        flops=int(flops), bytes_accessed=int(bytes_accessed), transcendentals=int(transcendentals)
    )


def params():
    return pltpu.CompilerParams(vmem_limit_bytes=VMEM_LIMIT)


def split_kernel(pairs, form, sub, *refs):
    keep, send = refs[2 * pairs :]
    total = mm(refs[0][...], refs[1][...], form)
    for p in range(1, pairs):
        total += mm(refs[2 * p][...], refs[2 * p + 1][...], form)
    low = total.astype(BF)
    for b in range(low.shape[0] // BLK):
        for k in range(8):
            target = send if k % 2 else keep
            start = b * BLK + k * sub
            target[k // 2, b * sub : (b + 1) * sub, :] = low[start : start + sub]


def split_product(pairs, form):
    width = pairs[0][1].shape[1]
    rows = pairs[0][0].shape[1 if form == TN else 0]
    depth = pairs[0][1].shape[0]
    tile = 512
    sub = BLK // 8
    specs, operands = [], []
    for left, right in pairs:
        specs += [whole_spec(left.shape), pl.BlockSpec((depth, tile), lambda j: (0, j))]
        operands += [left, right]
    shape = (4, rows // 8, width)
    return pl.pallas_call(
        functools.partial(split_kernel, len(pairs), form, sub),
        grid=(width // tile,),
        in_specs=specs,
        out_specs=[pl.BlockSpec((4, rows // 8, tile), lambda j: (0, 0, j))] * 2,
        out_shape=[jax.ShapeDtypeStruct(shape, BF)] * 2,
        compiler_params=params(),
        cost_estimate=cost(
            2 * rows * depth * width * len(pairs),
            2 * (rows * width + (rows + width) * depth * len(pairs)),
        ),
    )(*operands)


def mix_kernel(parts, sub, *refs):
    weight, keep, send = refs[parts:]
    at = 0
    for left in refs[:parts]:
        low = mm(left[...], weight[...]).astype(BF)
        for b in range(low.shape[0] // BLK):
            for k in range(8):
                target = send if k % 2 else keep
                start = b * BLK + k * sub
                target[k // 2, at : at + sub, :] = low[start : start + sub]
            at += sub


def mix_product(parts, weight):
    width = weight.shape[1]
    rows = sum(a.shape[0] for a in parts)
    tile = 256
    return pl.pallas_call(
        functools.partial(mix_kernel, len(parts), BLK // 8),
        grid=(width // tile,),
        in_specs=[whole_spec(a.shape) for a in parts]
        + [pl.BlockSpec((weight.shape[0], tile), lambda j: (0, j))],
        out_specs=[pl.BlockSpec((4, rows // 8, tile), lambda j: (0, 0, j))] * 2,
        out_shape=[jax.ShapeDtypeStruct((4, rows // 8, width), BF)] * 2,
        compiler_params=params(),
        cost_estimate=cost(2 * rows * weight.size, 2 * (rows * width + rows * weight.shape[0])),
    )(*parts, weight)


def join_rows(pieces, target):
    if len(pieces) == 1:
        target[...] = pieces[0][...]
        return
    blocks = target.shape[0] // BLK
    sub = BLK // 8
    for b in range(blocks):
        for k in range(8):
            start = b * BLK + k * sub
            source = ((k // 2) * blocks + b) * sub
            target[start : start + sub, :] = pieces[k % 2][source : source + sub, :]


def unit_kernel(count, *refs):
    pieces, (gates, ups, low, gate_out, up_out, hidden) = refs[:count], refs[count:]

    @pl.when(pl.program_id(0) == 0)
    def _():
        join_rows(pieces, low)

    rows = low[...]
    gate = mm(rows, gates[...], NT)
    up = mm(rows, ups[...], NT)
    gate_out[...] = gate.astype(BF)
    up_out[...] = up.astype(BF)
    hidden[...] = (gate * jax.nn.sigmoid(gate) * up).astype(BF)


def unit_products(pieces, gates, ups):
    rows = sum(p.shape[0] for p in pieces)
    units, depth = gates.shape
    tile = min(units, 256)
    weight = pl.BlockSpec((tile, depth), lambda j: (j, 0))
    result = pl.BlockSpec((rows, tile), lambda j: (0, j))
    return pl.pallas_call(
        functools.partial(unit_kernel, len(pieces)),
        grid=(units // tile,),
        in_specs=[whole_spec(p.shape) for p in pieces] + [weight, weight],
        out_specs=[whole_spec((rows, depth)), result, result, result],
        out_shape=[jax.ShapeDtypeStruct((rows, depth), BF)]
        + [jax.ShapeDtypeStruct((rows, units), BF)] * 3,
        compiler_params=params(),
        cost_estimate=cost(4 * rows * depth * units, 4 * depth * (rows + units), rows * units),
    )(*pieces, gates, ups)


def unit_grad_kernel(upstream, downs, gate_in, up_in, d_gate, d_up):
    d_hidden = mm(upstream[...], downs[...], NT)
    gate, up = gate_in[...].astype(F32), up_in[...].astype(F32)
    sigma = jax.nn.sigmoid(gate)
    silu = gate * sigma
    d_gate[...] = (d_hidden * up * (sigma + silu * (1.0 - sigma))).astype(BF)
    d_up[...] = (d_hidden * silu).astype(BF)


def unit_grads(upstream, first, rows, downs, gate, up):
    units, depth = downs.shape
    tile = min(units, 256)
    result = pl.BlockSpec((rows, tile), lambda j: (0, j))
    return pl.pallas_call(
        unit_grad_kernel,
        grid=(units // tile,),
        in_specs=[
            pl.BlockSpec((pl.Element(rows), pl.Element(depth)), lambda j: (first, 0)),
            pl.BlockSpec((tile, depth), lambda j: (j, 0)),
            result,
            result,
        ],
        out_specs=[result, result],
        out_shape=[jax.ShapeDtypeStruct((rows, units), BF)] * 2,
        compiler_params=params(),
        cost_estimate=cost(2 * rows * depth * units, 4 * depth * (rows + units), rows * units),
    )(upstream, downs, gate, up)


def head_kernel(count, *refs):
    pieces, (weight, joined, result) = refs[:count], refs[count:]
    join_rows(pieces, joined)
    result[...] = mm(weight[...], joined[...], NT).astype(BF)


def head_product(pieces, weight):
    depth = weight.shape[1]
    rows = sum(p.shape[0] for p in pieces)
    return pl.pallas_call(
        functools.partial(head_kernel, len(pieces)),
        out_shape=[
            jax.ShapeDtypeStruct((rows, depth), BF),
            jax.ShapeDtypeStruct((weight.shape[0], rows), BF),
        ],
        compiler_params=params(),
        cost_estimate=cost(2 * rows * depth * weight.shape[0], 4 * rows * depth),
    )(*pieces, weight)


def grad_kernel(parts, form, starts, *refs):
    rights = refs[parts:-1]
    total = None
    for p in range(parts):
        left = refs[p][...]
        if starts:
            count = left.shape[0]
            right = rights[0][starts[p] : starts[p] + count, :]
        else:
            right = rights[p][...]
        term = mm(left, right, form)
        total = term if total is None else total + term
    refs[-1][...] = total.astype(BF)


def grad_product(lefts, rights, form=TN, starts=()):
    rows = lefts[0].shape[1 if form == TN else 0]
    width = rights[0].shape[1]
    tile = 512
    tokens = sum(r.shape[0] for r in rights)
    return pl.pallas_call(
        functools.partial(grad_kernel, len(lefts), form, starts),
        grid=(width // tile,),
        in_specs=[whole_spec(a.shape) for a in lefts]
        + [pl.BlockSpec((b.shape[0], tile), lambda j: (0, j)) for b in rights],
        out_specs=pl.BlockSpec((rows, tile), lambda j: (0, j)),
        out_shape=jax.ShapeDtypeStruct((rows, width), BF),
        compiler_params=params(),
        cost_estimate=cost(2 * rows * width * tokens, 2 * tokens * (rows + width)),
    )(*lefts, *rights)


def join_kernel(d_qkv, low, weight, grad, share):
    total = mm(d_qkv[...], low[...])
    grad[...] = total.astype(BF)
    sums = jnp.sum(total * weight[...].astype(F32), 0, keepdims=True)
    share[...] = jnp.broadcast_to(sums, share.shape)


def join_product(d_qkv, low, weight):
    rows, width = weight.shape
    tile = 512
    return pl.pallas_call(
        join_kernel,
        grid=(width // tile,),
        in_specs=[
            whole_spec(d_qkv.shape),
            pl.BlockSpec((low.shape[0], tile), lambda j: (0, j)),
            pl.BlockSpec((rows, tile), lambda j: (0, j)),
        ],
        out_specs=[
            pl.BlockSpec((rows, tile), lambda j: (0, j)),
            pl.BlockSpec((8, tile), lambda j: (0, j)),
        ],
        out_shape=[jax.ShapeDtypeStruct((rows, width), BF), jax.ShapeDtypeStruct((8, width), F32)],
        compiler_params=params(),
        cost_estimate=cost(2 * rows * width * low.shape[0], 2 * low.shape[0] * (rows + width)),
    )(d_qkv, low, weight)


def last_kernel(places, d_qkv, weight, keep, send, whole):
    row, rank = places[1], places[2]
    sub = BLK // 8
    width = keep.shape[2]
    whole[...] = mm(d_qkv[...], weight[...], TN).astype(BF)
    for k in range(8):
        at = pl.ds(pl.multiple_of((rank ^ k) * sub, sub), sub)
        for j in range(4):
            target = send if j % 2 else keep
            source = pl.ds(pl.multiple_of((row ^ j) * width, width), width)
            target[j // 2, at, :] = whole[k * sub : (k + 1) * sub, source]


def last_product(places, d_qkv, weight):
    depth = weight.shape[1]
    per = BLOCKS // 2

    def out_map(i, places):
        return ((i // per) ^ places[0], i % per, 0)

    return pl.pallas_call(
        last_kernel,
        grid_spec=pltpu.PrefetchScalarGridSpec(
            num_scalar_prefetch=1,
            grid=(BLOCKS,),
            in_specs=[
                pl.BlockSpec((d_qkv.shape[0], BLK), lambda i, places: (0, i)),
                pl.BlockSpec(weight.shape, lambda i, places: (0, 0)),
            ],
            out_specs=[pl.BlockSpec((2, BLK, depth // 4), out_map)] * 2,
            scratch_shapes=[pltpu.VMEM((BLK, depth), BF)],
        ),
        out_shape=[jax.ShapeDtypeStruct((4, GTOK // 2, depth // 4), BF)] * 2,
        compiler_params=params(),
        cost_estimate=cost(2 * GTOK * depth * d_qkv.shape[0], 2 * GTOK * depth),
    )(places, d_qkv, weight)


def columns_of(values, count, width):
    return jnp.stack([values[..., k * width : (k + 1) * width] for k in range(count)])


def local(
    quick,
    hidden_in,
    gain_before,
    query_weight,
    key_weight,
    value_weight,
    output_weight,
    gain_middle,
    gate_weight,
    up_weight,
    down_weight,
    cotangent,
    branch_points,
    lengths,
):
    width = hidden_in.shape[1]
    depth = 4 * width
    head_width = query_weight.shape[1]
    heads = head_width // HD
    units = gate_weight.shape[1]
    local_tokens = hidden_in.shape[0]
    team = 4 * lax.axis_size("y")
    sub = BLK // team
    x, c = lax.axis_index("x"), lax.axis_index("c")
    z, y = lax.axis_index("z"), lax.axis_index("y")
    row = 2 * x + c
    rank = 4 * y + row
    order = rank if quick else jnp.int32(0)
    branch_row = pick(branch_points, z)
    length_row = pick(lengths, z)
    info = jnp.concatenate([branch_row, length_row, jnp.stack([order * sub])]).astype(jnp.int32)
    places = jnp.stack([y, row, rank]).astype(jnp.int32)

    def full_gather(share):
        blocks = share.shape[0] // sub
        got = lax.all_gather(share.reshape(blocks, sub, depth), TEAM, axis=1, tiled=False)
        return [got.reshape(-1, depth)]

    def full_scatter(partial):
        parts = partial.reshape(-1, team, sub, depth)
        parts = lax.psum_scatter(parts, TEAM, scatter_dimension=1, tiled=False)
        return parts.reshape(-1, depth).astype(F32)

    lines = Lines()
    tick = lines.tick

    def unit_rows(weight):
        pieces = yield from spread_steps(weight.reshape(4, units // 4, width))
        pieces = jnp.concatenate([pieces[k] for k in range(4)], 1)
        if quick:
            lines.extra.append(pieces)
        return [lax.all_gather(pieces, "z", axis=0, tiled=True), pieces]

    joined = jnp.stack([query_weight.T, key_weight.T, value_weight.T, output_weight])
    if heads % 4 == 0:
        per = heads // 4
        pieces = joined.reshape(4, 4, per * HD, width).transpose(1, 0, 2, 3)
        if quick:
            from_y = flip(hidden_in, "y")
            lines.start("heads", spread_steps(pieces))
            tick(None, "heads")
            lines.start("gate", unit_rows(after(gate_weight, lines.wanted["heads"][1][0][0]).T))
            tick(None, "heads")
            tick(None, "gate")
            from_x = flip(after(hidden_in, lines.wanted["gate"][1][0][0]), "x")
            tick(None, "gate")
            pieces = lines.results["heads"]
        else:
            pieces = spread(pieces)
        pieces = jnp.concatenate([pieces[k] for k in range(4)], -1)
        pieces = pieces.reshape(4, per, HD, depth).transpose(1, 0, 2, 3).reshape(per, 4 * HD, depth)
        attend_weights = lax.all_gather(pieces, "z", axis=0, tiled=True)
    else:
        pieces = lax.all_gather(joined, "z", axis=0, tiled=False)
        pieces = spread(pieces).reshape(4, 4, heads, HD, width).transpose(2, 1, 3, 0, 4)
        attend_weights = pieces.reshape(heads, 4 * HD, depth)
    join_weight = attend_weights[:, :ROWS].reshape(heads * ROWS, depth)
    out_weight = attend_weights[:, ROWS:].reshape(heads * HD, depth)

    gains = row_gather(after(jnp.stack([gain_before, gain_middle]), pieces))
    gains = gains.transpose(1, 0, 2).reshape(2, depth)
    gain_one, gain_two = gains[0], gains[1]

    ids = jnp.arange(GTOK, dtype=jnp.int32)
    slot_ids = (ids % BLK) ^ (order * sub)
    starts = jnp.concatenate([jnp.arange(PBLKS, dtype=jnp.int32) * BLK, branch_row])
    positions = jnp.repeat(starts, BLK) + slot_ids
    frequency = THETA ** (-2.0 * jnp.arange(HD // 2, dtype=F32) / HD)
    angles = positions.astype(F32)[None, :] * frequency[:, None]
    cosine, sine = jnp.cos(angles), jnp.sin(angles)

    steps = range(len(CHUNKS))
    ordered = sorted(steps, key=lambda k: CHUNKS[k][0])
    rows_of = [count * BLK for _, count in CHUNKS]
    shares = [slice(first * sub, (first + count) * sub) for first, count in CHUNKS]
    starts = tuple(first * BLK for first, _ in CHUNKS)
    conts = [k for k in ordered if CHUNKS[k][0] >= PBLKS]
    prompts = [k for k in ordered if CHUNKS[k][0] < PBLKS]
    attentions, middles, scales, norms, d_middles, notes = ({} for _ in range(6))
    attended, d_heads = {}, {}

    def to_middle(k, attention):
        middle = residual[shares[k]].astype(F32) + attention
        scale_two = lax.rsqrt(jnp.mean(middle * middle, -1, keepdims=True) + EPSILON)
        norm_two = middle * scale_two
        attentions[k], middles[k], scales[k], norms[k] = attention, middle, scale_two, norm_two
        return (norm_two * gain_two).astype(BF)

    def to_d_middle(k, d_two):
        notes[k] = jnp.sum(d_two * norms[k], 0)
        scaled_two = d_two * gain_two
        inner_two = jnp.mean(scaled_two * norms[k], -1, keepdims=True)
        d_middle = upstream[shares[k]].astype(F32) + scales[k] * (scaled_two - norms[k] * inner_two)
        d_middles[k] = d_middle
        return d_middle.astype(BF)

    def backward(parts, ties, before=None):
        d_out = jnp.concatenate([d_heads[k] for k in parts], 1)
        heads_out = jnp.concatenate([heads_parts[k] for k in ordered], 1)
        lse = jnp.concatenate([lse_parts[k] for k in ordered], 1)
        source = after(qkv, *ties) if ties else qkv
        operands = (source, keys, values, d_out, heads_out, lse, cosine, sine)
        return attend_backward(info, operands, heads, before)

    def total(grad):
        return lax.psum_scatter(grad, "z", scatter_dimension=0, tiled=True)

    def home_steps(part):
        part = yield from spread_steps(columns_of(part, 4, width))
        return part.reshape(-1, width)

    def squares_one():
        wide = hidden_in.astype(F32)
        return jnp.sum(wide * wide, -1)

    def outcome(layer_out, share):
        here = jnp.arange(BLOCKS, dtype=jnp.int32)
        bound = jnp.where(here < PBLKS, BLK, jnp.take(length_row, jnp.maximum(here - PBLKS, 0)))
        slots = rank * sub + jnp.arange(sub, dtype=jnp.int32)
        valid = (slots[None, :] < bound[:, None]).astype(F32).reshape(-1)

        def square_sum(part, weights):
            return jnp.sum(weights * jnp.sum(part * part, -1))

        squares = jnp.stack(
            [square_sum(layer_out.astype(F32), valid)]
            + [
                sum(square_sum(parts[k], valid[shares[k]]) for k in steps)
                for parts in (attentions, d_middles)
            ]
        )
        before_local = share / gain_one
        middle_local = sum(notes[k] for k in steps)
        return jnp.concatenate([before_local, middle_local, squares])

    heads_parts, lse_parts, lows, gates, ups, hiddens = ([] for _ in range(6))
    gate_parts, up_parts = [], []
    if quick:
        former, latter = flip(halves(from_y)[0], "x"), flip(halves(from_x)[1], "y")
        corner = jnp.concatenate([former, latter], 0)
        four = [hidden_in, from_x, from_y, corner]
        hidden_pieces = [p for piece in four for p in (piece, flip(piece, "c"))]
        lines.start("up", unit_rows(up_weight.T))
        lines.start("down", unit_rows(down_weight))
        lines.start("late", place_steps(after(cotangent, corner)))
        lines.launch("late")
        low_one, residual, qkv, keys, values = tick(
            lambda ties: assemble(
                places,
                after(hidden_pieces, *ties),
                gain_one,
                sub,
                (join_weight, cosine, sine),
                heads,
            ),
            "up",
        )

        def forward_line(k, partial):
            low = to_middle(k, (yield from sum_steps(*partial)))
            return (yield from gather_steps(low))

        def attend(k, *names):
            def large(ties):
                return attend_forward(info, after(qkv, *ties), keys, heads, *CHUNKS[k])

            head_part, lse = tick(large, *names)
            heads_parts.append(head_part)
            lse_parts.append(lse)
            partial = split_product([(head_part, out_weight)], TN)
            lines.last = [partial[0]]
            lines.start(k, forward_line(k, partial))

        attend(0, "up")
        lines.land("late")
        attend(1, 0, "late")
        attend(2, 0, 1, "down", "late")
        attend(3, 0, 1, 2)
        gate_rows, up_rows = lines.results["gate"][0], lines.results["up"][0]
        upstream_rows, upstream = tick(
            lambda ties: assemble(places, after(lines.results["late"], *ties), None, sub), 0, 1, 3
        )

        def unit(k, *names):
            def large(ties):
                return unit_products(after(lines.results[k], *ties), gate_rows, up_rows)

            low, gate, up, hidden = tick(large, *names)
            lows.append(low)
            gates.append(gate)
            ups.append(up)
            hiddens.append(hidden)

        def gathered(k):
            lines.last = [lines.wanted[k][1][0][0]]
            tick(None, k)

        tick(None, 0, "down")
        down_rows = lines.results["down"][0]
        gathered(0)
        unit(0, 1, 2)
        tick(None, 1, 2)
        gathered(1)
        unit(1, 2, 3)
        tick(None, 2, 3)
        gathered(2)
        lines.extra.append(down_rows)
        unit(2, 3)
        tick(None, 3)
        gathered(3)
        unit(3)
        down_grad = tick(lambda ties: grad_product(hiddens, [after(upstream_rows, *ties)], TN, starts))
        down_sum = total(down_grad)

        def backward_line(k, partial):
            low = to_d_middle(k, (yield from sum_steps(*partial)))
            pieces = yield from gather_steps(low)
            attended[k], d_heads[k] = head_product(pieces, out_weight)
            return d_heads[k]

        def unit_grad(k, first, second):
            def large(ties):
                source = after(gates[k], *ties)
                return unit_grads(upstream_rows, starts[k], rows_of[k], down_rows, source, ups[k])

            d_gate, d_up = tick(large, *first)
            gate_parts.append(d_gate)
            up_parts.append(d_up)

            def more(ties):
                return split_product([(after(d_gate, *ties), gate_rows), (d_up, up_rows)], NN)

            lines.start(k, backward_line(k, tick(more, *second)))

        unit_grad(0, (), ())
        unit_grad(1, (0,), (0,))
        unit_grad(2, (0, 1), (0, 1))
        unit_grad(3, (0, 1, 2), (0, 1, 2))
        def summed(values, axes):
            for axis in axes:
                (got,) = yield [(values, axis)]
                values = values + got
            return values

        gate_grad = tick(lambda ties: grad_product(after(gate_parts, *ties), lows), 1, 2, 3)
        gate_sum = total(gate_grad)
        mixed = tick(
            lambda ties: mix_product(after([hiddens[k] for k in ordered], *ties), down_rows),
            1,
            2,
            3,
        )
        lines.start("mixed", sum_steps(*mixed))
        before = tick(lambda ties: backward(conts, ties), 2, 3, "mixed")
        lines.start("scale", summed(squares_one(), ("x", "c")))
        up_grad = tick(lambda ties: grad_product(after(up_parts, *ties), lows), 2, 3, "scale")
        up_sum = total(up_grad)
        tick(None, 3, "scale")
        tick(None, 3)
        lines.start("down", home_steps(down_sum))
        lines.start("gate", home_steps(gate_sum))
        d_qkv, inner = tick(lambda ties: backward(prompts, ties, before), "mixed", "down", "gate")
        lines.start("up", home_steps(up_sum))
        own, other = tick(
            lambda ties: last_product(places, after(d_qkv, *ties), join_weight),
            "mixed",
            "down",
            "gate",
        )
        lines.start("last", sum_steps(own, other))
        mixed = lines.results["mixed"]
        layer_out = (jnp.concatenate([middles[k] for k in ordered], 0) + mixed).astype(BF)
        rows = local_tokens // team
        layer_pieces = jnp.stack(
            [
                layer_out[h * rows : (h + 1) * rows, k * width : (k + 1) * width]
                for h in range(2)
                for k in range(4)
            ]
        )
        lines.extra.append(layer_pieces)
        layer_pieces = lax.all_to_all(layer_pieces, TEAM, 0, 0, tiled=True)
        join_grad, share = tick(
            lambda ties: join_product(after(d_qkv, *ties), low_one, join_weight),
            "last",
            "up",
        )
        join_sum = total(join_grad)
        inner = after(inner, join_grad)
        inner = straighten(inner[0].reshape(BLOCKS, team, sub), rank).reshape(GTOK)
        lines.start("inner", summed(inner, ("x", "c", "y")))
        out_grad = tick(
            lambda ties: grad_product(
                after([heads_parts[k] for k in ordered], *ties), [attended[k] for k in ordered], NN
            ),
            "last",
            "inner",
            "up",
        )
        turned = lines.wanted["last"][1][0][0]
        sums = outcome(after(layer_out, out_grad), share[0])
        lines.start("sums", summed(sums, ("c", "z1", "z2", "x", "y")))
        tick(None, "sums", "inner")
        tick(None, "sums", "inner")
        tick(None, "sums")
        tick(None, "last")
        lines.last = [lines.results["last"]]
        for _ in range(2):
            tick(None, "sums")
        d_one, inner, sums = (lines.results[n] for n in ("last", "inner", "sums"))
        join_sum, out_sum = after((join_sum, total(out_grad)), d_one)
        lines.results["up"] = after(lines.results["up"], turned)
        lines.results["gate"], lines.results["down"], attended, layer_pieces, inner = after(
            (lines.results["gate"], lines.results["down"], attended, layer_pieces, inner), out_grad
        )
        gate_grad, up_grad, down_grad = (lines.results[n] for n in ("gate", "up", "down"))
    else:

        def full(values):
            values = lax.all_gather(values, "y", axis=0, tiled=True)
            return lax.all_gather(values, ROW, axis=1, tiled=True)

        def share_of(values):
            return pick(values.reshape(BLOCKS, team, sub, depth), rank, 1).reshape(-1, depth)

        gate_rows = complete(unit_rows(gate_weight.T))[0]
        up_rows = complete(unit_rows(up_weight.T))[0]
        down_rows = complete(unit_rows(down_weight))[0]
        hidden_rows = full(hidden_in)
        upstream_rows = full(cotangent)
        residual, upstream = share_of(hidden_rows), share_of(upstream_rows)
        wide = hidden_rows.astype(F32)
        scale = lax.rsqrt(jnp.mean(wide * wide, -1, keepdims=True) + EPSILON)
        low_one = (wide * scale * gain_one).astype(BF)
        qkv, keys, values = project(join_weight, low_one, cosine, sine, heads)
        for k in steps:
            head_part, lse = attend_forward(info, qkv, keys, heads, *CHUNKS[k])
            heads_parts.append(head_part)
            lse_parts.append(lse)
            low = to_middle(k, full_scatter(mm(head_part, out_weight, TN).astype(BF)))
            low, gate, up, hidden = unit_products(full_gather(low), gate_rows, up_rows)
            lows.append(low)
            hiddens.append(hidden)
            d_gate, d_up = unit_grads(upstream_rows, starts[k], rows_of[k], down_rows, gate, up)
            gate_parts.append(d_gate)
            up_parts.append(d_up)
            partial = (mm(d_gate, gate_rows) + mm(d_up, up_rows)).astype(BF)
            low = to_d_middle(k, full_scatter(partial))
            attended[k], d_heads[k] = head_product(full_gather(low), out_weight)
        gate_sum, up_sum = total(grad_product(gate_parts, lows)), total(grad_product(up_parts, lows))
        down_sum = total(grad_product(hiddens, [upstream_rows], TN, starts))
        mixed = full_scatter(
            jnp.concatenate([mm(hiddens[k], down_rows).astype(BF) for k in ordered], 0)
        )
        d_qkv, inner = backward(prompts, [], backward(conts, []))
        partial = mm(d_qkv, join_weight, TN).astype(BF)
        join_grad, share = join_product(d_qkv, low_one, join_weight)
        out_grad = grad_product([heads_parts[k] for k in ordered], [attended[k] for k in ordered], NN)
        layer_out = (jnp.concatenate([middles[k] for k in ordered], 0) + mixed).astype(BF)
        sums = lax.psum(outcome(layer_out, share[0]), EVERY)
        gate_grad, up_grad, down_grad = (
            complete(home_steps(part)) for part in (gate_sum, up_sum, down_sum)
        )

    attended = [attended[k] for k in ordered]
    gate_grad, up_grad = gate_grad.T.astype(F32), up_grad.T.astype(F32)
    down_grad = down_grad.astype(F32)
    if heads % 4 == 0:
        part = join_sum if quick else total(join_grad)
        part = part.reshape(heads // 4, 3, HD, depth).transpose(1, 0, 2, 3)
        part = spread(columns_of(part.reshape(3, heads // 4 * HD, depth), 4, width))
        part = part.transpose(1, 0, 2, 3).reshape(3, head_width, width)
        out_part = spread(columns_of(out_sum if quick else total(out_grad), 4, width)).reshape(1, head_width, width)
        part = jnp.concatenate([part, out_part], 0)
    else:
        part = jnp.concatenate(
            [join_grad.reshape(heads, 3, HD, depth), out_grad.reshape(heads, 1, HD, depth)], 1
        ).transpose(1, 0, 2, 3)
        part = spread(columns_of(part.reshape(4, heads * HD, depth), 4, width))
        part = lax.psum_scatter(part, "z", scatter_dimension=0, tiled=False)
    query_grad, key_grad, value_grad = (part[k].T.astype(F32) for k in range(3))
    output_grad = part[3].astype(F32)

    if quick:
        half = local_tokens
        inner = pick(inner.reshape(2, half), y)
        d_middle = jnp.concatenate(
            [lax.dynamic_slice_in_dim(a, row * width, width, 1) for a in attended], 0
        )
        d_middle = pick(d_middle.reshape(2, BLOCKS // 2, team, sub, width), y)
        d_middle = straighten(d_middle, rank).reshape(half, width).astype(F32)
        layer_out = layer_pieces.reshape(team, BLOCKS // 2, sub, width).transpose(1, 0, 2, 3)
        layer_out = layer_out.reshape(half, width)
    else:
        d_one = lax.psum_scatter(partial, "y", scatter_dimension=0, tiled=True)
        d_one = lax.psum_scatter(d_one, ROW, scatter_dimension=1, tiled=True).astype(F32)
        inner = lax.psum(inner[0], TEAM)
        inner = lax.dynamic_slice(inner, (y * local_tokens,), (local_tokens,))
        corner = (y * local_tokens, row * width)
        d_middle = lax.dynamic_slice(
            jnp.concatenate(attended, 0), corner, (local_tokens, width)
        ).astype(F32)
        layer_out = lax.all_gather(
            layer_out.reshape(BLOCKS, sub, depth), TEAM, axis=1, tiled=False
        ).reshape(GTOK, depth)
        layer_out = lax.dynamic_slice(layer_out, corner, (local_tokens, width))
    wide = hidden_in.astype(F32)
    row_squares = lines.results["scale"] if quick else row_sum(squares_one())
    scale_one = lax.rsqrt(row_squares / depth + EPSILON)[:, None]
    norm_one = wide * scale_one
    input_grad = d_middle + scale_one * (d_one * gain_before - norm_one * (inner / depth)[:, None])

    before_grad = lax.dynamic_slice(sums, (row * width,), (width,))
    middle_grad = lax.dynamic_slice(sums, (depth + row * width,), (width,))
    valid_count = (lengths.shape[0] * PROMPT + jnp.sum(lengths)).astype(F32)
    rms_values = jnp.sqrt(sums[2 * depth :] / (valid_count * depth))
    return (
        layer_out,
        input_grad,
        before_grad,
        query_grad,
        key_grad,
        value_grad,
        output_grad,
        middle_grad,
        gate_grad,
        up_grad,
        down_grad,
        rms_values,
    )


def solution(mesh):
    split = mesh.shape["col"] // GROUPS
    grid = Mesh(mesh.devices.reshape(2, 2, GROUPS, split), ("x", "c", "z", "y"))
    row, col = ("x", "c"), ("z", "y")
    return jax.shard_map(
        functools.partial(local, split == 2),
        mesh=grid,
        in_specs=(
            P(col, row),
            P(row),
            P(row, col),
            P(row, col),
            P(row, col),
            P(col, row),
            P(row),
            P(row, col),
            P(row, col),
            P(col, row),
            P(col, row),
            P(),
            P(),
        ),
        out_specs=(
            P(col, row),
            P(col, row),
            P(row),
            P(row, col),
            P(row, col),
            P(row, col),
            P(col, row),
            P(row),
            P(row, col),
            P(row, col),
            P(col, row),
            P(),
        ),
        check_vma=False,
    )
```
